256 devices in a mesh: batch: 4 (over y), lat: 4 (over x_hi, core), lon: 16 (over z, x_lo).
Axes of the slice: x: 4 (x_hi: 2, x_lo: 2; x = x_hi * 2 + x_lo), y: 4, z: 8, core: 2. Of those that a mesh axis runs over, the one named last changes fastest.
Arguments:
- bottom_codes: int32 [4, 128, 256], P('batch', 'lat', 'lon'), may hold values from 0 to 511
- mask_flags: int32 [4, 128, 256], P('batch', 'lat', 'lon'), may hold values 0 or 1
- top_codes: int32 [4, 64, 128], P('batch', 'lat', 'lon'), may hold values from 0 to 511
- bottom_table: bfloat16 [512, 1024], replicated, may hold values from -3 to 3
- top_table: bfloat16 [512, 1024], replicated, may hold values from -3 to 3
- mask_vector: bfloat16 [1024], replicated, may hold values from -3 to 3
- qkv_weight: bfloat16 [1024, 1536], replicated, may hold values from -0.3 to 0.3
- out_weight: bfloat16 [1024, 512], replicated, may hold values from -0.5 to 0.5
- cotangent: bfloat16 [4, 128, 256, 1024], P('batch', 'lat', 'lon'), may hold values from -6 to 6
Outputs:
- output: bfloat16 [4, 128, 256, 1024], P('batch', 'lat', 'lon')
- grad_input: bfloat16 [4, 128, 256, 1024], P('batch', 'lat', 'lon')
- grad_qkv: float32 [1024, 1536], P(('lat', 'lon'))
- grad_out: float32 [1024, 512], P(('lat', 'lon'))
The draws below stay inside these ranges and needn't reach their ends.
All inputs are finite; a program needn't handle non-finite values. No bound on the sum of `mask_flags` on one device may be relied on, other than what follows from the above.
Results may differ from the reference program's by a relative error of at most 0.012.
Values may be sent and summed in bfloat16 or wider, within the bound.
No kernel may reach another device: no remote copies, remote signals or barrier semaphores. Data moves between devices by JAX's collectives and lax.ppermute only.
A program may use at most 192 MiB of HBM per device.

```python
import math
import jax
import jax.numpy as jnp
from jax import lax

D = 1024
HEADS = 8
HDIM = 64
WIN = 8
VB = 512
VT = 512
HW = 512
SHIFT = 4
B = 4
NH = 128
NW = 256


weight_bound = 0.296875


def draw_qkv_weight(key, part):
    key = jax.random.fold_in(key, 7)
    base = jax.random.normal(key, (D, 3 * HW), jnp.float32) / D ** 0.5
    return jnp.clip(base, -weight_bound, weight_bound).astype(jnp.bfloat16)


def set_ends(values, rng, smallest, high):
    shape = values.shape
    place = [jax.random.randint(jax.random.fold_in(rng, axis), (), 0, shape[axis]) for axis in range(len(shape))]
    values = values.at[tuple(place)].set(smallest)
    longest = shape.index(max(shape))
    place[longest] = (place[longest] + 1) % shape[longest]
    return values.at[tuple(place)].set(high)


def shard_levels(key, extent, cuts, smallest, largest):
    def one(axis_at, blocks):
        heights = jax.random.uniform(jax.random.fold_in(jax.random.fold_in(key, 6), axis_at), (blocks,), jnp.float32, smallest / len(cuts), largest / len(cuts))
        return jnp.repeat(jnp.exp(heights), extent[axis_at] // blocks).reshape((-1,) + (1,) * (len(extent) - axis_at - 1))

    loudness = one(*cuts[0])
    for cut in cuts[1:]:
        loudness = loudness * one(*cut)
    return loudness


def normal_values(stream_key, shape, deviation, limit, cuts=(), kind=jnp.bfloat16):
    loudness = shard_levels(stream_key, shape, cuts, -0.22, 0.18) if cuts else 1.0
    drawn = jax.random.normal(stream_key, shape, jnp.float32) * deviation * loudness
    return jnp.minimum(jnp.maximum(drawn, -limit), limit).astype(kind)


def setup_inputs(seed: int = 0) -> dict:
    seeds = jax.random.split(jax.random.key(seed), 10)
    return {
        "bottom_codes": set_ends(jax.random.randint(seeds[0], (B, NH, NW), 0, VB), jax.random.fold_in(seeds[0], 1), 0, VB - 1).astype(jnp.int32),
        "mask_flags": set_ends((jax.random.randint(seeds[1], (B, NH, NW), 0, 2) < 1).astype(jnp.int32), jax.random.fold_in(seeds[1], 1), 0, 1),
        "top_codes": set_ends(jax.random.randint(seeds[2], (B, NH // 2, NW // 2), 0, VT), jax.random.fold_in(seeds[2], 1), 0, VT - 1).astype(jnp.int32),
        "bottom_table": normal_values(seeds[3], (VB, D), 0.5, 3.0),
        "top_table": normal_values(seeds[4], (VT, D), 0.5, 3.0),
        "mask_vector": normal_values(seeds[5], (D,), 0.5, 3.0),
        "qkv_weight": draw_qkv_weight(jax.random.fold_in(seeds[9], 71), 0),
        "out_weight": normal_values(seeds[7], (D, HW), (HW // 4) ** -0.5, 0.5),
        "cotangent": normal_values(seeds[8], (B, NH, NW, D), 1.0, 6.0, ((0, 4), (1, 4), (2, 16))),
    }


epsilon = 1e-05

def contract(form, left_side, right_side):
    return jnp.einsum(form, left_side.astype(jnp.float32), right_side.astype(jnp.float32))

def window_split(grid, height, breadth):
    features = grid.shape[-1]
    grid = grid.reshape(height // WIN, WIN, breadth // WIN, WIN, features)
    grid = grid.transpose(0, 2, 1, 3, 4)
    return grid.reshape(height // WIN * (breadth // WIN), WIN * WIN, features)

def window_join(windows, height, breadth):
    features = windows.shape[-1]
    grid = windows.reshape(height // WIN, breadth // WIN, WIN, WIN, features)
    grid = grid.transpose(0, 2, 1, 3, 4)
    return grid.reshape(height, breadth, features)

def embed_codes(bottom_grid, mask_grid, top_grid, bottom_table, top_table, mask_vector):
    bottom_rows = jnp.take(bottom_table, bottom_grid, axis=0).astype(jnp.float32)
    bottom_rows = jnp.where((mask_grid == 1)[:, :, None], mask_vector.astype(jnp.float32)[None, None, :], bottom_rows)
    upper_rows = jnp.take(top_table, top_grid, axis=0).astype(jnp.float32)
    top_height, top_breadth, model_width = upper_rows.shape
    upper_rows = jnp.broadcast_to(upper_rows[:, None, :, None, :], (top_height, 2, top_breadth, 2, model_width))
    upper_rows = upper_rows.reshape(2 * top_height, 2 * top_breadth, model_width)
    return (bottom_rows + upper_rows).astype(jnp.bfloat16)

def block_pass(embedded, cotangent, qkv_weight, out_weight, wrap_part):
    height, breadth, model_width = embedded.shape
    token_count = height * breadth
    score_scale = 1.0 / math.sqrt(HDIM)
    inputs = embedded.reshape(token_count, model_width).astype(jnp.float32)
    centred = inputs - lax.optimization_barrier(jnp.mean(inputs, axis=1, keepdims=True))
    inverse = lax.rsqrt(lax.optimization_barrier(jnp.mean(centred * centred, axis=1, keepdims=True)) + epsilon)
    standard = centred * inverse
    normed = standard.astype(jnp.bfloat16)
    projected = jnp.dot(normed, qkv_weight, preferred_element_type=jnp.float32).astype(jnp.bfloat16)
    windows = window_split(projected.reshape(height, breadth, 3 * HW), height, breadth)
    window_count = windows.shape[0]
    per_head = windows.reshape(window_count, WIN * WIN, 3, HEADS, HDIM)
    query_heads = per_head[:, :, 0]
    key_heads = per_head[:, :, 1]
    value_heads = per_head[:, :, 2]
    parts = window_split(wrap_part.astype(jnp.int32)[:, :, None], height, breadth)[:, :, 0]
    allowed = parts[:, :, None] == parts[:, None, :]
    scores = contract('wqhd,wkhd->whqk', query_heads, key_heads) * score_scale
    scores = jnp.where(allowed[:, None, :, :], scores, -1e+30)
    highest = lax.optimization_barrier(jnp.max(scores, axis=-1, keepdims=True))
    powers = jnp.exp(scores - highest)
    shares = powers / lax.optimization_barrier(jnp.sum(powers, axis=-1, keepdims=True))
    shares_bf = shares.astype(jnp.bfloat16)
    mixed = contract('whqk,wkhd->wqhd', shares_bf, value_heads).astype(jnp.bfloat16)
    attended = window_join(mixed.reshape(window_count, WIN * WIN, HW), height, breadth).reshape(token_count, HW)
    branch = lax.dot_general(attended, out_weight, (((1,), (1,)), ((), ())), preferred_element_type=jnp.float32)
    output = (inputs + branch).astype(jnp.bfloat16)
    upstream = cotangent.reshape(token_count, model_width)
    grad_attended = jnp.dot(upstream, out_weight, preferred_element_type=jnp.float32).astype(jnp.bfloat16)
    grad_heads = window_split(grad_attended.reshape(height, breadth, HW), height, breadth)
    grad_heads = grad_heads.reshape(window_count, WIN * WIN, HEADS, HDIM)
    grad_shares = contract('wqhd,wkhd->whqk', grad_heads, value_heads)
    row_delta = lax.optimization_barrier(jnp.sum(shares * grad_shares, axis=-1, keepdims=True))
    grad_scores = (shares * (grad_shares - row_delta) * score_scale).astype(jnp.bfloat16)
    grad_query = contract('whqk,wkhd->wqhd', grad_scores, key_heads)
    grad_key = contract('whqk,wqhd->wkhd', grad_scores, query_heads)
    grad_value = contract('whqk,wqhd->wkhd', shares_bf, grad_heads)
    grad_windows = jnp.stack([grad_query, grad_key, grad_value], axis=2).astype(jnp.bfloat16)
    grad_windows = grad_windows.reshape(window_count, WIN * WIN, 3 * HW)
    grad_projected = window_join(grad_windows, height, breadth).reshape(token_count, 3 * HW)
    grad_standard = lax.dot_general(grad_projected, qkv_weight, (((1,), (1,)), ((), ())), preferred_element_type=jnp.float32)
    grad_inputs = inverse * (grad_standard - lax.optimization_barrier(jnp.mean(grad_standard, axis=1, keepdims=True)) - standard * lax.optimization_barrier(jnp.mean(grad_standard * standard, axis=1, keepdims=True)))
    grad_embedded = (upstream.astype(jnp.float32) + grad_inputs).astype(jnp.bfloat16)
    return (output.reshape(height, breadth, model_width), grad_embedded.reshape(height, breadth, model_width), normed, grad_projected, attended, upstream)

def reference(bottom_codes, mask_flags, top_codes, bottom_table, top_table, mask_vector, qkv_weight, out_weight, cotangent):
    wrap_part = jnp.broadcast_to((jnp.arange(NH) < SHIFT)[:, None], (NH, NW))

    def panorama(inputs):
        bottom_grid, mask_grid, top_grid, grad_grid = inputs
        embedded = embed_codes(bottom_grid, mask_grid, top_grid, bottom_table, top_table, mask_vector)
        rolled = jnp.roll(embedded, (SHIFT, SHIFT), (0, 1))
        rolled_grad = jnp.roll(grad_grid, (SHIFT, SHIFT), (0, 1))
        output, grad_embedded, normed, grad_projected, attended, upstream = block_pass(rolled, rolled_grad, qkv_weight, out_weight, wrap_part)
        qkv_term = lax.dot_general(normed, grad_projected, (((0,), (0,)), ((), ())), preferred_element_type=jnp.float32)
        out_term = lax.dot_general(upstream, attended, (((0,), (0,)), ((), ())), preferred_element_type=jnp.float32)
        return (jnp.roll(output, (-SHIFT, -SHIFT), (0, 1)), jnp.roll(grad_embedded, (-SHIFT, -SHIFT), (0, 1)), qkv_term, out_term)
    outputs, grads, qkv_terms, out_terms = lax.map(panorama, (bottom_codes, mask_flags, top_codes, cotangent))
    factor = 1.0 / math.sqrt(B * NH * NW)
    return (outputs, grads, lax.optimization_barrier(jnp.sum(qkv_terms, axis=0)) * factor, lax.optimization_barrier(jnp.sum(out_terms, axis=0)) * factor)
```

```python
import functools
import math

import jax
import jax.numpy as jnp
from jax import lax
from jax.experimental import pallas as pl
from jax.experimental.pallas import tpu as pltpu
from jax.sharding import PartitionSpec as P

HEADS = 8
HDIM = 64
WIN = 8
HW = 512
SHIFT = 4
EPS = 1e-05
MODEL = 1024
ROWS, COLS = 32, 16
TOKENS = ROWS * COLS
BAND = WIN * COLS
BANDS = TOKENS // BAND
CHUNKS = 2
CW = HW // CHUNKS
F32 = jnp.float32
BF16 = jnp.bfloat16
GRID = ("xh", "core", "z", "xl")
NB, NLAT, NLON = 4, 4, 16


def dot(a, b, ca, cb):
    return lax.dot_general(a, b, (((ca,), (cb,)), ((), ())), preferred_element_type=F32)


def vmem():
    return pl.BlockSpec(memory_space=pltpu.VMEM)


def smem():
    return pl.BlockSpec(memory_space=pltpu.SMEM)


def call(kernel, outs, operands, specs, flops, nbytes, trans=0, limit=28, name=None):
    return pl.pallas_call(
        kernel,
        out_shape=outs,
        in_specs=specs,
        out_specs=jax.tree.map(lambda _: vmem(), outs),
        compiler_params=pltpu.CompilerParams(vmem_limit_bytes=limit * 2**20),
        cost_estimate=pl.CostEstimate(flops=flops, bytes_accessed=nbytes, transcendentals=trans),
        name=name,
    )(*operands)


def sds(shape, dtype=BF16):
    return jax.ShapeDtypeStruct(shape, dtype)


def iota(shape, dim):
    return lax.broadcasted_iota(jnp.int32, shape, dim)


def moments(x):
    mean = jnp.mean(x, axis=1, keepdims=True)
    centred = x - mean
    inverse = lax.rsqrt(jnp.mean(centred * centred, axis=1, keepdims=True) + EPS)
    return centred, inverse


CODES = 128
WIDE = MODEL + CODES
MSG = SHIFT * (ROWS - SHIFT)
OWN = (ROWS - SHIFT) * COLS
LATE = COLS - SHIFT


def hot(mask):
    return mask.astype(F32).astype(BF16)


def pack_kernel(bottom, flags, top, cot, own, up, left, diag):
    def digits(codes, rows, row_of, lane_of):
        width = codes.shape[1]
        parts = jnp.concatenate([codes >> 4, codes & 15], axis=1).astype(F32).astype(BF16)
        pick = hot(row_of(iota((TOKENS, rows), 0)) == iota((TOKENS, rows), 1))
        spread = dot(pick, parts, 1, 0)
        t, lane = iota(spread.shape, 0), iota(spread.shape, 1)
        inside = jnp.where(lane < width, lane, lane - width) == lane_of(t)
        spread = jnp.where(inside, spread, 0.0)
        return (
            jnp.sum(jnp.where(lane < width, spread, 0.0), axis=1, keepdims=True),
            jnp.sum(jnp.where(lane < width, 0.0, spread), axis=1, keepdims=True),
        )

    code = jnp.where(flags[...] == 1, 512, bottom[...])
    bh, bl = digits(code, ROWS, lambda t: t >> 4, lambda t: t & 15)
    th, tl = digits(top[...], ROWS // 2, lambda t: t >> 5, lambda t: (t & 15) >> 1)
    lane = iota((TOKENS, CODES), 1)
    block = jnp.where(lane == 0, bh, jnp.where(lane == 1, bl, jnp.where(lane == 2, th, tl)))
    block = jnp.where(lane < 4, block, 0.0).astype(BF16)
    own[...] = block
    up[:, :MODEL] = cot[OWN:]
    up[:, MODEL:] = block[OWN:]
    m, t = iota((MSG, OWN), 0), iota((MSG, OWN), 1)
    pick = hot(t == (m >> 2) * COLS + LATE + (m & 3))
    left[:, :MODEL] = dot(pick, cot[:OWN], 1, 0).astype(BF16)
    left[:, MODEL:] = dot(pick, block[:OWN], 1, 0).astype(BF16)
    m, t = iota((16, 64), 0), iota((16, 64), 1)
    pick = hot(t == (m >> 2) * COLS + LATE + (m & 3))
    diag[:, :MODEL] = dot(pick, cot[OWN:], 1, 0).astype(BF16)
    diag[:, MODEL:] = dot(pick, block[OWN:], 1, 0).astype(BF16)


def embed(codes, bt, tt, mv, wq):
    digit = codes.astype(F32)
    cb = (digit[:, 0:1] * 16.0 + digit[:, 1:2]).astype(jnp.int32)
    ct = (digit[:, 2:3] * 16.0 + digit[:, 3:4]).astype(jnp.int32)
    lanes = iota((codes.shape[0], 512), 1)
    x = dot(hot(lanes == cb), bt[...], 1, 0)
    x = jnp.where(cb == 512, mv[...].astype(F32), x)
    x = (x + dot(hot(lanes == ct), tt[...], 1, 0)).astype(BF16)
    centred, inverse = moments(x.astype(F32))
    n = (centred * inverse).astype(BF16)
    return x, n, dot(n, wq[...], 1, 0).astype(BF16)


def own_kernel(codes, bt, tt, mv, wq, emb, normed, proj):
    step = 112
    for at in range(0, OWN, step):
        here = slice(at, at + step)
        emb[here], normed[here], proj[here] = embed(codes[here], bt, tt, mv, wq)


def halo_kernel(up, left, diag, cot, oemb, onormed, oproj, bt, tt, mv, wq, emb, normed, proj, grad):
    p = iota((64, 1), 0) & 15
    m, t = iota((64, 16), 1), iota((64, 16), 0)
    corner = dot(hot(t == (m >> 2) * COLS + LATE + (m & 3)), diag[...], 1, 0)
    upper = jnp.where(p >= LATE, corner, up[...].astype(F32)).astype(BF16)
    grad[0:64] = upper[:, :MODEL]
    emb[0:64], normed[0:64], proj[0:64] = embed(upper[:, MODEL:], bt, tt, mv, wq)
    new = embed(left[:, MODEL:], bt, tt, mv, wq)
    step = 64
    p = iota((step, 1), 0) & 15
    for at in range(0, OWN, step):
        m, t = iota((step, MSG), 1), at + iota((step, MSG), 0)
        spread = hot(t == (m >> 2) * COLS + LATE + (m & 3))
        old, out = slice(at, at + step), slice(64 + at, 64 + at + step)
        for source, values, ref in (
            (cot, left[:, :MODEL], grad),
            (oemb, new[0], emb),
            (onormed, new[1], normed),
            (oproj, new[2], proj),
        ):
            values = dot(spread, values, 1, 0)
            ref[out] = jnp.where(p >= LATE, values, source[old].astype(F32)).astype(BF16)


def attend_kernel(place, q, k, v, normed, cot, ow, att, gp, keep, send):
    grad = dot(cot[...], ow[...], 1, 0).astype(BF16)
    lane = iota((BAND, 128), 1) < 64
    tk, tq = iota((BAND, BAND), 0), iota((BAND, BAND), 1)

    def side(t):
        c = t & 15
        return ((c >= 4) & (c < 12)).astype(jnp.int32)

    same = side(tk) == side(tq)
    whole = (tk >> 6) == (tq >> 6)
    zero = jnp.zeros((BAND, BAND), F32)
    plain = jnp.where(same, zero, -1e30)
    first = jnp.where(whole | (place[0] != 0), plain, -1e30)

    def split(x):
        none = jnp.zeros_like(x)
        return jnp.concatenate([jnp.where(lane, x, none), jnp.where(lane, none, x)], axis=0)

    def pick(x):
        return jnp.where(lane, x[:BAND], x[BAND:])

    for b in range(BANDS):
        bias = first if b == 0 else plain
        here = slice(b * BAND, (b + 1) * BAND)
        for p in range(CW // 128):
            cols = slice(p * 128, (p + 1) * 128)
            qq = q[here, cols]
            kk, vv = split(k[here, cols]), split(v[here, cols])
            da = grad[here, cols]
            s = dot(kk, qq, 1, 1).reshape(2, BAND, BAND) * 0.125 + bias
            e = jnp.exp(s - jnp.max(s, axis=1, keepdims=True))
            share = e * (1.0 / jnp.sum(e, axis=1, keepdims=True))
            sb = share.astype(BF16).reshape(2 * BAND, BAND)
            att[here, cols] = dot(sb, vv, 0, 0).astype(BF16)
            gs = dot(vv, da, 1, 1).reshape(2, BAND, BAND)
            delta = jnp.sum(share * gs, axis=1, keepdims=True)
            ds = (share * (gs - delta) * 0.125).astype(BF16).reshape(2 * BAND, BAND)
            at = p * 128
            gp[here, at : at + 128] = dot(ds, kk, 0, 0).astype(BF16)
            gp[here, CW + at : CW + at + 128] = pick(dot(ds, qq, 1, 0)).astype(BF16)
            gp[here, 2 * CW + at : 2 * CW + at + 128] = pick(dot(sb, da, 1, 0)).astype(BF16)

    core = place[1]
    for half in range(2):
        for out, flip in ((send, 1), (keep, 0)):
            cut = pl.ds(pl.multiple_of(half * 512 + (core ^ flip) * 256, 256), 256)
            out[half, :, 0 : 3 * CW] = dot(normed[:, cut], gp[...], 0, 0).astype(out.dtype)
            out[half, :, 3 * CW :] = dot(cot[:, cut], att[...], 0, 0).astype(out.dtype)


def finish_kernel(emb, cot, wq, ow, att0, att1, gp0, gp1, both):
    for block in range(BANDS):
        here = slice(block * BAND, (block + 1) * BAND)
        x = emb[here].astype(F32)
        att = jnp.concatenate([att0[here], att1[here]], axis=1)
        both[0, here] = (x + dot(att, ow[...], 1, 1)).astype(BF16)
        g0, g1 = gp0[here], gp1[here]
        parts = []
        for i in range(3):
            parts += [g0[:, i * CW : (i + 1) * CW], g1[:, i * CW : (i + 1) * CW]]
        gst = dot(jnp.concatenate(parts, axis=1), wq[...], 1, 1)
        centred, inverse = moments(x)
        standard = centred * inverse
        m1 = jnp.mean(gst, axis=1, keepdims=True)
        m2 = jnp.mean(gst * standard, axis=1, keepdims=True)
        both[1, here] = (cot[here].astype(F32) + inverse * (gst - m1 - standard * m2)).astype(BF16)


W = 4 * CW
Q = W // 4


def cut_x1(place, total, keep, send):
    g = place[2] ^ place[3]
    for xh in range(2):
        keep[xh] = total(xh, xh ^ g)
        send[xh] = total(xh, xh ^ g ^ 1).astype(BF16)


def cut_y1(place, total, keep, send):
    g = place[4] ^ place[5]
    for yh in range(2):
        keep[..., yh * Q : (yh + 1) * Q] = total(2 * yh + (yh ^ g))
        send[..., yh * Q : (yh + 1) * Q] = total(2 * yh + (yh ^ g ^ 1)).astype(BF16)


def lanes(i):
    return pl.ds(pl.multiple_of(i * Q, Q), Q)


def x_core(place, a, b, keep, send):
    cut_x1(place, lambda u, v: a[u, :, v] + b[u, :, v].astype(F32), keep, send)


def x_pair(place, a, b, keep, send):
    xh = place[2]
    keep[...] = a[xh] + b[xh].astype(F32)
    send[...] = (a[xh ^ 1] + b[xh ^ 1].astype(F32)).astype(BF16)


def y_core(place, a, b, keep, send):
    cut_y1(place, lambda i: a[:, :, lanes(i)] + b[:, :, lanes(i)].astype(F32), keep, send)


def y_pair(place, a, b, keep, send):
    yh = place[4]
    keep[...] = a[:, :, lanes(yh)] + b[:, :, lanes(yh)].astype(F32)
    send[...] = (a[:, :, lanes(yh ^ 1)] + b[:, :, lanes(yh ^ 1)].astype(F32)).astype(BF16)


def z_first(place, a, b, c, d, keep, send):
    bit = place[6] & 1
    for k in range(4):
        for out, at in ((keep, 2 * k + bit), (send, 2 * k + (bit ^ 1))):
            out[k, :, 0:Q] = (a[at] + b[at].astype(F32)).astype(out.dtype)
            out[k, :, Q:] = (c[at] + d[at].astype(F32)).astype(out.dtype)


def z_second(place, a, b, keep, send):
    bit = (place[6] >> 1) & 1
    for k in range(2):
        for out, at in ((keep, 2 * k + bit), (send, 2 * k + (bit ^ 1))):
            out[k] = (a[at] + b[at].astype(F32)).astype(out.dtype)


def z_third(place, a, b, keep, send):
    bit = place[6] >> 2
    keep[...] = a[bit] + b[bit].astype(F32)
    send[...] = (a[bit ^ 1] + b[bit ^ 1].astype(F32)).astype(BF16)


def level_kernel(factor, a, b, out):
    out[...] = (a[...] + b[...].astype(F32)) * factor


def spread_kernel(place, *refs):
    qkv, outw = refs[4:]
    for d in range(4):
        who = (2 * place[4] + place[5]) ^ d
        for c in range(CHUNKS):

            @pl.when(who < 3)
            def _():
                qkv[:, pl.ds(pl.multiple_of(who * HW + c * CW, CW), CW)] = refs[d][:, c * Q : (c + 1) * Q]

            @pl.when(who == 3)
            def _():
                outw[:, c * CW : (c + 1) * CW] = refs[d][:, c * Q : (c + 1) * Q]


def permute(x, where):
    pairs = []
    for la in range(NLAT):
        for lo in range(NLON):
            tl, to = where(la, lo)
            pairs.append((la * NLON + lo, tl * NLON + to))
    return lax.ppermute(x, GRID, pairs)


def shift(x, down, right):
    return permute(x, lambda la, lo: ((la + down) % NLAT, (lo + right) % NLON))


def swap(x, axis, flip):
    return lax.ppermute(x, axis, [(i, i ^ flip) for i in range(lax.axis_size(axis))])


def swap_x(x, flip):
    return permute(x, lambda la, lo: (la ^ (flip & 2), lo ^ (flip & 1)))


def halve(kernel, shape, place, *terms):
    size = math.prod(shape)
    return call(
        kernel,
        [sds(shape, F32), sds(shape)],
        (place, *terms),
        [smem()] + [vmem()] * len(terms),
        2 * size,
        16 * size,
        limit=16,
        name=kernel.__name__,
    )


def sum_x_first(place, keep, send):
    fold = (2, 8, 2, 16, W)
    recv = swap(send, "core", 1)
    keep, send = halve(x_core, (2, 8, 16, W), place, keep.reshape(fold), recv.reshape(fold))
    keep, send = halve(x_pair, (8, 16, W), place, keep, swap_x(send, 1))
    keep, send = halve(y_core, (8, 16, 2 * Q), place, keep, swap_x(send, 3))
    keep, send = halve(y_pair, (8, 16, Q), place, keep, swap(send, "batch", 1))
    return keep, swap(send, "batch", 3)


def sum_y_first(place, keep, send):
    recv = swap(send, "core", 1)
    keep, send = halve(y_core, (2, 256, 2 * Q), place, keep, recv)
    keep, send = halve(y_pair, (2, 256, Q), place, keep, swap(send, "batch", 1))
    fold = (2, 8, 2, 16, Q)
    recv = swap(send, "batch", 3)
    keep, send = halve(x_core, (2, 8, 16, Q), place, keep.reshape(fold), recv.reshape(fold))
    keep, send = halve(x_pair, (8, 16, Q), place, keep, swap_x(send, 1))
    return keep, swap_x(send, 3)


def shards(
    bottom_codes, mask_flags, top_codes, bottom_table, top_table, mask_vector, qkv_weight, out_weight, cotangent
):
    core, xh, xl = lax.axis_index("core"), lax.axis_index("xh"), lax.axis_index("xl")
    y, z = lax.axis_index("batch"), lax.axis_index("z")
    place = jnp.stack([2 * xh + core, core, xh, xl, y >> 1, y & 1, z]).astype(jnp.int32)
    grads = cotangent.reshape(TOKENS, MODEL)
    codes, up, left, diag = call(
        pack_kernel,
        [sds((TOKENS, CODES)), sds((64, WIDE)), sds((MSG, WIDE)), sds((16, WIDE))],
        (bottom_codes[0], mask_flags[0], top_codes[0], grads),
        [vmem()] * 4,
        2**28,
        3 * 2**20,
        limit=16,
        name="pack",
    )
    up, left, diag = shift(up, 1, 0), shift(left, 0, 1), shift(diag, 1, 1)
    tables = (bottom_table, top_table, mask_vector.reshape(1, MODEL), qkv_weight)
    own = call(
        own_kernel,
        [sds((OWN, MODEL)), sds((OWN, MODEL)), sds((OWN, 3 * HW))],
        (codes, *tables),
        [vmem()] * 5,
        2 * OWN * 1024 * 2560,
        9 * 2**20,
        limit=24,
        name="own",
    )
    emb, normed, proj, cot = call(
        halo_kernel,
        [sds((TOKENS, MODEL)), sds((TOKENS, MODEL)), sds((TOKENS, 3 * HW)), sds((TOKENS, MODEL))],
        (up, left, diag, grads, *own, *tables),
        [vmem()] * 11,
        2 * 176 * 1024 * 2560,
        12 * 2**20,
        limit=32,
        name="halo",
    )
    atts, gps, summed = [], [], []
    for c in range(CHUNKS):
        block = lambda i: pl.BlockSpec((TOKENS, CW), lambda g, i=i: (0, i))
        full = lambda *shape: pl.BlockSpec(shape, lambda g: (0,) * len(shape))
        att, gp, keep, send = pl.pallas_call(
            attend_kernel,
            grid=(1,),
            out_shape=[
                sds((TOKENS, CW)),
                sds((TOKENS, 3 * CW)),
                sds((2, 256, W), F32),
                sds((2, 256, W)),
            ],
            in_specs=[
                smem(),
                block(c),
                block(CHUNKS + c),
                block(2 * CHUNKS + c),
                full(TOKENS, MODEL),
                full(TOKENS, MODEL),
                pl.BlockSpec((MODEL, CW), lambda g, c=c: (0, c)),
            ],
            out_specs=[
                full(TOKENS, CW),
                full(TOKENS, 3 * CW),
                full(2, 256, W),
                full(2, 256, W),
            ],
            compiler_params=pltpu.CompilerParams(vmem_limit_bytes=28 * 2**20),
            cost_estimate=pl.CostEstimate(flops=3 * 2**30, bytes_accessed=8 * 2**20, transcendentals=2**19),
            name="attend",
        )(place, proj, proj, proj, normed, cot, out_weight)
        atts.append(att)
        gps.append(gp)
        summed += (sum_y_first if c else sum_x_first)(place, keep, send)
    both = call(
        finish_kernel,
        sds((2, TOKENS, MODEL)),
        (emb, cot, qkv_weight, out_weight, *atts, *gps),
        [vmem()] * 8,
        2 * TOKENS * 1024 * 2048,
        10 * 2**20,
        name="finish",
    )
    both = both.reshape(2, ROWS, COLS, MODEL)
    r_up = shift(both[:, :SHIFT], -1, 0)
    r_left = shift(both[:, SHIFT:, LATE:], 0, -1)
    r_diag = shift(both[:, :SHIFT, LATE:], -1, -1)

    def back(i):
        upper = jnp.concatenate([both[i, SHIFT:, :LATE], r_left[i]], axis=1)
        lower = jnp.concatenate([r_up[i, :, :LATE], r_diag[i]], axis=1)
        return jnp.concatenate([upper, lower], axis=0)[None]

    factor = 1.0 / math.sqrt(TOKENS * NB * NLAT * NLON)
    keep, send = halve(z_first, (4, 16, 2 * Q), place, *summed)
    keep, send = halve(z_second, (2, 16, 2 * Q), place, keep, swap(send, "z", 1))
    keep, send = halve(z_third, (16, 2 * Q), place, keep, swap(send, "z", 2))
    level = call(
        functools.partial(level_kernel, factor),
        sds((16, 2 * Q), F32),
        (keep, swap(send, "z", 4)),
        [vmem()] * 2,
        2**14,
        2**16,
        limit=16,
        name="level",
    )
    g_qkv, g_out = call(
        spread_kernel,
        [sds((16, 3 * HW), F32), sds((16, HW), F32)],
        (place, level, *[swap(level, "batch", d) for d in (1, 2, 3)]),
        [smem()] + [vmem()] * 4,
        2**15,
        2**18,
        limit=16,
        name="spread",
    )
    return (back(0), back(1), g_qkv, g_out)


def solution(mesh):
    devices = mesh.devices.reshape(NB, 2, 2, 8, 2)
    fine = jax.sharding.Mesh(devices, ("batch",) + GRID)
    rows, cols = ("xh", "core"), ("z", "xl")
    grid, whole = P("batch", rows, cols), P()
    return jax.shard_map(
        shards,
        mesh=fine,
        in_specs=(grid, grid, grid, whole, whole, whole, whole, whole, P("batch", rows, cols, None)),
        out_specs=(
            P("batch", rows, cols, None),
            P("batch", rows, cols, None),
            P(GRID, None),
            P(GRID, None),
        ),
        check_vma=False,
    )
```

```python
import functools
import math

import jax
import jax.numpy as jnp
from jax import lax
from jax.experimental import pallas as pl
from jax.experimental.pallas import tpu as pltpu
from jax.sharding import PartitionSpec as P

HEADS = 8
HDIM = 64
WIN = 8
HW = 512
SHIFT = 4
EPS = 1e-05
MODEL = 1024
ROWS, COLS = 32, 16
TOKENS = ROWS * COLS
BAND = WIN * COLS
BANDS = TOKENS // BAND
CHUNKS = 2
CW = HW // CHUNKS
F32 = jnp.float32
BF16 = jnp.bfloat16
GRID = ("xh", "core", "z", "xl")
NB, NLAT, NLON = 4, 4, 16


def dot(a, b, ca, cb):
    return lax.dot_general(a, b, (((ca,), (cb,)), ((), ())), preferred_element_type=F32)


def vmem():
    return pl.BlockSpec(memory_space=pltpu.VMEM)


def smem():
    return pl.BlockSpec(memory_space=pltpu.SMEM)


def call(kernel, outs, operands, specs, flops, nbytes, trans=0, limit=40, name=None, scratch=()):
    return pl.pallas_call(
        kernel,
        out_shape=outs,
        in_specs=specs,
        out_specs=jax.tree.map(lambda _: vmem(), outs),
        scratch_shapes=scratch,
        compiler_params=pltpu.CompilerParams(vmem_limit_bytes=limit * 2**20),
        cost_estimate=pl.CostEstimate(flops=flops, bytes_accessed=nbytes, transcendentals=trans),
        name=name,
    )(*operands)


def hbm():
    return pl.BlockSpec(memory_space=pltpu.HBM)


def sems(n):
    return pltpu.SemaphoreType.DMA((n,))


def sds(shape, dtype=BF16):
    return jax.ShapeDtypeStruct(shape, dtype)


def iota(shape, dim):
    return lax.broadcasted_iota(jnp.int32, shape, dim)


def moments(x):
    mean = jnp.mean(x, axis=1, keepdims=True)
    centred = x - mean
    inverse = lax.rsqrt(jnp.mean(centred * centred, axis=1, keepdims=True) + EPS)
    return centred, inverse


MSG = SHIFT * (ROWS - SHIFT)
OWN = (ROWS - SHIFT) * COLS
LATE = COLS - SHIFT


def hot(mask):
    return mask.astype(F32).astype(BF16)


def late_cells(cells, rows, by_row):
    dims = (0, 1) if by_row else (1, 0)
    shape = (rows, cells) if by_row else (cells, rows)
    m, t = iota(shape, dims[0]), iota(shape, dims[1])
    return hot(t == (m >> 2) * COLS + LATE + (m & 3))


def slice_kernel(cot, up, left, diag, held, sem):
    copy = pltpu.make_async_copy(cot, held, sem)
    copy.start()
    pick, corner = late_cells(OWN, MSG, True), late_cells(64, 16, True)
    copy.wait()
    up[...] = held[OWN:]
    left[...] = dot(pick, held[:OWN], 1, 0).astype(BF16)
    diag[...] = dot(corner, held[OWN:], 1, 0).astype(BF16)


def embed_kernel(own, up, left, diag, bt, tt, mv, wq, emb, normed, proj, tables, weight, sems):
    copies = [
        pltpu.make_async_copy(bt, tables.at[0], sems.at[0]),
        pltpu.make_async_copy(tt, tables.at[1], sems.at[1]),
        pltpu.make_async_copy(wq, weight, sems.at[2]),
    ]
    for copy in copies:
        copy.start()
    r, j = iota((80, 16), 0), iota((80, 16), 1)
    low = jnp.where(r >= 64, r - 50, r & 31) >= 28
    late = jnp.where(r >= 64, 2 * j, j) >= LATE
    grid = jnp.where(
        low,
        jnp.where(late, diag[...], up[...]),
        jnp.where(late, left[...], own[...]),
    )
    bottom = jnp.where(grid[32:64] == 1, 512, grid[0:32])
    upper = grid[64:80, 0:8]

    def column(codes, rows, row_of, lane_of):
        width = codes.shape[1]
        parts = jnp.concatenate([codes >> 4, codes & 15], axis=1).astype(F32).astype(BF16)
        pick = hot(row_of(iota((TOKENS, rows), 0)) == iota((TOKENS, rows), 1))
        spread = dot(pick, parts, 1, 0)
        t, lane = iota(spread.shape, 0), iota(spread.shape, 1)
        inside = jnp.where(lane < width, lane, lane - width) == lane_of(t)
        weight = jnp.where(lane < width, 16.0, 1.0)
        code = jnp.sum(jnp.where(inside, spread * weight, 0.0), axis=1, keepdims=True)
        return code.astype(jnp.int32)

    def source_row(t):
        return ((t >> 4) + (ROWS - SHIFT)) & (ROWS - 1)

    code_b = column(bottom, 32, source_row, lambda t: t & 15)
    code_t = column(upper, 16, lambda t: source_row(t) >> 1, lambda t: (t & 15) >> 1)
    copies[0].wait()
    copies[1].wait()
    for block in range(BANDS):
        here = slice(block * BAND, (block + 1) * BAND)
        cb, ct = code_b[here], code_t[here]
        lane = iota((BAND, 512), 1)
        x = dot(hot(lane == cb), tables[0], 1, 0)
        x = jnp.where(cb == 512, mv[...].astype(F32), x)
        x = (x + dot(hot(lane == ct), tables[1], 1, 0)).astype(BF16)
        emb[here] = x
        centred, inverse = moments(x.astype(F32))
        normed[here] = (centred * inverse).astype(BF16)
    copies[2].wait()
    for block in range(BANDS):
        here = slice(block * BAND, (block + 1) * BAND)
        proj[here] = dot(normed[here], weight[...], 1, 0).astype(BF16)


def merge(cot, grads, up, left, diag):
    p = iota((64, 1), 0) & 15
    corner = dot(late_cells(64, 16, False), diag[...], 1, 0)
    cot[0:64] = jnp.where(p >= LATE, corner, up[...].astype(F32)).astype(BF16)
    for at in range(0, OWN, 64):
        m, t = iota((64, MSG), 1), at + iota((64, MSG), 0)
        spread = hot(t == (m >> 2) * COLS + LATE + (m & 3))
        values = dot(spread, left[...], 1, 0)
        values = jnp.where(p >= LATE, values, grads[at : at + 64].astype(F32))
        cot[64 + at : 128 + at] = values.astype(BF16)


def attend_first(place, proj, normed, grads, up, left, diag, ow, att, gp, keep, send, cot, own, weight, sems):
    copies = [
        pltpu.make_async_copy(grads, own, sems.at[0]),
        pltpu.make_async_copy(ow.at[:, 0:CW], weight, sems.at[1]),
    ]
    for copy in copies:
        copy.start()
    copies[0].wait()
    merge(cot, own, up, left, diag)
    copies[1].wait()
    attend(0, place, proj, normed, cot, weight, att, gp, keep, send)


def attend_next(place, proj, normed, cot, ow, att, gp, keep, send, weight, sem):
    copy = pltpu.make_async_copy(ow.at[:, CW:], weight, sem)
    copy.start()
    copy.wait()
    attend(1, place, proj, normed, cot, weight, att, gp, keep, send)


def attend(chunk, place, proj, normed, cot, ow, att, gp, keep, send):
    grad = dot(cot[...], ow[...], 1, 0).astype(BF16)
    lane = iota((BAND, 128), 1) < 64
    tk, tq = iota((BAND, BAND), 0), iota((BAND, BAND), 1)

    def side(t):
        c = t & 15
        return ((c >= 4) & (c < 12)).astype(jnp.int32)

    same = side(tk) == side(tq)
    whole = (tk >> 6) == (tq >> 6)
    zero = jnp.zeros((BAND, BAND), F32)
    plain = jnp.where(same, zero, -1e30)
    first = jnp.where(whole | (place[0] != 0), plain, -1e30)

    def split(x):
        none = jnp.zeros_like(x)
        return jnp.concatenate([jnp.where(lane, x, none), jnp.where(lane, none, x)], axis=0)

    def pick(x):
        return jnp.where(lane, x[:BAND], x[BAND:])

    for b in range(BANDS):
        bias = first if b == 0 else plain
        here = slice(b * BAND, (b + 1) * BAND)
        for p in range(CW // 128):
            cols = slice(p * 128, (p + 1) * 128)
            first_col = chunk * CW + p * 128
            qq, kk, vv = (proj[here, i * HW + first_col : i * HW + first_col + 128] for i in range(3))
            kk, vv = split(kk), split(vv)
            da = grad[here, cols]
            s = dot(kk, qq, 1, 1).reshape(2, BAND, BAND) * 0.125 + bias
            e = jnp.exp(s - jnp.max(s, axis=1, keepdims=True))
            share = e * (1.0 / jnp.sum(e, axis=1, keepdims=True))
            sb = share.astype(BF16).reshape(2 * BAND, BAND)
            att[here, cols] = dot(sb, vv, 0, 0).astype(BF16)
            gs = dot(vv, da, 1, 1).reshape(2, BAND, BAND)
            delta = jnp.sum(share * gs, axis=1, keepdims=True)
            ds = (share * (gs - delta) * 0.125).astype(BF16).reshape(2 * BAND, BAND)
            at = p * 128
            gp[here, at : at + 128] = dot(ds, kk, 0, 0).astype(BF16)
            gp[here, CW + at : CW + at + 128] = pick(dot(ds, qq, 1, 0)).astype(BF16)
            gp[here, 2 * CW + at : 2 * CW + at + 128] = pick(dot(sb, da, 1, 0)).astype(BF16)

    core = place[1]
    for half in range(2):
        for out, flip in ((send, 1), (keep, 0)):
            cut = pl.ds(pl.multiple_of(half * 512 + (core ^ flip) * 256, 256), 256)
            out[half, :, 0 : 3 * CW] = dot(normed[:, cut], gp[...], 0, 0).astype(out.dtype)
            out[half, :, 3 * CW :] = dot(cot[:, cut], att[...], 0, 0).astype(out.dtype)


def finish_kernel(emb, cot, wq, ow, att0, att1, gp0, gp1, both, weight, last, sems):
    copies = [
        pltpu.make_async_copy(ow, last, sems.at[0]),
        pltpu.make_async_copy(wq, weight, sems.at[1]),
    ]
    for copy in copies:
        copy.start()
    for copy in copies:
        copy.wait()
    for block in range(BANDS):
        here = slice(block * BAND, (block + 1) * BAND)
        x = emb[here].astype(F32)
        att = jnp.concatenate([att0[here], att1[here]], axis=1)
        both[0, here] = (x + dot(att, last[...], 1, 1)).astype(BF16)
        g0, g1 = gp0[here], gp1[here]
        parts = []
        for i in range(3):
            parts += [g0[:, i * CW : (i + 1) * CW], g1[:, i * CW : (i + 1) * CW]]
        gst = dot(jnp.concatenate(parts, axis=1), weight[...], 1, 1)
        centred, inverse = moments(x)
        standard = centred * inverse
        m1 = jnp.mean(gst, axis=1, keepdims=True)
        m2 = jnp.mean(gst * standard, axis=1, keepdims=True)
        both[1, here] = (cot[here].astype(F32) + inverse * (gst - m1 - standard * m2)).astype(BF16)


W = 4 * CW
Q = W // 4


def parity_core(place, a, b, keep, send):
    g = place[2] ^ place[3]
    for u in range(2):
        for out, v in ((keep, u ^ g), (send, u ^ g ^ 1)):
            out[u] = (a[u, :, v] + b[u, :, v].astype(F32)).astype(out.dtype)


def parity_pair(place, a, b, keep, send):
    for out, u in ((keep, place[2]), (send, place[2] ^ 1)):
        out[...] = (a[u] + b[u].astype(F32)).astype(out.dtype)


def high_core(place, a, b, keep, send):
    for out, u in ((keep, place[2]), (send, place[2] ^ 1)):
        for v in range(2):
            out[v] = (a[u, :, v] + b[u, :, v].astype(F32)).astype(out.dtype)


def high_pair(place, a, b, keep, send):
    for out, v in ((keep, place[3]), (send, place[3] ^ 1)):
        out[...] = (a[v] + b[v].astype(F32)).astype(out.dtype)


def join_kernel(a, b, c, d, out):
    out[:, :, 0:W] = (a[...] + b[...].astype(F32)).astype(BF16)
    out[:, :, W:] = (c[...] + d[...].astype(F32)).astype(BF16)


def depth_kernel(ref, keep, send):
    total = sum(ref[i].astype(F32) for i in range(8))
    keep[...] = total
    send[...] = total.astype(BF16)


def level_kernel(factor, own, *refs):
    qkv, outw = refs[3:]
    total = (own[...] + sum(r[...].astype(F32) for r in refs[:3])) * factor
    for c in range(CHUNKS):
        for i in range(3):
            qkv[:, i * HW + c * CW : i * HW + (c + 1) * CW] = total[:, c * W + i * Q : c * W + (i + 1) * Q]
        outw[:, c * CW : (c + 1) * CW] = total[:, c * W + 3 * Q : (c + 1) * W]


def permute(x, where):
    pairs = []
    for la in range(NLAT):
        for lo in range(NLON):
            tl, to = where(la, lo)
            pairs.append((la * NLON + lo, tl * NLON + to))
    return lax.ppermute(x, GRID, pairs)


def shift(x, down, right):
    return permute(x, lambda la, lo: ((la + down) % NLAT, (lo + right) % NLON))


def swap(x, axis, flip):
    return lax.ppermute(x, axis, [(i, i ^ flip) for i in range(lax.axis_size(axis))])


def swap_x(x, flip):
    return permute(x, lambda la, lo: (la ^ (flip & 2), lo ^ (flip & 1)))


def halve(kernel, shape, place, *terms):
    size = math.prod(shape)
    return call(
        kernel,
        [sds(shape, F32), sds(shape)],
        (place, *terms),
        [smem()] + [vmem()] * len(terms),
        2 * size,
        16 * size,
        limit=16,
        name=kernel.__name__,
    )


def sum_x(place, keep, send, order):
    fold = (2, 8, 2, 16, W)
    core, pair = (parity_core, parity_pair) if order[0] == 1 else (high_core, high_pair)
    recv = swap(send, "core", 1)
    keep, send = halve(core, (2, 8, 16, W), place, keep.reshape(fold), recv.reshape(fold))
    keep, send = halve(pair, (8, 16, W), place, keep, swap_x(send, order[0]))
    return [keep, swap_x(send, order[1])]


def shards(
    bottom_codes, mask_flags, top_codes, bottom_table, top_table, mask_vector, qkv_weight, out_weight, cotangent
):
    core, xh, xl = lax.axis_index("core"), lax.axis_index("xh"), lax.axis_index("xl")
    place = jnp.stack([2 * xh + core, core, xh, xl]).astype(jnp.int32)
    own = jnp.concatenate(
        [bottom_codes[0], mask_flags[0], jnp.pad(top_codes[0], ((0, 0), (0, 8)))], axis=0
    )
    near = (own, shift(own, 1, 0), shift(own, 0, 1), shift(own, 1, 1))
    pin = lambda x: pltpu.with_memory_space_constraint(x, pltpu.HBM)
    grads = pin(cotangent.reshape(TOKENS, MODEL))
    bottom_table, top_table = pin(bottom_table), pin(top_table)
    qkv_weight, out_weight = pin(qkv_weight), pin(out_weight)
    up, left, diag = call(
        slice_kernel,
        [sds((64, MODEL)), sds((MSG, MODEL)), sds((16, MODEL))],
        (grads,),
        [hbm()],
        2**28,
        2**21,
        name="slices",
        scratch=[pltpu.VMEM((TOKENS, MODEL), BF16), pltpu.SemaphoreType.DMA],
    )
    up, left, diag = shift(up, 1, 0), shift(left, 0, 1), shift(diag, 1, 1)
    emb, normed, proj = call(
        embed_kernel,
        [sds((TOKENS, MODEL)), sds((TOKENS, MODEL)), sds((TOKENS, 3 * HW))],
        (*near, bottom_table, top_table, mask_vector.reshape(1, MODEL), qkv_weight),
        [vmem()] * 4 + [hbm(), hbm(), vmem(), hbm()],
        2 * TOKENS * 1024 * 2560,
        9 * 2**20,
        name="embed",
        scratch=[pltpu.VMEM((2, 512, MODEL), BF16), pltpu.VMEM((MODEL, 3 * HW), BF16), sems(3)],
    )
    outs = [sds((TOKENS, CW)), sds((TOKENS, 3 * CW)), sds((2, 256, W), F32), sds((2, 256, W))]
    column = pltpu.VMEM((MODEL, CW), BF16)
    att0, gp0, keep0, send0, cot = call(
        attend_first,
        outs + [sds((TOKENS, MODEL))],
        (place, proj, normed, grads, up, left, diag, out_weight),
        [smem(), vmem(), vmem(), hbm(), vmem(), vmem(), vmem(), hbm()],
        3 * 2**30,
        8 * 2**20,
        2**19,
        name="attend",
        scratch=[pltpu.VMEM((TOKENS, MODEL), BF16), column, sems(2)],
    )
    att1, gp1, keep1, send1 = call(
        attend_next,
        outs,
        (place, proj, normed, cot, out_weight),
        [smem(), vmem(), vmem(), vmem(), hbm()],
        3 * 2**30,
        8 * 2**20,
        2**19,
        name="attend",
        scratch=[column, pltpu.SemaphoreType.DMA],
    )
    summed = sum_x(place, keep0, send0, (1, 3)) + sum_x(place, keep1, send1, (3, 1))
    both = call(
        finish_kernel,
        sds((2, TOKENS, MODEL)),
        (emb, cot, qkv_weight, out_weight, att0, att1, gp0, gp1),
        [vmem(), vmem(), hbm(), hbm()] + [vmem()] * 4,
        2 * TOKENS * 1024 * 2048,
        10 * 2**20,
        name="finish",
        scratch=[pltpu.VMEM((MODEL, 3 * HW), BF16), pltpu.VMEM((MODEL, HW), BF16), sems(2)],
    )
    both = both.reshape(2, ROWS, COLS, MODEL)
    r_up = shift(both[:, :SHIFT], -1, 0)
    r_left = shift(both[:, SHIFT:, LATE:], 0, -1)
    r_diag = shift(both[:, :SHIFT, LATE:], -1, -1)

    def back(i):
        upper = jnp.concatenate([both[i, SHIFT:, :LATE], r_left[i]], axis=1)
        lower = jnp.concatenate([r_up[i, :, :LATE], r_diag[i]], axis=1)
        return jnp.concatenate([upper, lower], axis=0)[None]

    factor = 1.0 / math.sqrt(TOKENS * NB * NLAT * NLON)
    joined = call(
        join_kernel, sds((8, 16, 2 * W)), summed, [vmem()] * 4, 2**19, 2**21, limit=16, name="join"
    )
    depth = lax.all_to_all(joined, "z", 0, 0, tiled=True)
    keep, send = call(
        depth_kernel,
        [sds((16, 2 * W), F32), sds((16, 2 * W))],
        (depth,),
        [vmem()],
        2**18,
        2**20,
        limit=16,
        name="depth",
    )
    g_qkv, g_out = call(
        functools.partial(level_kernel, factor),
        [sds((16, 3 * HW), F32), sds((16, HW), F32)],
        (keep, *[swap(send, "batch", d) for d in (1, 2, 3)]),
        [vmem()] * 4,
        2**17,
        2**19,
        limit=16,
        name="level",
    )
    return (back(0), back(1), g_qkv, g_out)


def solution(mesh):
    devices = mesh.devices.reshape(NB, 2, 2, 8, 2)
    fine = jax.sharding.Mesh(devices, ("batch",) + GRID)
    rows, cols = ("xh", "core"), ("z", "xl")
    grid, whole = P("batch", rows, cols), P()
    return jax.shard_map(
        shards,
        mesh=fine,
        in_specs=(grid, grid, grid, whole, whole, whole, whole, whole, P("batch", rows, cols, None)),
        out_specs=(
            P("batch", rows, cols, None),
            P("batch", rows, cols, None),
            P(GRID, None),
            P(GRID, None),
        ),
        check_vma=False,
    )
```

```python
import functools
import math

import jax
import jax.numpy as jnp
from jax import lax
from jax.experimental import pallas as pl
from jax.experimental.pallas import tpu as pltpu
from jax.sharding import PartitionSpec as P

HEADS = 8
HDIM = 64
WIN = 8
HW = 512
SHIFT = 4
EPS = 1e-05
MODEL = 1024
ROWS, COLS = 32, 16
TOKENS = ROWS * COLS
BAND = WIN * COLS
BANDS = TOKENS // BAND
CHUNKS = 2
CW = HW // CHUNKS
F32 = jnp.float32
BF16 = jnp.bfloat16
GRID = ("xh", "core", "z", "xl")
NB, NLAT, NLON = 4, 4, 16


def dot(a, b, ca, cb):
    return lax.dot_general(a, b, (((ca,), (cb,)), ((), ())), preferred_element_type=F32)


def vmem():
    return pl.BlockSpec(memory_space=pltpu.VMEM)


def smem():
    return pl.BlockSpec(memory_space=pltpu.SMEM)


def call(kernel, outs, operands, specs, flops, nbytes, trans=0, limit=40, name=None, scratch=()):
    return pl.pallas_call(
        kernel,
        out_shape=outs,
        in_specs=specs,
        out_specs=jax.tree.map(lambda _: vmem(), outs),
        scratch_shapes=scratch,
        compiler_params=pltpu.CompilerParams(vmem_limit_bytes=limit * 2**20),
        cost_estimate=pl.CostEstimate(flops=flops, bytes_accessed=nbytes, transcendentals=trans),
        name=name,
    )(*operands)


def hbm():
    return pl.BlockSpec(memory_space=pltpu.HBM)


def sems(n):
    return pltpu.SemaphoreType.DMA((n,))


def sds(shape, dtype=BF16):
    return jax.ShapeDtypeStruct(shape, dtype)


def iota(shape, dim):
    return lax.broadcasted_iota(jnp.int32, shape, dim)


def moments(x):
    mean = jnp.mean(x, axis=1, keepdims=True)
    centred = x - mean
    inverse = lax.rsqrt(jnp.mean(centred * centred, axis=1, keepdims=True) + EPS)
    return centred, inverse


MSG = SHIFT * (ROWS - SHIFT)
OWN = (ROWS - SHIFT) * COLS
LATE = COLS - SHIFT


def hot(mask):
    return mask.astype(F32).astype(BF16)


def late_cells(cells, rows, by_row):
    dims = (0, 1) if by_row else (1, 0)
    shape = (rows, cells) if by_row else (cells, rows)
    m, t = iota(shape, dims[0]), iota(shape, dims[1])
    return hot(t == (m >> 2) * COLS + LATE + (m & 3))


def slice_kernel(cot, up, left, diag, held, sem):
    copy = pltpu.make_async_copy(cot, held, sem)
    copy.start()
    pick, corner = late_cells(OWN, MSG, True), late_cells(64, 16, True)
    copy.wait()
    up[...] = held[OWN:]
    left[...] = dot(pick, held[:OWN], 1, 0).astype(BF16)
    diag[...] = dot(corner, held[OWN:], 1, 0).astype(BF16)


def embed_kernel(own, up, left, diag, bt, tt, mv, wq, emb, normed, proj, tables, weight, sems):
    copies = [
        pltpu.make_async_copy(bt, tables.at[0], sems.at[0]),
        pltpu.make_async_copy(tt, tables.at[1], sems.at[1]),
        pltpu.make_async_copy(wq, weight, sems.at[2]),
    ]
    for copy in copies:
        copy.start()
    r, j = iota((80, 16), 0), iota((80, 16), 1)
    low = jnp.where(r >= 64, r - 50, r & 31) >= 28
    late = jnp.where(r >= 64, 2 * j, j) >= LATE
    grid = jnp.where(
        low,
        jnp.where(late, diag[...], up[...]),
        jnp.where(late, left[...], own[...]),
    )
    bottom = jnp.where(grid[32:64] == 1, 512, grid[0:32])
    upper = grid[64:80, 0:8]

    def column(codes, rows, row_of, lane_of):
        width = codes.shape[1]
        parts = jnp.concatenate([codes >> 4, codes & 15], axis=1).astype(F32).astype(BF16)
        pick = hot(row_of(iota((TOKENS, rows), 0)) == iota((TOKENS, rows), 1))
        spread = dot(pick, parts, 1, 0)
        t, lane = iota(spread.shape, 0), iota(spread.shape, 1)
        inside = jnp.where(lane < width, lane, lane - width) == lane_of(t)
        weight = jnp.where(lane < width, 16.0, 1.0)
        code = jnp.sum(jnp.where(inside, spread * weight, 0.0), axis=1, keepdims=True)
        return code.astype(jnp.int32)

    def source_row(t):
        return ((t >> 4) + (ROWS - SHIFT)) & (ROWS - 1)

    code_b = column(bottom, 32, source_row, lambda t: t & 15)
    code_t = column(upper, 16, lambda t: source_row(t) >> 1, lambda t: (t & 15) >> 1)
    copies[0].wait()
    copies[1].wait()
    for block in range(BANDS):
        here = slice(block * BAND, (block + 1) * BAND)
        cb, ct = code_b[here], code_t[here]
        lane = iota((BAND, 512), 1)
        x = dot(hot(lane == cb), tables[0], 1, 0)
        x = jnp.where(cb == 512, mv[...].astype(F32).reshape(1, MODEL), x)
        x = (x + dot(hot(lane == ct), tables[1], 1, 0)).astype(BF16)
        emb[here] = x
        centred, inverse = moments(x.astype(F32))
        normed[here] = (centred * inverse).astype(BF16)
    copies[2].wait()
    for block in range(BANDS):
        here = slice(block * BAND, (block + 1) * BAND)
        proj[here] = dot(normed[here], weight[...], 1, 0).astype(BF16)


def merge(cot, grads, up, left, diag):
    p = iota((64, 1), 0) & 15
    corner = dot(late_cells(64, 16, False), diag[...], 1, 0)
    cot[0:64] = jnp.where(p >= LATE, corner, up[...].astype(F32)).astype(BF16)
    for at in range(0, OWN, 64):
        m, t = iota((64, MSG), 1), at + iota((64, MSG), 0)
        spread = hot(t == (m >> 2) * COLS + LATE + (m & 3))
        values = dot(spread, left[...], 1, 0)
        values = jnp.where(p >= LATE, values, grads[at : at + 64].astype(F32))
        cot[64 + at : 128 + at] = values.astype(BF16)


def attend_first(place, proj, normed, grads, up, left, diag, ow, att, gp, keep, send, cot, own, weight, sems):
    copies = [
        pltpu.make_async_copy(grads, own, sems.at[0]),
        pltpu.make_async_copy(ow.at[:, 0:CW], weight, sems.at[1]),
    ]
    for copy in copies:
        copy.start()
    copies[0].wait()
    merge(cot, own, up, left, diag)
    copies[1].wait()
    attend(0, place, proj, normed, cot, weight, att, gp, keep, send)


def attend_next(place, proj, normed, cot, ow, att, gp, keep, send, weight, sem):
    copy = pltpu.make_async_copy(ow.at[:, CW:], weight, sem)
    copy.start()
    copy.wait()
    attend(1, place, proj, normed, cot, weight, att, gp, keep, send)


def attend(chunk, place, proj, normed, cot, ow, att, gp, keep, send):
    grad = dot(cot[...], ow[...], 1, 0).astype(BF16)
    lane = iota((BAND, 128), 1) < 64
    tk, tq = iota((BAND, BAND), 0), iota((BAND, BAND), 1)

    def side(t):
        c = t & 15
        return ((c >= 4) & (c < 12)).astype(jnp.int32)

    same = side(tk) == side(tq)
    whole = (tk >> 6) == (tq >> 6)
    zero = jnp.zeros((BAND, BAND), F32)
    plain = jnp.where(same, zero, -1e30)
    first = jnp.where(whole | (place[0] != 0), plain, -1e30)

    def split(x):
        none = jnp.zeros_like(x)
        return jnp.concatenate([jnp.where(lane, x, none), jnp.where(lane, none, x)], axis=0)

    def pick(x):
        return jnp.where(lane, x[:BAND], x[BAND:])

    for b in range(BANDS):
        bias = first if b == 0 else plain
        here = slice(b * BAND, (b + 1) * BAND)
        for p in range(CW // 128):
            cols = slice(p * 128, (p + 1) * 128)
            first_col = chunk * CW + p * 128
            qq, kk, vv = (proj[here, i * HW + first_col : i * HW + first_col + 128] for i in range(3))
            kk, vv = split(kk), split(vv)
            da = grad[here, cols]
            s = dot(kk, qq, 1, 1).reshape(2, BAND, BAND) * 0.125 + bias
            e = jnp.exp(s - jnp.max(s, axis=1, keepdims=True))
            share = e * (1.0 / jnp.sum(e, axis=1, keepdims=True))
            sb = share.astype(BF16).reshape(2 * BAND, BAND)
            att[here, cols] = dot(sb, vv, 0, 0).astype(BF16)
            gs = dot(vv, da, 1, 1).reshape(2, BAND, BAND)
            delta = jnp.sum(share * gs, axis=1, keepdims=True)
            ds = (share * (gs - delta) * 0.125).astype(BF16).reshape(2 * BAND, BAND)
            at = p * 128
            gp[here, at : at + 128] = dot(ds, kk, 0, 0).astype(BF16)
            gp[here, CW + at : CW + at + 128] = pick(dot(ds, qq, 1, 0)).astype(BF16)
            gp[here, 2 * CW + at : 2 * CW + at + 128] = pick(dot(sb, da, 1, 0)).astype(BF16)

    core = place[1]
    for half in range(2):
        for out, flip in ((send, 1), (keep, 0)):
            cut = pl.ds(pl.multiple_of(half * 512 + (core ^ flip) * 256, 256), 256)
            out[half, :, 0 : 3 * CW] = dot(normed[:, cut], gp[...], 0, 0).astype(out.dtype)
            out[half, :, 3 * CW :] = dot(cot[:, cut], att[...], 0, 0).astype(out.dtype)


def finish_kernel(emb, cot, wq, ow, att0, att1, gp0, gp1, mid, up, left, diag, tick, weight, last, sems):
    copies = [
        pltpu.make_async_copy(ow, last, sems.at[0]),
        pltpu.make_async_copy(wq, weight, sems.at[1]),
    ]
    for copy in copies:
        copy.start()
    copies[0].wait()

    def put(i, block, values):
        if block == 0:
            up[i] = values[:64]
            mid[i, 0:64] = values[64:]
        else:
            at = block * BAND - 64
            mid[i, at : at + BAND] = values

    for block in range(BANDS):
        here = slice(block * BAND, (block + 1) * BAND)
        att = jnp.concatenate([att0[here], att1[here]], axis=1)
        put(0, block, (emb[here].astype(F32) + dot(att, last[...], 1, 1)).astype(BF16))
    copies[1].wait()
    for block in range(BANDS):
        here = slice(block * BAND, (block + 1) * BAND)
        g0, g1 = gp0[here], gp1[here]
        parts = []
        for i in range(3):
            parts += [g0[:, i * CW : (i + 1) * CW], g1[:, i * CW : (i + 1) * CW]]
        gst = dot(jnp.concatenate(parts, axis=1), weight[...], 1, 1)
        centred, inverse = moments(emb[here].astype(F32))
        standard = centred * inverse
        m1 = jnp.mean(gst, axis=1, keepdims=True)
        m2 = jnp.mean(gst * standard, axis=1, keepdims=True)
        values = cot[here].astype(F32) + inverse * (gst - m1 - standard * m2)
        put(1, block, values.astype(BF16))
    pick, corner = late_cells(OWN, MSG, True), late_cells(64, 16, True)
    for i in range(2):
        left[i] = dot(pick, mid[i], 1, 0).astype(BF16)
        diag[i] = dot(corner, up[i], 1, 0).astype(BF16)
    tick[...] = jnp.zeros(tick.shape, F32)


def place_kernel(mid, up, left, diag, out, gin):
    late = (iota((64, 1), 0) & 15) >= LATE
    corner = late_cells(64, 16, False)
    for i, ref in enumerate((out, gin)):
        ref[OWN:] = jnp.where(late, dot(corner, diag[i], 1, 0), up[i].astype(F32)).astype(BF16)
        for at in range(0, OWN, 64):
            m, t = iota((64, MSG), 1), at + iota((64, MSG), 0)
            spread = hot(t == (m >> 2) * COLS + LATE + (m & 3))
            values = dot(spread, left[i], 1, 0)
            ref[at : at + 64] = jnp.where(late, values, mid[i, at : at + 64].astype(F32)).astype(BF16)


W = 4 * CW
Q = W // 4


def parity_core(place, a, b, keep, send):
    g = place[2] ^ place[3]
    for u in range(2):
        for out, v in ((keep, u ^ g), (send, u ^ g ^ 1)):
            out[u] = (a[u, :, v] + b[u, :, v].astype(F32)).astype(out.dtype)


def parity_pair(place, a, b, tick, keep, send):
    for out, u in ((keep, place[2]), (send, place[2] ^ 1)):
        out[...] = (a[u] + b[u].astype(F32)).astype(out.dtype)


def high_core(place, a, b, keep, send):
    for out, u in ((keep, place[2]), (send, place[2] ^ 1)):
        for v in range(2):
            out[v] = (a[u, :, v] + b[u, :, v].astype(F32)).astype(out.dtype)


def high_pair(place, a, b, tick, keep, send):
    for out, v in ((keep, place[3]), (send, place[3] ^ 1)):
        out[...] = (a[v] + b[v].astype(F32)).astype(out.dtype)


def join_kernel(a, b, c, d, out):
    out[:, :, 0:W] = (a[...] + b[...].astype(F32)).astype(BF16)
    out[:, :, W:] = (c[...] + d[...].astype(F32)).astype(BF16)


def depth_kernel(ref, keep, send):
    total = sum(ref[i].astype(F32) for i in range(8))
    keep[...] = total
    send[...] = total.astype(BF16)


def level_kernel(factor, own, *refs):
    qkv, outw = refs[3:]
    total = (own[...] + sum(r[...].astype(F32) for r in refs[:3])) * factor
    for c in range(CHUNKS):
        for i in range(3):
            qkv[:, i * HW + c * CW : i * HW + (c + 1) * CW] = total[:, c * W + i * Q : c * W + (i + 1) * Q]
        outw[:, c * CW : (c + 1) * CW] = total[:, c * W + 3 * Q : (c + 1) * W]


def permute(x, where):
    pairs = []
    for la in range(NLAT):
        for lo in range(NLON):
            tl, to = where(la, lo)
            pairs.append((la * NLON + lo, tl * NLON + to))
    return lax.ppermute(x, GRID, pairs)


def shift(x, down, right):
    return permute(x, lambda la, lo: ((la + down) % NLAT, (lo + right) % NLON))


def swap(x, axis, flip):
    return lax.ppermute(x, axis, [(i, i ^ flip) for i in range(lax.axis_size(axis))])


def swap_x(x, flip):
    return permute(x, lambda la, lo: (la ^ (flip & 2), lo ^ (flip & 1)))


def halve(kernel, shape, place, *terms):
    size = math.prod(shape)
    return call(
        kernel,
        [sds(shape, F32), sds(shape)],
        (place, *terms),
        [smem()] + [vmem()] * len(terms),
        2 * size,
        16 * size,
        limit=16,
        name=kernel.__name__,
    )


def sum_x(place, keep, send, tick, order):
    fold = (2, 8, 2, 16, W)
    core, pair = (parity_core, parity_pair) if order[0] == 1 else (high_core, high_pair)
    recv = swap(send, "core", 1)
    keep, send = halve(core, (2, 8, 16, W), place, keep.reshape(fold), recv.reshape(fold))
    keep, send = halve(pair, (8, 16, W), place, keep, swap_x(send, order[0]), tick)
    return [keep, swap_x(send, order[1])]


def shards(
    bottom_codes, mask_flags, top_codes, bottom_table, top_table, mask_vector, qkv_weight, out_weight, cotangent
):
    core, xh, xl = lax.axis_index("core"), lax.axis_index("xh"), lax.axis_index("xl")
    place = jnp.stack([2 * xh + core, core, xh, xl]).astype(jnp.int32)
    own = jnp.concatenate(
        [bottom_codes[0], mask_flags[0], jnp.pad(top_codes[0], ((0, 0), (0, 8)))], axis=0
    )
    near = (own, shift(own, 1, 0), shift(own, 0, 1), shift(own, 1, 1))
    pin = lambda x: pltpu.with_memory_space_constraint(x, pltpu.HBM)
    grads = pin(cotangent.reshape(TOKENS, MODEL))
    bottom_table, top_table = pin(bottom_table), pin(top_table)
    qkv_weight, out_weight = pin(qkv_weight), pin(out_weight)
    up, left, diag = call(
        slice_kernel,
        [sds((64, MODEL)), sds((MSG, MODEL)), sds((16, MODEL))],
        (grads,),
        [hbm()],
        2**28,
        2**21,
        name="slices",
        scratch=[pltpu.VMEM((TOKENS, MODEL), BF16), pltpu.SemaphoreType.DMA],
    )
    up, left, diag = shift(up, 1, 0), shift(left, 0, 1), shift(diag, 1, 1)
    emb, normed, proj = call(
        embed_kernel,
        [sds((TOKENS, MODEL)), sds((TOKENS, MODEL)), sds((TOKENS, 3 * HW))],
        (*near, bottom_table, top_table, mask_vector, qkv_weight),
        [vmem()] * 4 + [hbm(), hbm(), vmem(), hbm()],
        2 * TOKENS * 1024 * 2560,
        9 * 2**20,
        name="embed",
        scratch=[pltpu.VMEM((2, 512, MODEL), BF16), pltpu.VMEM((MODEL, 3 * HW), BF16), sems(3)],
    )
    outs = [sds((TOKENS, CW)), sds((TOKENS, 3 * CW)), sds((2, 256, W), F32), sds((2, 256, W))]
    column = pltpu.VMEM((MODEL, CW), BF16)
    att0, gp0, keep0, send0, cot = call(
        attend_first,
        outs + [sds((TOKENS, MODEL))],
        (place, proj, normed, grads, up, left, diag, out_weight),
        [smem(), vmem(), vmem(), hbm(), vmem(), vmem(), vmem(), hbm()],
        3 * 2**30,
        8 * 2**20,
        2**19,
        name="attend",
        scratch=[pltpu.VMEM((TOKENS, MODEL), BF16), column, sems(2)],
    )
    att1, gp1, keep1, send1 = call(
        attend_next,
        outs,
        (place, proj, normed, cot, out_weight),
        [smem(), vmem(), vmem(), vmem(), hbm()],
        3 * 2**30,
        8 * 2**20,
        2**19,
        name="attend",
        scratch=[column, pltpu.SemaphoreType.DMA],
    )
    *sent, tick = call(
        finish_kernel,
        [sds((2, OWN, MODEL)), sds((2, 64, MODEL)), sds((2, MSG, MODEL)), sds((2, 16, MODEL)), sds((8, 128), F32)],
        (emb, cot, qkv_weight, out_weight, att0, att1, gp0, gp1),
        [vmem(), vmem(), hbm(), hbm()] + [vmem()] * 4,
        2 * TOKENS * 1024 * 2048,
        10 * 2**20,
        name="finish",
        scratch=[pltpu.VMEM((MODEL, 3 * HW), BF16), pltpu.VMEM((MODEL, HW), BF16), sems(2)],
    )
    summed = sum_x(place, keep0, send0, tick, (1, 3)) + sum_x(place, keep1, send1, tick, (3, 1))
    mid, up, left, diag = sent
    up, left, diag = shift(up, -1, 0), shift(left, 0, -1), shift(diag, -1, -1)
    out, gin = call(
        place_kernel,
        [sds((TOKENS, MODEL))] * 2,
        (mid, up, left, diag),
        [vmem()] * 4,
        2**28,
        5 * 2**20,
        limit=24,
        name="place",
    )
    factor = 1.0 / math.sqrt(TOKENS * NB * NLAT * NLON)
    joined = call(
        join_kernel, sds((8, 16, 2 * W)), summed, [vmem()] * 4, 2**19, 2**21, limit=16, name="join"
    )
    depth = lax.all_to_all(joined, "z", 0, 0, tiled=True)
    keep, send = call(
        depth_kernel,
        [sds((16, 2 * W), F32), sds((16, 2 * W))],
        (depth,),
        [vmem()],
        2**18,
        2**20,
        limit=16,
        name="depth",
    )
    g_qkv, g_out = call(
        functools.partial(level_kernel, factor),
        [sds((16, 3 * HW), F32), sds((16, HW), F32)],
        (keep, *[swap(send, "batch", d) for d in (1, 2, 3)]),
        [vmem()] * 4,
        2**17,
        2**19,
        limit=16,
        name="level",
    )
    shape = (1, ROWS, COLS, MODEL)
    return (out.reshape(shape), gin.reshape(shape), g_qkv, g_out)


def solution(mesh):
    devices = mesh.devices.reshape(NB, 2, 2, 8, 2)
    fine = jax.sharding.Mesh(devices, ("batch",) + GRID)
    rows, cols = ("xh", "core"), ("z", "xl")
    grid, whole = P("batch", rows, cols), P()
    return jax.shard_map(
        shards,
        mesh=fine,
        in_specs=(grid, grid, grid, whole, whole, whole, whole, whole, P("batch", rows, cols, None)),
        out_specs=(
            P("batch", rows, cols, None),
            P("batch", rows, cols, None),
            P(GRID, None),
            P(GRID, None),
        ),
        check_vma=False,
    )
```

```python
import functools
import math

import jax
import jax.numpy as jnp
from jax import lax
from jax.experimental import pallas as pl
from jax.experimental.pallas import tpu as pltpu
from jax.sharding import PartitionSpec as P

HEADS = 8
HDIM = 64
WIN = 8
HW = 512
SHIFT = 4
EPS = 1e-05
MODEL = 1024
ROWS, COLS = 32, 16
TOKENS = ROWS * COLS
BAND = WIN * COLS
BANDS = TOKENS // BAND
CHUNKS = 2
CW = HW // CHUNKS
F32 = jnp.float32
BF16 = jnp.bfloat16
GRID = ("xh", "core", "z", "xl")
NB, NLAT, NLON = 4, 4, 16


def dot(a, b, ca, cb):
    return lax.dot_general(a, b, (((ca,), (cb,)), ((), ())), preferred_element_type=F32)


def vmem():
    return pl.BlockSpec(memory_space=pltpu.VMEM)


def smem():
    return pl.BlockSpec(memory_space=pltpu.SMEM)


def call(kernel, outs, operands, specs, flops, nbytes, trans=0, limit=40, name=None, scratch=()):
    return pl.pallas_call(
        kernel,
        out_shape=outs,
        in_specs=specs,
        out_specs=jax.tree.map(lambda _: vmem(), outs),
        scratch_shapes=scratch,
        compiler_params=pltpu.CompilerParams(vmem_limit_bytes=limit * 2**20),
        cost_estimate=pl.CostEstimate(flops=flops, bytes_accessed=nbytes, transcendentals=trans),
        name=name,
    )(*operands)


def hbm():
    return pl.BlockSpec(memory_space=pltpu.HBM)


def sems(n):
    return pltpu.SemaphoreType.DMA((n,))


def sds(shape, dtype=BF16):
    return jax.ShapeDtypeStruct(shape, dtype)


def iota(shape, dim):
    return lax.broadcasted_iota(jnp.int32, shape, dim)


def moments(x):
    mean = jnp.mean(x, axis=1, keepdims=True)
    centred = x - mean
    inverse = lax.rsqrt(jnp.mean(centred * centred, axis=1, keepdims=True) + EPS)
    return centred, inverse


MSG = SHIFT * (ROWS - SHIFT)
OWN = (ROWS - SHIFT) * COLS
LATE = COLS - SHIFT


def hot(mask):
    return mask.astype(F32).astype(BF16)


def late_cells(cells, rows, by_row):
    dims = (0, 1) if by_row else (1, 0)
    shape = (rows, cells) if by_row else (cells, rows)
    m, t = iota(shape, dims[0]), iota(shape, dims[1])
    return hot(t == (m >> 2) * COLS + LATE + (m & 3))


def slice_kernel(cot, up, left, diag, held, sem):
    copy = pltpu.make_async_copy(cot, held, sem)
    copy.start()
    pick, corner = late_cells(OWN, MSG, True), late_cells(64, 16, True)
    copy.wait()
    up[...] = held[OWN:]
    left[...] = dot(pick, held[:OWN], 1, 0).astype(BF16)
    diag[...] = dot(corner, held[OWN:], 1, 0).astype(BF16)


def embed_kernel(own, up, left, diag, bt, tt, mv, wq, emb, normed, proj, tables, weight, sems):
    copies = [
        pltpu.make_async_copy(bt, tables.at[0], sems.at[0]),
        pltpu.make_async_copy(tt, tables.at[1], sems.at[1]),
        pltpu.make_async_copy(wq, weight, sems.at[2]),
    ]
    for copy in copies:
        copy.start()
    r, j = iota((80, 16), 0), iota((80, 16), 1)
    low = jnp.where(r >= 64, r - 50, r & 31) >= 28
    late = jnp.where(r >= 64, 2 * j, j) >= LATE
    grid = jnp.where(
        low,
        jnp.where(late, diag[...], up[...]),
        jnp.where(late, left[...], own[...]),
    )
    bottom = jnp.where(grid[32:64] == 1, 512, grid[0:32])
    upper = grid[64:80, 0:8]

    def column(codes, rows, row_of, lane_of):
        width = codes.shape[1]
        parts = jnp.concatenate([codes >> 4, codes & 15], axis=1).astype(F32).astype(BF16)
        pick = hot(row_of(iota((TOKENS, rows), 0)) == iota((TOKENS, rows), 1))
        spread = dot(pick, parts, 1, 0)
        t, lane = iota(spread.shape, 0), iota(spread.shape, 1)
        inside = jnp.where(lane < width, lane, lane - width) == lane_of(t)
        weight = jnp.where(lane < width, 16.0, 1.0)
        code = jnp.sum(jnp.where(inside, spread * weight, 0.0), axis=1, keepdims=True)
        return code.astype(jnp.int32)

    def source_row(t):
        return ((t >> 4) + (ROWS - SHIFT)) & (ROWS - 1)

    code_b = column(bottom, 32, source_row, lambda t: t & 15)
    code_t = column(upper, 16, lambda t: source_row(t) >> 1, lambda t: (t & 15) >> 1)
    copies[0].wait()
    copies[1].wait()
    step = 256
    for at in range(0, TOKENS, step):
        here = slice(at, at + step)
        cb, ct = code_b[here], code_t[here]
        lane = iota((step, 512), 1)
        x = dot(hot(lane == cb), tables[0], 1, 0)
        x = jnp.where(cb == 512, mv[...].astype(F32).reshape(1, MODEL), x)
        x = (x + dot(hot(lane == ct), tables[1], 1, 0)).astype(BF16)
        emb[here] = x
        centred, inverse = moments(x.astype(F32))
        normed[here] = (centred * inverse).astype(BF16)
    copies[2].wait()
    proj[...] = dot(normed[...], weight[...], 1, 0).astype(BF16)


def merge(cot, grads, up, left, diag):
    p = iota((64, 1), 0) & 15
    corner = dot(late_cells(64, 16, False), diag[...], 1, 0)
    cot[0:64] = jnp.where(p >= LATE, corner, up[...].astype(F32)).astype(BF16)
    for at in range(0, OWN, 64):
        m, t = iota((64, MSG), 1), at + iota((64, MSG), 0)
        spread = hot(t == (m >> 2) * COLS + LATE + (m & 3))
        values = dot(spread, left[...], 1, 0)
        values = jnp.where(p >= LATE, values, grads[at : at + 64].astype(F32))
        cot[64 + at : 128 + at] = values.astype(BF16)


def attend_first(place, proj, normed, grads, up, left, diag, ow, att, gp, keep, send, cot, own, weight, sems):
    copies = [
        pltpu.make_async_copy(grads, own, sems.at[0]),
        pltpu.make_async_copy(ow.at[:, 0:CW], weight, sems.at[1]),
    ]
    for copy in copies:
        copy.start()
    copies[0].wait()
    merge(cot, own, up, left, diag)
    copies[1].wait()
    attend(0, place, proj, normed, cot, weight, att, gp, keep, send)


def attend_next(place, proj, normed, cot, ow, att, gp, keep, send, weight, sem):
    copy = pltpu.make_async_copy(ow.at[:, CW:], weight, sem)
    copy.start()
    copy.wait()
    attend(1, place, proj, normed, cot, weight, att, gp, keep, send)


def attend(chunk, place, proj, normed, cot, ow, att, gp, keep, send):
    grad = dot(cot[...], ow[...], 1, 0).astype(BF16)
    lane = iota((BAND, 128), 1) < 64
    tk, tq = iota((BAND, BAND), 0), iota((BAND, BAND), 1)

    def side(t):
        c = t & 15
        return ((c >= 4) & (c < 12)).astype(jnp.int32)

    same = side(tk) == side(tq)
    whole = (tk >> 6) == (tq >> 6)
    zero = jnp.zeros((BAND, BAND), F32)
    plain = jnp.where(same, zero, -1e30)
    first = jnp.where(whole | (place[0] != 0), plain, -1e30)

    def split(x):
        none = jnp.zeros_like(x)
        return jnp.concatenate([jnp.where(lane, x, none), jnp.where(lane, none, x)], axis=0)

    def pick(x):
        return jnp.where(lane, x[:BAND], x[BAND:])

    for b in range(BANDS):
        bias = first if b == 0 else plain
        here = slice(b * BAND, (b + 1) * BAND)
        for p in range(CW // 128):
            cols = slice(p * 128, (p + 1) * 128)
            first_col = chunk * CW + p * 128
            qq, kk, vv = (proj[here, i * HW + first_col : i * HW + first_col + 128] for i in range(3))
            kk, vv = split(kk), split(vv)
            da = grad[here, cols]
            s = dot(kk, qq, 1, 1).reshape(2, BAND, BAND) * 0.125 + bias
            e = jnp.exp(s - jnp.max(s, axis=1, keepdims=True))
            share = e * (1.0 / jnp.sum(e, axis=1, keepdims=True))
            sb = share.astype(BF16).reshape(2 * BAND, BAND)
            att[here, cols] = dot(sb, vv, 0, 0).astype(BF16)
            gs = dot(vv, da, 1, 1).reshape(2, BAND, BAND)
            delta = jnp.sum(share * gs, axis=1, keepdims=True)
            ds = (share * (gs - delta) * 0.125).astype(BF16).reshape(2 * BAND, BAND)
            at = p * 128
            gp[here, at : at + 128] = dot(ds, kk, 0, 0).astype(BF16)
            gp[here, CW + at : CW + at + 128] = pick(dot(ds, qq, 1, 0)).astype(BF16)
            gp[here, 2 * CW + at : 2 * CW + at + 128] = pick(dot(sb, da, 1, 0)).astype(BF16)

    core = place[1]
    for half in range(2):
        for out, flip in ((send, 1), (keep, 0)):
            cut = pl.ds(pl.multiple_of(half * 512 + (core ^ flip) * 256, 256), 256)
            out[half, :, 0 : 3 * CW] = dot(normed[:, cut], gp[...], 0, 0).astype(out.dtype)
            out[half, :, 3 * CW :] = dot(cot[:, cut], att[...], 0, 0).astype(out.dtype)


def finish_kernel(emb, cot, wq, ow, att0, att1, gp0, gp1, mid, up, left, diag, tick, weight, last, big, sems):
    copies = [
        pltpu.make_async_copy(ow, last, sems.at[0]),
        pltpu.make_async_copy(wq, weight, sems.at[1]),
    ]
    for copy in copies:
        copy.start()
    copies[0].wait()

    def put(i, block, values):
        if block == 0:
            up[i] = values[:64]
            mid[i, 0:64] = values[64:]
        else:
            at = block * BAND - 64
            mid[i, at : at + BAND] = values

    def each(i, update):
        for block in range(BANDS):
            here = slice(block * BAND, (block + 1) * BAND)
            put(i, block, update(here, emb[here].astype(F32), big[here]).astype(BF16))

    def gradient(here, x, gst):
        centred, inverse = moments(x)
        standard = centred * inverse
        m1 = jnp.mean(gst, axis=1, keepdims=True)
        m2 = jnp.mean(gst * standard, axis=1, keepdims=True)
        return cot[here].astype(F32) + inverse * (gst - m1 - standard * m2)

    att = jnp.concatenate([att0[...], att1[...]], axis=1)
    big[...] = dot(att, last[...], 1, 1)
    each(0, lambda here, x, branch: x + branch)
    copies[1].wait()
    parts = []
    for i in range(3):
        parts += [g[:, i * CW : (i + 1) * CW] for g in (gp0, gp1)]
    big[...] = dot(jnp.concatenate(parts, axis=1), weight[...], 1, 1)
    each(1, gradient)
    pick, corner = late_cells(OWN, MSG, True), late_cells(64, 16, True)
    for i in range(2):
        left[i] = dot(pick, mid[i], 1, 0).astype(BF16)
        diag[i] = dot(corner, up[i], 1, 0).astype(BF16)
    tick[...] = jnp.zeros(tick.shape, F32)


def place_kernel(mid, up, left, diag, out, gin, tick):
    tick[...] = jnp.zeros(tick.shape, F32)
    late = (iota((64, 1), 0) & 15) >= LATE
    corner = late_cells(64, 16, False)
    for i, ref in enumerate((out, gin)):
        ref[OWN:] = jnp.where(late, dot(corner, diag[i], 1, 0), up[i].astype(F32)).astype(BF16)
        for at in range(0, OWN, 64):
            m, t = iota((64, MSG), 1), at + iota((64, MSG), 0)
            spread = hot(t == (m >> 2) * COLS + LATE + (m & 3))
            values = dot(spread, left[i], 1, 0)
            ref[at : at + 64] = jnp.where(late, values, mid[i, at : at + 64].astype(F32)).astype(BF16)


W = 4 * CW
Q = W // 4


def lanes(i):
    return pl.ds(pl.multiple_of(i * Q, Q), Q)


def parity_core(place, a, b, keep, send):
    g = place[2] ^ place[3]
    for u in range(2):
        for out, v in ((keep, u ^ g), (send, u ^ g ^ 1)):
            cut = lanes(2 * u + v)
            out[:, :, u * Q : (u + 1) * Q] = (a[:, :, cut] + b[:, :, cut].astype(F32)).astype(out.dtype)


def high_core(place, a, b, keep, send):
    for out, u in ((keep, place[2]), (send, place[2] ^ 1)):
        for v in range(2):
            cut = lanes(2 * u + v)
            out[:, :, v * Q : (v + 1) * Q] = (a[:, :, cut] + b[:, :, cut].astype(F32)).astype(out.dtype)


def pair(bit, place, a, b, tick, keep, send):
    for out, u in ((keep, place[bit]), (send, place[bit] ^ 1)):
        out[...] = (a[:, :, lanes(u)] + b[:, :, lanes(u)].astype(F32)).astype(out.dtype)


def join_kernel(a, b, c, d, placed, out):
    out[:, :, 0:Q] = (a[...] + b[...].astype(F32)).astype(BF16)
    out[:, :, Q:] = (c[...] + d[...].astype(F32)).astype(BF16)


def total_kernel(factor, ref, out):
    out[...] = sum(ref[i].astype(F32) for i in range(32)) * factor


def level_kernel(place, *refs):
    qkv, outw = refs[4:]
    for d in range(4):
        who = (2 * place[2] + place[3]) ^ d
        for c in range(CHUNKS):
            cut = slice(c * Q, (c + 1) * Q)

            @pl.when(who < 3)
            def _():
                qkv[:, pl.ds(pl.multiple_of(who * HW + c * CW, CW), CW)] = refs[d][:, cut]

            @pl.when(who == 3)
            def _():
                outw[:, c * CW : (c + 1) * CW] = refs[d][:, cut]


def permute(x, where):
    pairs = []
    for la in range(NLAT):
        for lo in range(NLON):
            tl, to = where(la, lo)
            pairs.append((la * NLON + lo, tl * NLON + to))
    return lax.ppermute(x, GRID, pairs)


def shift(x, down, right):
    return permute(x, lambda la, lo: ((la + down) % NLAT, (lo + right) % NLON))


def swap(x, axis, flip):
    return lax.ppermute(x, axis, [(i, i ^ flip) for i in range(lax.axis_size(axis))])


def halve(name, kernel, shape, place, *terms):
    size = math.prod(shape)
    return call(
        kernel,
        [sds(shape, F32), sds(shape)],
        (place, *terms),
        [smem()] + [vmem()] * len(terms),
        2 * size,
        16 * size,
        limit=16,
        name=name,
    )


def sum_y(place, keep, send, tick, order):
    core, bit = (parity_core, 2) if order[0] == 1 else (high_core, 3)
    recv = swap(send, "core", 1)
    keep, send = halve("sum_core", core, (2, 256, 2 * Q), place, keep, recv)
    recv = swap(send, "batch", order[0])
    keep, send = halve("sum_pair", functools.partial(pair, bit), (2, 256, Q), place, keep, recv, tick)
    return [x.reshape(32, 16, Q) for x in (keep, swap(send, "batch", order[1]))]


def shards(
    bottom_codes, mask_flags, top_codes, bottom_table, top_table, mask_vector, qkv_weight, out_weight, cotangent
):
    core, y = lax.axis_index("core"), lax.axis_index("batch")
    place = jnp.stack([2 * lax.axis_index("xh") + core, core, y >> 1, y & 1]).astype(jnp.int32)
    own = jnp.concatenate(
        [bottom_codes[0], mask_flags[0], jnp.pad(top_codes[0], ((0, 0), (0, 8)))], axis=0
    )
    near = (own, shift(own, 1, 0), shift(own, 0, 1), shift(own, 1, 1))
    pin = lambda x: pltpu.with_memory_space_constraint(x, pltpu.HBM)
    grads = pin(cotangent.reshape(TOKENS, MODEL))
    bottom_table, top_table = pin(bottom_table), pin(top_table)
    qkv_weight, out_weight = pin(qkv_weight), pin(out_weight)
    up, left, diag = call(
        slice_kernel,
        [sds((64, MODEL)), sds((MSG, MODEL)), sds((16, MODEL))],
        (grads,),
        [hbm()],
        2**28,
        2**21,
        name="slices",
        scratch=[pltpu.VMEM((TOKENS, MODEL), BF16), pltpu.SemaphoreType.DMA],
    )
    up, left, diag = shift(up, 1, 0), shift(left, 0, 1), shift(diag, 1, 1)
    emb, normed, proj = call(
        embed_kernel,
        [sds((TOKENS, MODEL)), sds((TOKENS, MODEL)), sds((TOKENS, 3 * HW))],
        (*near, bottom_table, top_table, mask_vector, qkv_weight),
        [vmem()] * 4 + [hbm(), hbm(), vmem(), hbm()],
        2 * TOKENS * 1024 * 2560,
        9 * 2**20,
        name="embed",
        scratch=[pltpu.VMEM((2, 512, MODEL), BF16), pltpu.VMEM((MODEL, 3 * HW), BF16), sems(3)],
    )
    outs = [sds((TOKENS, CW)), sds((TOKENS, 3 * CW)), sds((2, 256, W), F32), sds((2, 256, W))]
    column = pltpu.VMEM((MODEL, CW), BF16)
    att0, gp0, keep0, send0, cot = call(
        attend_first,
        outs + [sds((TOKENS, MODEL))],
        (place, proj, normed, grads, up, left, diag, out_weight),
        [smem(), vmem(), vmem(), hbm(), vmem(), vmem(), vmem(), hbm()],
        3 * 2**30,
        8 * 2**20,
        2**19,
        name="attend",
        scratch=[pltpu.VMEM((TOKENS, MODEL), BF16), column, sems(2)],
    )
    att1, gp1, keep1, send1 = call(
        attend_next,
        outs,
        (place, proj, normed, cot, out_weight),
        [smem(), vmem(), vmem(), vmem(), hbm()],
        3 * 2**30,
        8 * 2**20,
        2**19,
        name="attend",
        scratch=[column, pltpu.SemaphoreType.DMA],
    )
    *sent, tick = call(
        finish_kernel,
        [sds((2, OWN, MODEL)), sds((2, 64, MODEL)), sds((2, MSG, MODEL)), sds((2, 16, MODEL)), sds((8, 128), F32)],
        (emb, cot, qkv_weight, out_weight, att0, att1, gp0, gp1),
        [vmem(), vmem(), hbm(), hbm()] + [vmem()] * 4,
        2 * TOKENS * 1024 * 2048,
        10 * 2**20,
        name="finish",
        scratch=[
            pltpu.VMEM((MODEL, 3 * HW), BF16),
            pltpu.VMEM((MODEL, HW), BF16),
            pltpu.VMEM((TOKENS, MODEL), F32),
            sems(2),
        ],
    )
    summed = sum_y(place, keep0, send0, tick, (1, 3)) + sum_y(place, keep1, send1, tick, (3, 1))
    mid, up, left, diag = sent
    up, left, diag = shift(up, -1, 0), shift(left, 0, -1), shift(diag, -1, -1)
    out, gin, placed = call(
        place_kernel,
        [sds((TOKENS, MODEL))] * 2 + [sds((8, 128), F32)],
        (mid, up, left, diag),
        [vmem()] * 4,
        2**28,
        5 * 2**20,
        limit=24,
        name="place",
    )
    factor = 1.0 / math.sqrt(TOKENS * NB * NLAT * NLON)
    joined = call(
        join_kernel, sds((32, 16, 2 * Q)), (*summed, placed), [vmem()] * 5, 2**19, 2**21, limit=16, name="join"
    )
    spread = lax.all_to_all(joined, ("xh", "z", "xl"), 0, 0, tiled=True)
    total = call(
        functools.partial(total_kernel, factor),
        sds((16, 2 * Q), F32),
        (spread,),
        [vmem()],
        2**18,
        2**20,
        limit=16,
        name="total",
    )
    g_qkv, g_out = call(
        level_kernel,
        [sds((16, 3 * HW), F32), sds((16, HW), F32)],
        (place, total, *[swap(total, "batch", d) for d in (1, 2, 3)]),
        [smem()] + [vmem()] * 4,
        2**15,
        2**18,
        limit=16,
        name="level",
    )
    shape = (1, ROWS, COLS, MODEL)
    return (out.reshape(shape), gin.reshape(shape), g_qkv, g_out)


def solution(mesh):
    devices = mesh.devices.reshape(NB, 2, 2, 8, 2)
    fine = jax.sharding.Mesh(devices, ("batch",) + GRID)
    rows, cols = ("xh", "core"), ("z", "xl")
    grid, whole = P("batch", rows, cols), P()
    return jax.shard_map(
        shards,
        mesh=fine,
        in_specs=(grid, grid, grid, whole, whole, whole, whole, whole, P("batch", rows, cols, None)),
        out_specs=(
            P("batch", rows, cols, None),
            P("batch", rows, cols, None),
            P(GRID, None),
            P(GRID, None),
        ),
        check_vma=False,
    )
```

```python
import functools
import math

import jax
import jax.numpy as jnp
from jax import lax
from jax.experimental import pallas as pl
from jax.experimental.pallas import tpu as pltpu
from jax.sharding import PartitionSpec as P

HEADS = 8
HDIM = 64
WIN = 8
HW = 512
SHIFT = 4
EPS = 1e-05
MODEL = 1024
ROWS, COLS = 32, 16
TOKENS = ROWS * COLS
BAND = WIN * COLS
BANDS = TOKENS // BAND
CHUNKS = 2
CW = HW // CHUNKS
F32 = jnp.float32
BF16 = jnp.bfloat16
GRID = ("xh", "core", "z", "xl")
NB, NLAT, NLON = 4, 4, 16


def dot(a, b, ca, cb):
    return lax.dot_general(a, b, (((ca,), (cb,)), ((), ())), preferred_element_type=F32)


def vmem():
    return pl.BlockSpec(memory_space=pltpu.VMEM)


def smem():
    return pl.BlockSpec(memory_space=pltpu.SMEM)


def call(kernel, outs, operands, specs, flops, nbytes, trans=0, limit=40, name=None, scratch=()):
    return pl.pallas_call(
        kernel,
        out_shape=outs,
        in_specs=specs,
        out_specs=jax.tree.map(lambda _: vmem(), outs),
        scratch_shapes=scratch,
        compiler_params=pltpu.CompilerParams(vmem_limit_bytes=limit * 2**20),
        cost_estimate=pl.CostEstimate(flops=flops, bytes_accessed=nbytes, transcendentals=trans),
        name=name,
    )(*operands)


def hbm():
    return pl.BlockSpec(memory_space=pltpu.HBM)


def sems(n):
    return pltpu.SemaphoreType.DMA((n,))


def sds(shape, dtype=BF16):
    return jax.ShapeDtypeStruct(shape, dtype)


def iota(shape, dim):
    return lax.broadcasted_iota(jnp.int32, shape, dim)


def moments(x):
    mean = jnp.mean(x, axis=1, keepdims=True)
    centred = x - mean
    inverse = lax.rsqrt(jnp.mean(centred * centred, axis=1, keepdims=True) + EPS)
    return centred, inverse


MSG = SHIFT * (ROWS - SHIFT)
OWN = (ROWS - SHIFT) * COLS
LATE = COLS - SHIFT


def hot(mask):
    return mask.astype(F32).astype(BF16)


def late_cells(cells, rows, by_row):
    dims = (0, 1) if by_row else (1, 0)
    shape = (rows, cells) if by_row else (cells, rows)
    m, t = iota(shape, dims[0]), iota(shape, dims[1])
    return hot(t == (m >> 2) * COLS + LATE + (m & 3))


def slice_kernel(cot, up, left, diag, held, sem):
    copy = pltpu.make_async_copy(cot, held, sem)
    copy.start()
    pick, corner = late_cells(OWN, MSG, True), late_cells(64, 16, True)
    copy.wait()
    up[...] = held[OWN:]
    left[...] = dot(pick, held[:OWN], 1, 0).astype(BF16)
    diag[...] = dot(corner, held[OWN:], 1, 0).astype(BF16)


def embed_kernel(own, up, left, diag, bt, tt, mv, wq, emb, normed, proj, tables, weight, sems):
    copies = [
        pltpu.make_async_copy(bt, tables.at[0], sems.at[0]),
        pltpu.make_async_copy(tt, tables.at[1], sems.at[1]),
        pltpu.make_async_copy(wq, weight, sems.at[2]),
    ]
    copies[0].start()
    copies[1].start()
    r, j = iota((80, 16), 0), iota((80, 16), 1)
    low = jnp.where(r >= 64, r - 50, r & 31) >= 28
    late = jnp.where(r >= 64, 2 * j, j) >= LATE
    grid = jnp.where(
        low,
        jnp.where(late, diag[...], up[...]),
        jnp.where(late, left[...], own[...]),
    )
    bottom = jnp.where(grid[32:64] == 1, 512, grid[0:32])
    upper = grid[64:80, 0:8]

    def column(codes, rows, row_of, lane_of):
        width = codes.shape[1]
        parts = jnp.concatenate([codes >> 4, codes & 15], axis=1).astype(F32).astype(BF16)
        pick = hot(row_of(iota((TOKENS, rows), 0)) == iota((TOKENS, rows), 1))
        spread = dot(pick, parts, 1, 0)
        t, lane = iota(spread.shape, 0), iota(spread.shape, 1)
        inside = jnp.where(lane < width, lane, lane - width) == lane_of(t)
        weight = jnp.where(lane < width, 16.0, 1.0)
        code = jnp.sum(jnp.where(inside, spread * weight, 0.0), axis=1, keepdims=True)
        return code.astype(jnp.int32)

    def source_row(t):
        return ((t >> 4) + (ROWS - SHIFT)) & (ROWS - 1)

    code_b = column(bottom, 32, source_row, lambda t: t & 15)
    code_t = column(upper, 16, lambda t: source_row(t) >> 1, lambda t: (t & 15) >> 1)
    copies[0].wait()
    copies[1].wait()
    copies[2].start()
    step = 256
    for at in range(0, TOKENS, step):
        here = slice(at, at + step)
        cb, ct = code_b[here], code_t[here]
        lane = iota((step, 512), 1)
        x = dot(hot(lane == cb), tables[0], 1, 0)
        x = jnp.where(cb == 512, mv[...].astype(F32).reshape(1, MODEL), x)
        x = (x + dot(hot(lane == ct), tables[1], 1, 0)).astype(BF16)
        emb[here] = x
        centred, inverse = moments(x.astype(F32))
        normed[here] = (centred * inverse).astype(BF16)
    copies[2].wait()
    proj[...] = dot(normed[...], weight[...], 1, 0).astype(BF16)


def merge(cot, grads, up, left, diag):
    p = iota((64, 1), 0) & 15
    corner = dot(late_cells(64, 16, False), diag[...], 1, 0)
    cot[0:64] = jnp.where(p >= LATE, corner, up[...].astype(F32)).astype(BF16)
    for at in range(0, OWN, 64):
        m, t = iota((64, MSG), 1), at + iota((64, MSG), 0)
        spread = hot(t == (m >> 2) * COLS + LATE + (m & 3))
        values = dot(spread, left[...], 1, 0)
        values = jnp.where(p >= LATE, values, grads[at : at + 64].astype(F32))
        cot[64 + at : 128 + at] = values.astype(BF16)


def attend_first(place, proj, normed, grads, up, left, diag, ow, att, gp, keep, send, cot, own, weight, sems, *held):
    copies = [
        pltpu.make_async_copy(grads, own, sems.at[0]),
        pltpu.make_async_copy(ow.at[:, 0:CW], weight, sems.at[1]),
    ]
    for copy in copies:
        copy.start()
    units = forward(0, place, proj, att, *held)
    copies[0].wait()
    merge(cot, own, up, left, diag)
    copies[1].wait()
    backward(units, place, normed, cot, weight, att, gp, keep, send, *held)


def attend_next(place, proj, normed, cot, ow, att, gp, keep, send, weight, sem, *held):
    copy = pltpu.make_async_copy(ow.at[:, CW:], weight, sem)
    copy.start()
    units = forward(1, place, proj, att, *held)
    copy.wait()
    backward(units, place, normed, cot, weight, att, gp, keep, send, *held)


def first_lanes():
    return iota((BAND, 128), 1) < 64


def split(x):
    none = jnp.zeros_like(x)
    first = first_lanes()
    return jnp.concatenate([jnp.where(first, x, none), jnp.where(first, none, x)], axis=0)


def forward(chunk, place, proj, att, share, share_bf, ds):
    tk, tq = iota((BAND, BAND), 0), iota((BAND, BAND), 1)

    def side(t):
        c = t & 15
        return ((c >= 4) & (c < 12)).astype(jnp.int32)

    same = side(tk) == side(tq)
    whole = (tk >> 6) == (tq >> 6)
    zero = jnp.zeros((BAND, BAND), F32)
    plain = jnp.where(same, zero, -1e30)
    first = jnp.where(whole | (place[0] != 0), plain, -1e30)
    units = []
    for p in range(CW // 128):
        for b in range(BANDS):
            here, at = slice(b * BAND, (b + 1) * BAND), chunk * CW + p * 128
            loads = [functools.partial(lambda c, h: proj[h, c : c + 128], i * HW + at, here) for i in range(3)]
            units.append((b, here, p * 128, *loads))
    for u, (b, here, at, q, k, v) in enumerate(units):
        share[u] = dot(split(k()), q(), 1, 1).reshape(2, BAND, BAND) * 0.125 + (first if b == 0 else plain)
    for u in range(len(units)):
        s = share[u]
        e = jnp.exp(s - jnp.max(s, axis=1, keepdims=True))
        e = e * (1.0 / jnp.sum(e, axis=1, keepdims=True))
        share[u] = e
        share_bf[u] = e.astype(BF16).reshape(2 * BAND, BAND)
    for u, (b, here, at, q, k, v) in enumerate(units):
        att[here, at : at + 128] = dot(share_bf[u], split(v()), 0, 0).astype(BF16)
    return units


def backward(units, place, normed, cot, ow, att, gp, keep, send, share, share_bf, ds):
    grad = dot(cot[...], ow[...], 1, 0).astype(BF16)
    lane = first_lanes()

    def pick(x):
        return jnp.where(lane, x[:BAND], x[BAND:])

    for u, (b, here, at, q, k, v) in enumerate(units):
        gs = dot(split(v()), grad[here, at : at + 128], 1, 1).reshape(2, BAND, BAND)
        e = share[u]
        delta = jnp.sum(e * gs, axis=1, keepdims=True)
        ds[u] = (e * (gs - delta) * 0.125).astype(BF16).reshape(2 * BAND, BAND)
    for u, (b, here, at, q, k, v) in enumerate(units):
        d = ds[u]
        gp[here, at : at + 128] = dot(d, split(k()), 0, 0).astype(BF16)
        gp[here, CW + at : CW + at + 128] = pick(dot(d, q(), 1, 0)).astype(BF16)
        gp[here, 2 * CW + at : 2 * CW + at + 128] = pick(
            dot(share_bf[u], grad[here, at : at + 128], 1, 0)
        ).astype(BF16)
    core = place[1]
    for half in range(2):
        for out, flip in ((send, 1), (keep, 0)):
            cut = pl.ds(pl.multiple_of(half * 512 + (core ^ flip) * 256, 256), 256)
            out[half, :, 0 : 3 * CW] = dot(normed[:, cut], gp[...], 0, 0).astype(out.dtype)
            out[half, :, 3 * CW :] = dot(cot[:, cut], att[...], 0, 0).astype(out.dtype)


def finish_kernel(emb, cot, wq, ow, att0, att1, gp0, gp1, mid, up, left, diag, tick, weight, last, big, sems):
    copies = [
        pltpu.make_async_copy(ow, last, sems.at[0]),
        pltpu.make_async_copy(wq, weight, sems.at[1]),
    ]
    for copy in copies:
        copy.start()
    copies[0].wait()

    def put(i, block, values):
        if block == 0:
            up[i] = values[:64]
            mid[i, 0:64] = values[64:]
        else:
            at = block * BAND - 64
            mid[i, at : at + BAND] = values

    def each(i, update):
        for block in range(BANDS):
            here = slice(block * BAND, (block + 1) * BAND)
            put(i, block, update(here, emb[here].astype(F32), big[here]).astype(BF16))

    def gradient(here, x, gst):
        centred, inverse = moments(x)
        standard = centred * inverse
        m1 = jnp.mean(gst, axis=1, keepdims=True)
        m2 = jnp.mean(gst * standard, axis=1, keepdims=True)
        return cot[here].astype(F32) + inverse * (gst - m1 - standard * m2)

    att = jnp.concatenate([att0[...], att1[...]], axis=1)
    big[...] = dot(att, last[...], 1, 1)
    each(0, lambda here, x, branch: x + branch)
    copies[1].wait()
    parts = []
    for i in range(3):
        parts += [g[:, i * CW : (i + 1) * CW] for g in (gp0, gp1)]
    big[...] = dot(jnp.concatenate(parts, axis=1), weight[...], 1, 1)
    each(1, gradient)
    pick, corner = late_cells(OWN, MSG, True), late_cells(64, 16, True)
    for i in range(2):
        left[i] = dot(pick, mid[i], 1, 0).astype(BF16)
        diag[i] = dot(corner, up[i], 1, 0).astype(BF16)
    tick[...] = jnp.zeros(tick.shape, F32)


def place_kernel(mid, up, left, diag, out, gin):
    late = (iota((64, 1), 0) & 15) >= LATE
    corner = late_cells(64, 16, False)
    for i, ref in enumerate((out, gin)):
        ref[OWN:] = jnp.where(late, dot(corner, diag[i], 1, 0), up[i].astype(F32)).astype(BF16)
        for at in range(0, OWN, 64):
            m, t = iota((64, MSG), 1), at + iota((64, MSG), 0)
            spread = hot(t == (m >> 2) * COLS + LATE + (m & 3))
            values = dot(spread, left[i], 1, 0)
            ref[at : at + 64] = jnp.where(late, values, mid[i, at : at + 64].astype(F32)).astype(BF16)


W = 4 * CW
Q = W // 4


def parity_core(place, a, b, keep, send):
    g = place[2] ^ place[3]
    for u in range(2):
        for out, v in ((keep, u ^ g), (send, u ^ g ^ 1)):
            out[u] = (a[u, :, v] + b[u, :, v].astype(F32)).astype(out.dtype)


def parity_pair(place, a, b, tick, keep, send):
    for out, u in ((keep, place[2]), (send, place[2] ^ 1)):
        out[...] = (a[u] + b[u].astype(F32)).astype(out.dtype)


def high_core(place, a, b, keep, send):
    for out, u in ((keep, place[2]), (send, place[2] ^ 1)):
        for v in range(2):
            out[v] = (a[u, :, v] + b[u, :, v].astype(F32)).astype(out.dtype)


def high_pair(place, a, b, tick, keep, send):
    for out, v in ((keep, place[3]), (send, place[3] ^ 1)):
        out[...] = (a[v] + b[v].astype(F32)).astype(out.dtype)


def join_kernel(a, b, c, d, arrived, out):
    out[:, :, 0:W] = (a[...] + b[...].astype(F32)).astype(BF16)
    out[:, :, W:] = (c[...] + d[...].astype(F32)).astype(BF16)


def depth_kernel(ref, keep, send):
    total = sum(ref[i].astype(F32) for i in range(8))
    keep[...] = total
    send[...] = total.astype(BF16)


def level_kernel(factor, own, *refs):
    qkv, outw = refs[3:]
    total = (own[...] + sum(r[...].astype(F32) for r in refs[:3])) * factor
    for c in range(CHUNKS):
        for i in range(3):
            qkv[:, i * HW + c * CW : i * HW + (c + 1) * CW] = total[:, c * W + i * Q : c * W + (i + 1) * Q]
        outw[:, c * CW : (c + 1) * CW] = total[:, c * W + 3 * Q : (c + 1) * W]


def permute(x, where):
    pairs = []
    for la in range(NLAT):
        for lo in range(NLON):
            tl, to = where(la, lo)
            pairs.append((la * NLON + lo, tl * NLON + to))
    return lax.ppermute(x, GRID, pairs)


def shift(x, down, right):
    return permute(x, lambda la, lo: ((la + down) % NLAT, (lo + right) % NLON))


def swap(x, axis, flip):
    return lax.ppermute(x, axis, [(i, i ^ flip) for i in range(lax.axis_size(axis))])


def swap_x(x, flip):
    return permute(x, lambda la, lo: (la ^ (flip & 2), lo ^ (flip & 1)))


def halve(name, kernel, shape, place, *terms):
    size = math.prod(shape)
    return call(
        kernel,
        [sds(shape, F32), sds(shape)],
        (place, *terms),
        [smem()] + [vmem()] * len(terms),
        2 * size,
        16 * size,
        limit=16,
        name=name,
    )


def sum_x(place, keep, send, tick, order):
    fold = (2, 8, 2, 16, W)
    core, pair = (parity_core, parity_pair) if order[0] == 1 else (high_core, high_pair)
    recv = swap(send, "core", 1)
    keep, send = halve("sum_core", core, (2, 8, 16, W), place, keep.reshape(fold), recv.reshape(fold))
    keep, send = halve("sum_pair", pair, (8, 16, W), place, keep, swap_x(send, order[0]), tick)
    return [keep, swap_x(send, order[1])]


def shards(
    bottom_codes, mask_flags, top_codes, bottom_table, top_table, mask_vector, qkv_weight, out_weight, cotangent
):
    core, xh, xl = lax.axis_index("core"), lax.axis_index("xh"), lax.axis_index("xl")
    place = jnp.stack([2 * xh + core, core, xh, xl]).astype(jnp.int32)
    own = jnp.concatenate(
        [bottom_codes[0], mask_flags[0], jnp.pad(top_codes[0], ((0, 0), (0, 8)))], axis=0
    )
    near = (own, shift(own, 1, 0), shift(own, 0, 1), shift(own, 1, 1))
    pin = lambda x: pltpu.with_memory_space_constraint(x, pltpu.HBM)
    grads = pin(cotangent.reshape(TOKENS, MODEL))
    bottom_table, top_table = pin(bottom_table), pin(top_table)
    qkv_weight, out_weight = pin(qkv_weight), pin(out_weight)
    up, left, diag = call(
        slice_kernel,
        [sds((64, MODEL)), sds((MSG, MODEL)), sds((16, MODEL))],
        (grads,),
        [hbm()],
        2**28,
        2**21,
        name="slices",
        scratch=[pltpu.VMEM((TOKENS, MODEL), BF16), pltpu.SemaphoreType.DMA],
    )
    up, left, diag = shift(up, 1, 0), shift(left, 0, 1), shift(diag, 1, 1)
    emb, normed, proj = call(
        embed_kernel,
        [sds((TOKENS, MODEL)), sds((TOKENS, MODEL)), sds((TOKENS, 3 * HW))],
        (*near, bottom_table, top_table, mask_vector, qkv_weight),
        [vmem()] * 4 + [hbm(), hbm(), vmem(), hbm()],
        2 * TOKENS * 1024 * 2560,
        9 * 2**20,
        name="embed",
        scratch=[pltpu.VMEM((2, 512, MODEL), BF16), pltpu.VMEM((MODEL, 3 * HW), BF16), sems(3)],
    )
    outs = [sds((TOKENS, CW)), sds((TOKENS, 3 * CW)), sds((2, 256, W), F32), sds((2, 256, W))]
    column = pltpu.VMEM((MODEL, CW), BF16)
    units = BANDS * CW // 128
    held = [pltpu.VMEM((units, 2, BAND, BAND), F32)] + [pltpu.VMEM((units, 2 * BAND, BAND), BF16)] * 2
    att0, gp0, keep0, send0, cot = call(
        attend_first,
        outs + [sds((TOKENS, MODEL))],
        (place, proj, normed, grads, up, left, diag, out_weight),
        [smem(), vmem(), vmem(), hbm(), vmem(), vmem(), vmem(), hbm()],
        3 * 2**30,
        8 * 2**20,
        2**19,
        name="attend",
        scratch=[pltpu.VMEM((TOKENS, MODEL), BF16), column, sems(2), *held],
    )
    att1, gp1, keep1, send1 = call(
        attend_next,
        outs,
        (place, proj, normed, cot, out_weight),
        [smem(), vmem(), vmem(), vmem(), hbm()],
        3 * 2**30,
        8 * 2**20,
        2**19,
        name="attend",
        scratch=[column, pltpu.SemaphoreType.DMA, *held],
    )
    *sent, tick = call(
        finish_kernel,
        [sds((2, OWN, MODEL)), sds((2, 64, MODEL)), sds((2, MSG, MODEL)), sds((2, 16, MODEL)), sds((8, 128), F32)],
        (emb, cot, qkv_weight, out_weight, att0, att1, gp0, gp1),
        [vmem(), vmem(), hbm(), hbm()] + [vmem()] * 4,
        2 * TOKENS * 1024 * 2048,
        10 * 2**20,
        name="finish",
        scratch=[
            pltpu.VMEM((MODEL, 3 * HW), BF16),
            pltpu.VMEM((MODEL, HW), BF16),
            pltpu.VMEM((TOKENS, MODEL), F32),
            sems(2),
        ],
    )
    summed = sum_x(place, keep0, send0, tick, (1, 3)) + sum_x(place, keep1, send1, tick, (3, 1))
    mid, up, left, diag = sent
    up, left, diag = shift(up, -1, 0), shift(left, 0, -1), shift(diag, -1, -1)
    out, gin = call(
        place_kernel,
        [sds((TOKENS, MODEL))] * 2,
        (mid, up, left, diag),
        [vmem()] * 4,
        2**28,
        5 * 2**20,
        limit=24,
        name="place",
    )
    factor = 1.0 / math.sqrt(TOKENS * NB * NLAT * NLON)
    joined = call(
        join_kernel,
        sds((8, 16, 2 * W)),
        (*summed, left),
        [vmem()] * 4 + [hbm()],
        2**19,
        2**21,
        limit=16,
        name="join",
    )
    depth = lax.all_to_all(joined, "z", 0, 0, tiled=True)
    keep, send = call(
        depth_kernel,
        [sds((16, 2 * W), F32), sds((16, 2 * W))],
        (depth,),
        [vmem()],
        2**18,
        2**20,
        limit=16,
        name="depth",
    )
    g_qkv, g_out = call(
        functools.partial(level_kernel, factor),
        [sds((16, 3 * HW), F32), sds((16, HW), F32)],
        (keep, *[swap(send, "batch", d) for d in (1, 2, 3)]),
        [vmem()] * 4,
        2**17,
        2**19,
        limit=16,
        name="level",
    )
    shape = (1, ROWS, COLS, MODEL)
    return (out.reshape(shape), gin.reshape(shape), g_qkv, g_out)


def solution(mesh):
    devices = mesh.devices.reshape(NB, 2, 2, 8, 2)
    fine = jax.sharding.Mesh(devices, ("batch",) + GRID)
    rows, cols = ("xh", "core"), ("z", "xl")
    grid, whole = P("batch", rows, cols), P()
    return jax.shard_map(
        shards,
        mesh=fine,
        in_specs=(grid, grid, grid, whole, whole, whole, whole, whole, P("batch", rows, cols, None)),
        out_specs=(
            P("batch", rows, cols, None),
            P("batch", rows, cols, None),
            P(GRID, None),
            P(GRID, None),
        ),
        check_vma=False,
    )
```

```python
import functools
import math

import jax
import jax.numpy as jnp
from jax import lax
from jax.experimental import pallas as pl
from jax.experimental.pallas import tpu as pltpu
from jax.sharding import PartitionSpec as P

HEADS = 8
HDIM = 64
WIN = 8
HW = 512
SHIFT = 4
EPS = 1e-05
MODEL = 1024
ROWS, COLS = 32, 16
TOKENS = ROWS * COLS
BAND = WIN * COLS
BANDS = TOKENS // BAND
CHUNKS = 2
CW = HW // CHUNKS
F32 = jnp.float32
BF16 = jnp.bfloat16
GRID = ("xh", "core", "z", "xl")
NB, NLAT, NLON = 4, 4, 16


def dot(a, b, ca, cb):
    return lax.dot_general(a, b, (((ca,), (cb,)), ((), ())), preferred_element_type=F32)


def vmem():
    return pl.BlockSpec(memory_space=pltpu.VMEM)


def smem():
    return pl.BlockSpec(memory_space=pltpu.SMEM)


def call(kernel, outs, operands, specs, flops, nbytes, trans=0, limit=40, name=None, scratch=()):
    return pl.pallas_call(
        kernel,
        out_shape=outs,
        in_specs=specs,
        out_specs=jax.tree.map(lambda _: vmem(), outs),
        scratch_shapes=scratch,
        compiler_params=pltpu.CompilerParams(vmem_limit_bytes=limit * 2**20),
        cost_estimate=pl.CostEstimate(flops=flops, bytes_accessed=nbytes, transcendentals=trans),
        name=name,
    )(*operands)


def hbm():
    return pl.BlockSpec(memory_space=pltpu.HBM)


def anywhere():
    return pl.BlockSpec(memory_space=pl.ANY)


def sems(n):
    return pltpu.SemaphoreType.DMA((n,))


def sds(shape, dtype=BF16):
    return jax.ShapeDtypeStruct(shape, dtype)


def iota(shape, dim):
    return lax.broadcasted_iota(jnp.int32, shape, dim)


def moments(x):
    mean = jnp.mean(x, axis=1, keepdims=True)
    centred = x - mean
    inverse = lax.rsqrt(jnp.mean(centred * centred, axis=1, keepdims=True) + EPS)
    return centred, inverse


MSG = SHIFT * (ROWS - SHIFT)
OWN = (ROWS - SHIFT) * COLS
LATE = COLS - SHIFT


def hot(mask):
    return mask.astype(F32).astype(BF16)


def late_cells(cells, rows, by_row):
    dims = (0, 1) if by_row else (1, 0)
    shape = (rows, cells) if by_row else (cells, rows)
    m, t = iota(shape, dims[0]), iota(shape, dims[1])
    return hot(t == (m >> 2) * COLS + LATE + (m & 3))


def slice_kernel(cot, up, left, diag, held, sem):
    copy = pltpu.make_async_copy(cot, held, sem)
    copy.start()
    pick, corner = late_cells(OWN, MSG, True), late_cells(64, 16, True)
    copy.wait()
    up[...] = held[OWN:]
    left[...] = dot(pick, held[:OWN], 1, 0).astype(BF16)
    diag[...] = dot(corner, held[OWN:], 1, 0).astype(BF16)


def embed_kernel(own, up, left, diag, bt, tt, mv, wq, emb, normed, proj, tables, weight, sems):
    copies = [
        pltpu.make_async_copy(bt, tables.at[0], sems.at[0]),
        pltpu.make_async_copy(tt, tables.at[1], sems.at[1]),
        pltpu.make_async_copy(wq, weight, sems.at[2]),
    ]
    copies[0].start()
    copies[1].start()
    r, j = iota((80, 16), 0), iota((80, 16), 1)
    low = jnp.where(r >= 64, r - 50, r & 31) >= 28
    late = jnp.where(r >= 64, 2 * j, j) >= LATE
    grid = jnp.where(
        low,
        jnp.where(late, diag[...], up[...]),
        jnp.where(late, left[...], own[...]),
    )
    bottom = jnp.where(grid[32:64] == 1, 512, grid[0:32])
    upper = grid[64:80, 0:8]

    def column(codes, rows, row_of, lane_of):
        width = codes.shape[1]
        parts = jnp.concatenate([codes >> 4, codes & 15], axis=1).astype(F32).astype(BF16)
        pick = hot(row_of(iota((TOKENS, rows), 0)) == iota((TOKENS, rows), 1))
        spread = dot(pick, parts, 1, 0)
        t, lane = iota(spread.shape, 0), iota(spread.shape, 1)
        inside = jnp.where(lane < width, lane, lane - width) == lane_of(t)
        weight = jnp.where(lane < width, 16.0, 1.0)
        code = jnp.sum(jnp.where(inside, spread * weight, 0.0), axis=1, keepdims=True)
        return code.astype(jnp.int32)

    def source_row(t):
        return ((t >> 4) + (ROWS - SHIFT)) & (ROWS - 1)

    code_b = column(bottom, 32, source_row, lambda t: t & 15)
    code_t = column(upper, 16, lambda t: source_row(t) >> 1, lambda t: (t & 15) >> 1)
    copies[0].wait()
    copies[1].wait()
    copies[2].start()
    step = 256
    for at in range(0, TOKENS, step):
        here = slice(at, at + step)
        cb, ct = code_b[here], code_t[here]
        lane = iota((step, 512), 1)
        x = dot(hot(lane == cb), tables[0], 1, 0)
        x = jnp.where(cb == 512, mv[...].astype(F32).reshape(1, MODEL), x)
        x = (x + dot(hot(lane == ct), tables[1], 1, 0)).astype(BF16)
        emb[here] = x
        centred, inverse = moments(x.astype(F32))
        normed[here] = (centred * inverse).astype(BF16)
    copies[2].wait()
    proj[...] = dot(normed[...], weight[...], 1, 0).astype(BF16)


def merge(cot, grads, up, left, diag):
    p = iota((64, 1), 0) & 15
    corner = dot(late_cells(64, 16, False), diag[...], 1, 0)
    cot[0:64] = jnp.where(p >= LATE, corner, up[...].astype(F32)).astype(BF16)
    for at in range(0, OWN, 64):
        m, t = iota((64, MSG), 1), at + iota((64, MSG), 0)
        spread = hot(t == (m >> 2) * COLS + LATE + (m & 3))
        values = dot(spread, left[...], 1, 0)
        values = jnp.where(p >= LATE, values, grads[at : at + 64].astype(F32))
        cot[64 + at : 128 + at] = values.astype(BF16)


def attend_first(place, proj, normed, grads, up, left, diag, ow, att, gp, keep, send, cot, own, weight, sems, *held):
    copies = [
        pltpu.make_async_copy(grads, own, sems.at[0]),
        pltpu.make_async_copy(ow.at[:, 0:CW], weight, sems.at[1]),
    ]
    for copy in copies:
        copy.start()
    units = forward(0, place, proj, att, *held)
    copies[0].wait()
    merge(cot, own, up, left, diag)
    copies[1].wait()
    backward(units, place, normed, cot, weight, att, gp, keep, send, *held)


def attend_next(chunk, place, proj, normed, cot, ow, *refs):
    att, gp, keep, send, weight, sem, *held = refs[1:] if chunk > 1 else refs
    copy = pltpu.make_async_copy(ow.at[:, chunk * CW : (chunk + 1) * CW], weight, sem)
    copy.start()
    units = forward(chunk, place, proj, att, *held)
    copy.wait()
    backward(units, place, normed, cot, weight, att, gp, keep, send, *held)


def first_lanes():
    return iota((BAND, 128), 1) < 64


def split(x):
    none = jnp.zeros_like(x)
    first = first_lanes()
    return jnp.concatenate([jnp.where(first, x, none), jnp.where(first, none, x)], axis=0)


def forward(chunk, place, proj, att, share, share_bf, ds):
    tk, tq = iota((BAND, BAND), 0), iota((BAND, BAND), 1)

    def side(t):
        c = t & 15
        return ((c >= 4) & (c < 12)).astype(jnp.int32)

    same = side(tk) == side(tq)
    whole = (tk >> 6) == (tq >> 6)
    zero = jnp.zeros((BAND, BAND), F32)
    plain = jnp.where(same, zero, -1e30)
    first = jnp.where(whole | (place[0] != 0), plain, -1e30)
    units = []
    for p in range(CW // 128):
        for b in range(BANDS):
            here, at = slice(b * BAND, (b + 1) * BAND), chunk * CW + p * 128
            loads = [functools.partial(lambda c, h: proj[h, c : c + 128], i * HW + at, here) for i in range(3)]
            units.append((b, here, p * 128, *loads))
    for u, (b, here, at, q, k, v) in enumerate(units):
        share[u] = dot(split(k()), q(), 1, 1).reshape(2, BAND, BAND) * 0.125 + (first if b == 0 else plain)
    for u in range(len(units)):
        s = share[u]
        e = jnp.exp(s - jnp.max(s, axis=1, keepdims=True))
        e = e * (1.0 / jnp.sum(e, axis=1, keepdims=True))
        share[u] = e
        share_bf[u] = e.astype(BF16).reshape(2 * BAND, BAND)
    for u, (b, here, at, q, k, v) in enumerate(units):
        att[here, at : at + 128] = dot(share_bf[u], split(v()), 0, 0).astype(BF16)
    return units


def backward(units, place, normed, cot, ow, att, gp, keep, send, share, share_bf, ds):
    grad = dot(cot[...], ow[...], 1, 0).astype(BF16)
    lane = first_lanes()

    def pick(x):
        return jnp.where(lane, x[:BAND], x[BAND:])

    for u, (b, here, at, q, k, v) in enumerate(units):
        gs = dot(split(v()), grad[here, at : at + 128], 1, 1).reshape(2, BAND, BAND)
        e = share[u]
        delta = jnp.sum(e * gs, axis=1, keepdims=True)
        ds[u] = (e * (gs - delta) * 0.125).astype(BF16).reshape(2 * BAND, BAND)
    for u, (b, here, at, q, k, v) in enumerate(units):
        d = ds[u]
        gp[here, at : at + 128] = dot(d, split(k()), 0, 0).astype(BF16)
        gp[here, CW + at : CW + at + 128] = pick(dot(d, q(), 1, 0)).astype(BF16)
        gp[here, 2 * CW + at : 2 * CW + at + 128] = pick(
            dot(share_bf[u], grad[here, at : at + 128], 1, 0)
        ).astype(BF16)
    core = place[1]
    for half in range(2):
        for out, flip in ((send, 1), (keep, 0)):
            cut = pl.ds(pl.multiple_of(half * 512 + (core ^ flip) * 256, 256), 256)
            out[half, :, 0 : 3 * CW] = dot(normed[:, cut], gp[...], 0, 0).astype(out.dtype)
            out[half, :, 3 * CW :] = dot(cot[:, cut], att[...], 0, 0).astype(out.dtype)


def finish_kernel(emb, cot, wq, ow, *refs):
    atts, gps = refs[:CHUNKS], refs[CHUNKS : 2 * CHUNKS]
    mid, up, left, diag, tick, weight, last, big, sems = refs[2 * CHUNKS :]
    copies = [
        pltpu.make_async_copy(ow, last, sems.at[0]),
        pltpu.make_async_copy(wq, weight, sems.at[1]),
    ]
    for copy in copies:
        copy.start()
    copies[0].wait()

    def put(i, block, values):
        if block == 0:
            up[i] = values[:64]
            mid[i, 0:64] = values[64:]
        else:
            at = block * BAND - 64
            mid[i, at : at + BAND] = values

    def each(i, update):
        for block in range(BANDS):
            here = slice(block * BAND, (block + 1) * BAND)
            put(i, block, update(here, emb[here].astype(F32), big[here]).astype(BF16))

    def gradient(here, x, gst):
        centred, inverse = moments(x)
        standard = centred * inverse
        m1 = jnp.mean(gst, axis=1, keepdims=True)
        m2 = jnp.mean(gst * standard, axis=1, keepdims=True)
        return cot[here].astype(F32) + inverse * (gst - m1 - standard * m2)

    att = jnp.concatenate([a[...] for a in atts], axis=1)
    big[...] = dot(att, last[...], 1, 1)
    each(0, lambda here, x, branch: x + branch)
    copies[1].wait()
    parts = []
    for i in range(3):
        parts += [g[:, i * CW : (i + 1) * CW] for g in gps]
    big[...] = dot(jnp.concatenate(parts, axis=1), weight[...], 1, 1)
    each(1, gradient)
    pick, corner = late_cells(OWN, MSG, True), late_cells(64, 16, True)
    for i in range(2):
        left[i] = dot(pick, mid[i], 1, 0).astype(BF16)
        diag[i] = dot(corner, up[i], 1, 0).astype(BF16)
    tick[...] = jnp.zeros(tick.shape, F32)


def place_kernel(mid, up, left, diag, out, gin):
    late = (iota((64, 1), 0) & 15) >= LATE
    corner = late_cells(64, 16, False)
    for i, ref in enumerate((out, gin)):
        ref[OWN:] = jnp.where(late, dot(corner, diag[i], 1, 0), up[i].astype(F32)).astype(BF16)
        for at in range(0, OWN, 64):
            m, t = iota((64, MSG), 1), at + iota((64, MSG), 0)
            spread = hot(t == (m >> 2) * COLS + LATE + (m & 3))
            values = dot(spread, left[i], 1, 0)
            ref[at : at + 64] = jnp.where(late, values, mid[i, at : at + 64].astype(F32)).astype(BF16)


W = 4 * CW
Q = W // 4


def parity_core(place, a, b, keep, send):
    g = place[2] ^ place[3]
    for u in range(2):
        for out, v in ((keep, u ^ g), (send, u ^ g ^ 1)):
            out[u] = (a[u, :, v] + b[u, :, v].astype(F32)).astype(out.dtype)


def parity_pair(place, a, b, tick, keep, send):
    for out, u in ((keep, place[2]), (send, place[2] ^ 1)):
        out[...] = (a[u] + b[u].astype(F32)).astype(out.dtype)


def high_core(place, a, b, keep, send):
    for out, u in ((keep, place[2]), (send, place[2] ^ 1)):
        for v in range(2):
            out[v] = (a[u, :, v] + b[u, :, v].astype(F32)).astype(out.dtype)


def high_pair(place, a, b, tick, keep, send):
    for out, v in ((keep, place[3]), (send, place[3] ^ 1)):
        out[...] = (a[v] + b[v].astype(F32)).astype(out.dtype)


def join_kernel(*refs):
    out = refs[-1]
    for c in range(CHUNKS):
        out[:, :, c * W : (c + 1) * W] = (refs[2 * c][...] + refs[2 * c + 1][...].astype(F32)).astype(BF16)


def depth_kernel(ref, out):
    out[...] = sum(ref[i].astype(F32) for i in range(8)).astype(BF16)


def couple_kernel(a, b, out):
    out[...] = (a[...].astype(F32) + b[...].astype(F32)).astype(BF16)


def level_kernel(factor, a, b, qkv, outw):
    total = (a[...].astype(F32) + b[...].astype(F32)) * factor
    for c in range(CHUNKS):
        for i in range(3):
            qkv[:, i * HW + c * CW : i * HW + (c + 1) * CW] = total[:, c * W + i * Q : c * W + (i + 1) * Q]
        outw[:, c * CW : (c + 1) * CW] = total[:, c * W + 3 * Q : (c + 1) * W]


def permute(x, where):
    pairs = []
    for la in range(NLAT):
        for lo in range(NLON):
            tl, to = where(la, lo)
            pairs.append((la * NLON + lo, tl * NLON + to))
    return lax.ppermute(x, GRID, pairs)


def shift(x, down, right):
    return permute(x, lambda la, lo: ((la + down) % NLAT, (lo + right) % NLON))


def swap(x, axis, flip):
    return lax.ppermute(x, axis, [(i, i ^ flip) for i in range(lax.axis_size(axis))])


def swap_x(x, flip):
    return permute(x, lambda la, lo: (la ^ (flip & 2), lo ^ (flip & 1)))


def halve(name, kernel, shape, operands, specs):
    return call(
        kernel,
        [sds(shape, F32), sds(shape)],
        operands,
        specs,
        2**10,
        2**10,
        limit=16,
        name=name,
    )


def order(c):
    return (3, 1) if c % 2 else (1, 3)


def sum_core(place, keep, send, c):
    fold = (2, 8, 2, 16, W)
    kernel = high_core if c % 2 else parity_core
    recv = swap(send, "core", 1)
    operands = (place, keep.reshape(fold), recv.reshape(fold))
    return halve("sum_core", kernel, (2, 8, 16, W), operands, [smem(), vmem(), vmem()])


def sum_pair(place, keep, send, tick, c):
    kernel = high_pair if c % 2 else parity_pair
    recv = swap_x(send, order(c)[0])
    specs = [smem(), vmem(), vmem(), anywhere()]
    keep, send = halve("sum_pair", kernel, (8, 16, W), (place, keep, recv, tick), specs)
    return [keep, swap_x(send, order(c)[1])]


def shards(
    bottom_codes, mask_flags, top_codes, bottom_table, top_table, mask_vector, qkv_weight, out_weight, cotangent
):
    core, xh, xl = lax.axis_index("core"), lax.axis_index("xh"), lax.axis_index("xl")
    place = jnp.stack([2 * xh + core, core, xh, xl]).astype(jnp.int32)
    own = jnp.concatenate(
        [bottom_codes[0], mask_flags[0], jnp.pad(top_codes[0], ((0, 0), (0, 8)))], axis=0
    )
    near = (own, shift(own, 1, 0), shift(own, 0, 1), shift(own, 1, 1))
    pin = lambda x: pltpu.with_memory_space_constraint(x, pltpu.HBM)
    grads = pin(cotangent.reshape(TOKENS, MODEL))
    bottom_table, top_table = pin(bottom_table), pin(top_table)
    qkv_weight, out_weight = pin(qkv_weight), pin(out_weight)
    up, left, diag = call(
        slice_kernel,
        [sds((64, MODEL)), sds((MSG, MODEL)), sds((16, MODEL))],
        (grads,),
        [hbm()],
        2**28,
        2**21,
        name="slices",
        scratch=[pltpu.VMEM((TOKENS, MODEL), BF16), pltpu.SemaphoreType.DMA],
    )
    up, left, diag = shift(up, 1, 0), shift(left, 0, 1), shift(diag, 1, 1)
    emb, normed, proj = call(
        embed_kernel,
        [sds((TOKENS, MODEL)), sds((TOKENS, MODEL)), sds((TOKENS, 3 * HW))],
        (*near, bottom_table, top_table, mask_vector, qkv_weight),
        [vmem()] * 4 + [hbm(), hbm(), vmem(), hbm()],
        2 * TOKENS * 1024 * 2560,
        9 * 2**20,
        name="embed",
        scratch=[pltpu.VMEM((2, 512, MODEL), BF16), pltpu.VMEM((MODEL, 3 * HW), BF16), sems(3)],
    )
    outs = [sds((TOKENS, CW)), sds((TOKENS, 3 * CW)), sds((2, 256, W), F32), sds((2, 256, W))]
    column = pltpu.VMEM((MODEL, CW), BF16)
    units = BANDS * CW // 128
    held = [pltpu.VMEM((units, 2, BAND, BAND), F32)] + [pltpu.VMEM((units, 2 * BAND, BAND), BF16)] * 2
    att, gp, keep, send, cot = call(
        attend_first,
        outs + [sds((TOKENS, MODEL))],
        (place, proj, normed, grads, up, left, diag, out_weight),
        [smem(), vmem(), vmem(), hbm(), vmem(), vmem(), vmem(), hbm()],
        2**20,
        2**12,
        name="attend",
        scratch=[pltpu.VMEM((TOKENS, MODEL), BF16), column, sems(2), *held],
    )
    parts, cores = [(att, gp)], [sum_core(place, keep, send, 0)]
    for c in range(1, CHUNKS):
        after = [cores[c - 2][0]] if c > 1 else []
        att, gp, keep, send = call(
            functools.partial(attend_next, c),
            outs,
            (place, proj, normed, cot, out_weight, *after),
            [smem(), vmem(), vmem(), vmem(), hbm()] + [anywhere()] * len(after),
            2**20,
            2**12,
            name="attend",
            scratch=[column, pltpu.SemaphoreType.DMA, *held],
        )
        parts.append((att, gp))
        cores.append(sum_core(place, keep, send, c))
    *sent, tick = call(
        finish_kernel,
        [sds((2, OWN, MODEL)), sds((2, 64, MODEL)), sds((2, MSG, MODEL)), sds((2, 16, MODEL)), sds((8, 128), F32)],
        (emb, cot, qkv_weight, out_weight, *[p[0] for p in parts], *[p[1] for p in parts]),
        [vmem(), vmem(), hbm(), hbm()] + [vmem()] * 2 * CHUNKS,
        2**20,
        2**12,
        name="finish",
        scratch=[
            pltpu.VMEM((MODEL, 3 * HW), BF16),
            pltpu.VMEM((MODEL, HW), BF16),
            pltpu.VMEM((TOKENS, MODEL), F32),
            sems(2),
        ],
    )
    mid, up, left, diag = sent
    up, left, diag = shift(up, -1, 0), shift(left, 0, -1), shift(diag, -1, -1)
    summed = []
    for c, (keep, send) in enumerate(cores):
        summed += sum_pair(place, keep, send, diag if c else tick, c)
    out, gin = call(
        place_kernel,
        [sds((TOKENS, MODEL))] * 2,
        (mid, up, left, diag),
        [vmem()] * 4,
        2**28,
        5 * 2**20,
        limit=24,
        name="place",
    )
    factor = 1.0 / math.sqrt(TOKENS * NB * NLAT * NLON)
    joined = call(
        join_kernel,
        sds((8, 16, CHUNKS * W)),
        summed,
        [vmem()] * 2 * CHUNKS,
        2**19,
        2**21,
        limit=16,
        name="join",
    )
    depth = lax.all_to_all(joined, "z", 0, 0, tiled=True)
    small = dict(flops=2**17, nbytes=2**19, limit=16)
    wide = (16, CHUNKS * W)
    total = call(depth_kernel, sds(wide), (depth,), [vmem()], name="depth", **small)
    total = call(couple_kernel, sds(wide), (total, swap(total, "batch", 1)), [vmem()] * 2, name="couple", **small)
    g_qkv, g_out = call(
        functools.partial(level_kernel, factor),
        [sds((16, 3 * HW), F32), sds((16, HW), F32)],
        (total, swap(total, "batch", 3)),
        [vmem()] * 2,
        name="level",
        **small,
    )
    shape = (1, ROWS, COLS, MODEL)
    return (out.reshape(shape), gin.reshape(shape), g_qkv, g_out)


def solution(mesh):
    devices = mesh.devices.reshape(NB, 2, 2, 8, 2)
    fine = jax.sharding.Mesh(devices, ("batch",) + GRID)
    rows, cols = ("xh", "core"), ("z", "xl")
    grid, whole = P("batch", rows, cols), P()
    return jax.shard_map(
        shards,
        mesh=fine,
        in_specs=(grid, grid, grid, whole, whole, whole, whole, whole, P("batch", rows, cols, None)),
        out_specs=(
            P("batch", rows, cols, None),
            P("batch", rows, cols, None),
            P(GRID, None),
            P(GRID, None),
        ),
        check_vma=False,
    )
```

```python
import functools
import math

import jax
import jax.numpy as jnp
from jax import lax
from jax.experimental import pallas as pl
from jax.experimental.pallas import tpu as pltpu
from jax.sharding import PartitionSpec as P

HEADS = 8
HDIM = 64
WIN = 8
HW = 512
SHIFT = 4
EPS = 1e-05
MODEL = 1024
ROWS, COLS = 32, 16
TOKENS = ROWS * COLS
BAND = WIN * COLS
BANDS = TOKENS // BAND
CHUNKS = 2
CW = HW // CHUNKS
F32 = jnp.float32
BF16 = jnp.bfloat16
GRID = ("xh", "core", "z", "xl")
NB, NLAT, NLON = 4, 4, 16


def dot(a, b, ca, cb):
    return lax.dot_general(a, b, (((ca,), (cb,)), ((), ())), preferred_element_type=F32)


def vmem():
    return pl.BlockSpec(memory_space=pltpu.VMEM)


def smem():
    return pl.BlockSpec(memory_space=pltpu.SMEM)


def call(kernel, outs, operands, specs, flops, nbytes, trans=0, limit=40, name=None, scratch=()):
    return pl.pallas_call(
        kernel,
        out_shape=outs,
        in_specs=specs,
        out_specs=jax.tree.map(lambda _: vmem(), outs),
        scratch_shapes=scratch,
        compiler_params=pltpu.CompilerParams(vmem_limit_bytes=limit * 2**20),
        cost_estimate=pl.CostEstimate(flops=flops, bytes_accessed=nbytes, transcendentals=trans),
        name=name,
    )(*operands)


def hbm():
    return pl.BlockSpec(memory_space=pltpu.HBM)


def anywhere():
    return pl.BlockSpec(memory_space=pl.ANY)


def sems(n):
    return pltpu.SemaphoreType.DMA((n,))


def sds(shape, dtype=BF16):
    return jax.ShapeDtypeStruct(shape, dtype)


def iota(shape, dim):
    return lax.broadcasted_iota(jnp.int32, shape, dim)


def moments(x):
    mean = jnp.mean(x, axis=1, keepdims=True)
    centred = x - mean
    inverse = lax.rsqrt(jnp.mean(centred * centred, axis=1, keepdims=True) + EPS)
    return centred, inverse


MSG = SHIFT * (ROWS - SHIFT)
OWN = (ROWS - SHIFT) * COLS
LATE = COLS - SHIFT


def hot(mask):
    return mask.astype(F32).astype(BF16)


def late_cells(cells, rows, by_row):
    dims = (0, 1) if by_row else (1, 0)
    shape = (rows, cells) if by_row else (cells, rows)
    m, t = iota(shape, dims[0]), iota(shape, dims[1])
    return hot(t == (m >> 2) * COLS + LATE + (m & 3))


def slice_kernel(cot, up, left, diag, held, sem):
    copy = pltpu.make_async_copy(cot, held, sem)
    copy.start()
    pick, corner = late_cells(OWN, MSG, True), late_cells(64, 16, True)
    copy.wait()
    up[...] = held[OWN:]
    left[...] = dot(pick, held[:OWN], 1, 0).astype(BF16)
    diag[...] = dot(corner, held[OWN:], 1, 0).astype(BF16)


def embed_kernel(own, up, left, diag, bt, tt, mv, wq, emb, normed, proj, tables, weight, sems):
    copies = [
        pltpu.make_async_copy(bt, tables.at[0], sems.at[0]),
        pltpu.make_async_copy(tt, tables.at[1], sems.at[1]),
        pltpu.make_async_copy(wq, weight, sems.at[2]),
    ]
    copies[0].start()
    copies[1].start()
    r, j = iota((80, 16), 0), iota((80, 16), 1)
    low = jnp.where(r >= 64, r - 50, r & 31) >= 28
    late = jnp.where(r >= 64, 2 * j, j) >= LATE
    grid = jnp.where(
        low,
        jnp.where(late, diag[...], up[...]),
        jnp.where(late, left[...], own[...]),
    )
    bottom = jnp.where(grid[32:64] == 1, 512, grid[0:32])
    upper = grid[64:80, 0:8]

    def column(codes, rows, row_of, lane_of):
        width = codes.shape[1]
        parts = jnp.concatenate([codes >> 4, codes & 15], axis=1).astype(F32).astype(BF16)
        pick = hot(row_of(iota((TOKENS, rows), 0)) == iota((TOKENS, rows), 1))
        spread = dot(pick, parts, 1, 0)
        t, lane = iota(spread.shape, 0), iota(spread.shape, 1)
        inside = jnp.where(lane < width, lane, lane - width) == lane_of(t)
        weight = jnp.where(lane < width, 16.0, 1.0)
        code = jnp.sum(jnp.where(inside, spread * weight, 0.0), axis=1, keepdims=True)
        return code.astype(jnp.int32)

    def source_row(t):
        return ((t >> 4) + (ROWS - SHIFT)) & (ROWS - 1)

    code_b = column(bottom, 32, source_row, lambda t: t & 15)
    code_t = column(upper, 16, lambda t: source_row(t) >> 1, lambda t: (t & 15) >> 1)
    copies[0].wait()
    copies[1].wait()
    copies[2].start()
    step = 256
    for at in range(0, TOKENS, step):
        here = slice(at, at + step)
        cb, ct = code_b[here], code_t[here]
        lane = iota((step, 512), 1)
        x = dot(hot(lane == cb), tables[0], 1, 0)
        x = jnp.where(cb == 512, mv[...].astype(F32).reshape(1, MODEL), x)
        x = (x + dot(hot(lane == ct), tables[1], 1, 0)).astype(BF16)
        emb[here] = x
        centred, inverse = moments(x.astype(F32))
        normed[here] = (centred * inverse).astype(BF16)
    copies[2].wait()
    proj[...] = dot(normed[...], weight[...], 1, 0).astype(BF16)


def merge(cot, grads, up, left, diag):
    p = iota((64, 1), 0) & 15
    corner = dot(late_cells(64, 16, False), diag[...], 1, 0)
    cot[0:64] = jnp.where(p >= LATE, corner, up[...].astype(F32)).astype(BF16)
    for at in range(0, OWN, 64):
        m, t = iota((64, MSG), 1), at + iota((64, MSG), 0)
        spread = hot(t == (m >> 2) * COLS + LATE + (m & 3))
        values = dot(spread, left[...], 1, 0)
        values = jnp.where(p >= LATE, values, grads[at : at + 64].astype(F32))
        cot[64 + at : 128 + at] = values.astype(BF16)


def attend_first(place, proj, normed, grads, up, left, diag, ow, att, gp, keep, send, cot, own, weight, sems, *held):
    copies = [
        pltpu.make_async_copy(grads, own, sems.at[0]),
        pltpu.make_async_copy(ow.at[:, 0:CW], weight, sems.at[1]),
    ]
    for copy in copies:
        copy.start()
    units = forward(0, place, proj, att, *held)
    copies[0].wait()
    merge(cot, own, up, left, diag)
    copies[1].wait()
    backward(units, place, normed, cot, weight, att, gp, keep, send, *held)


def attend_next(chunk, place, proj, normed, cot, ow, *refs):
    att, gp, keep, send, weight, sem, *held = refs[1:] if chunk > 1 else refs
    copy = pltpu.make_async_copy(ow.at[:, chunk * CW : (chunk + 1) * CW], weight, sem)
    copy.start()
    units = forward(chunk, place, proj, att, *held)
    copy.wait()
    backward(units, place, normed, cot, weight, att, gp, keep, send, *held)


def first_lanes():
    return iota((BAND, 128), 1) < 64


def split(x):
    none = jnp.zeros_like(x)
    first = first_lanes()
    return jnp.concatenate([jnp.where(first, x, none), jnp.where(first, none, x)], axis=0)


def forward(chunk, place, proj, att, share, share_bf, ds):
    tk, tq = iota((BAND, BAND), 0), iota((BAND, BAND), 1)

    def side(t):
        c = t & 15
        return ((c >= 4) & (c < 12)).astype(jnp.int32)

    same = side(tk) == side(tq)
    whole = (tk >> 6) == (tq >> 6)
    zero = jnp.zeros((BAND, BAND), F32)
    plain = jnp.where(same, zero, -1e30)
    first = jnp.where(whole | (place[0] != 0), plain, -1e30)
    units = []
    for p in range(CW // 128):
        for b in range(BANDS):
            here, at = slice(b * BAND, (b + 1) * BAND), chunk * CW + p * 128
            loads = [functools.partial(lambda c, h: proj[h, c : c + 128], i * HW + at, here) for i in range(3)]
            units.append((b, here, p * 128, *loads))
    for u, (b, here, at, q, k, v) in enumerate(units):
        share[u] = dot(split(k()), q(), 1, 1).reshape(2, BAND, BAND) * 0.125 + (first if b == 0 else plain)
    for u in range(len(units)):
        s = share[u]
        e = jnp.exp(s - jnp.max(s, axis=1, keepdims=True))
        e = e * (1.0 / jnp.sum(e, axis=1, keepdims=True))
        share[u] = e
        share_bf[u] = e.astype(BF16).reshape(2 * BAND, BAND)
    for u, (b, here, at, q, k, v) in enumerate(units):
        att[here, at : at + 128] = dot(share_bf[u], split(v()), 0, 0).astype(BF16)
    return units


def backward(units, place, normed, cot, ow, att, gp, keep, send, share, share_bf, ds):
    grad = dot(cot[...], ow[...], 1, 0).astype(BF16)
    lane = first_lanes()

    def pick(x):
        return jnp.where(lane, x[:BAND], x[BAND:])

    for u, (b, here, at, q, k, v) in enumerate(units):
        gs = dot(split(v()), grad[here, at : at + 128], 1, 1).reshape(2, BAND, BAND)
        e = share[u]
        delta = jnp.sum(e * gs, axis=1, keepdims=True)
        ds[u] = (e * (gs - delta) * 0.125).astype(BF16).reshape(2 * BAND, BAND)
    for u, (b, here, at, q, k, v) in enumerate(units):
        d = ds[u]
        gp[here, at : at + 128] = dot(d, split(k()), 0, 0).astype(BF16)
        gp[here, CW + at : CW + at + 128] = pick(dot(d, q(), 1, 0)).astype(BF16)
        gp[here, 2 * CW + at : 2 * CW + at + 128] = pick(
            dot(share_bf[u], grad[here, at : at + 128], 1, 0)
        ).astype(BF16)
    core = place[1]
    for half in range(2):
        for out, flip in ((send, 1), (keep, 0)):
            cut = pl.ds(pl.multiple_of(half * 512 + (core ^ flip) * 256, 256), 256)
            out[half, :, 0 : 3 * CW] = dot(normed[:, cut], gp[...], 0, 0).astype(out.dtype)
            out[half, :, 3 * CW :] = dot(cot[:, cut], att[...], 0, 0).astype(out.dtype)


def finish_kernel(emb, cot, wq, ow, *refs):
    atts, gps = refs[:CHUNKS], refs[CHUNKS : 2 * CHUNKS]
    mid, up, left, diag, tick, weight, last, big, sems = refs[2 * CHUNKS :]
    copies = [
        pltpu.make_async_copy(ow, last, sems.at[0]),
        pltpu.make_async_copy(wq, weight, sems.at[1]),
    ]
    for copy in copies:
        copy.start()
    copies[0].wait()

    def put(i, block, values):
        if block == 0:
            up[i] = values[:64]
            mid[i, 0:64] = values[64:]
        else:
            at = block * BAND - 64
            mid[i, at : at + BAND] = values

    def each(i, update):
        for block in range(BANDS):
            here = slice(block * BAND, (block + 1) * BAND)
            put(i, block, update(here, emb[here].astype(F32), big[here]).astype(BF16))

    def gradient(here, x, gst):
        centred, inverse = moments(x)
        standard = centred * inverse
        m1 = jnp.mean(gst, axis=1, keepdims=True)
        m2 = jnp.mean(gst * standard, axis=1, keepdims=True)
        return cot[here].astype(F32) + inverse * (gst - m1 - standard * m2)

    att = jnp.concatenate([a[...] for a in atts], axis=1)
    big[...] = dot(att, last[...], 1, 1)
    each(0, lambda here, x, branch: x + branch)
    copies[1].wait()
    parts = []
    for i in range(3):
        parts += [g[:, i * CW : (i + 1) * CW] for g in gps]
    big[...] = dot(jnp.concatenate(parts, axis=1), weight[...], 1, 1)
    each(1, gradient)
    pick, corner = late_cells(OWN, MSG, True), late_cells(64, 16, True)
    for i in range(2):
        left[i] = dot(pick, mid[i], 1, 0).astype(BF16)
        diag[i] = dot(corner, up[i], 1, 0).astype(BF16)
    tick[...] = jnp.zeros(tick.shape, F32)


def place_kernel(mid, up, left, diag, out, gin):
    late = (iota((64, 1), 0) & 15) >= LATE
    corner = late_cells(64, 16, False)
    for i, ref in enumerate((out, gin)):
        ref[OWN:] = jnp.where(late, dot(corner, diag[i], 1, 0), up[i].astype(F32)).astype(BF16)
        for at in range(0, OWN, 64):
            m, t = iota((64, MSG), 1), at + iota((64, MSG), 0)
            spread = hot(t == (m >> 2) * COLS + LATE + (m & 3))
            values = dot(spread, left[i], 1, 0)
            ref[at : at + 64] = jnp.where(late, values, mid[i, at : at + 64].astype(F32)).astype(BF16)


W = 4 * CW
Q = W // 4


def parity_core(place, a, b, keep, send):
    g = place[2] ^ place[3]
    for u in range(2):
        for out, v in ((keep, u ^ g), (send, u ^ g ^ 1)):
            out[u] = (a[u, :, v] + b[u, :, v].astype(F32)).astype(out.dtype)


def parity_pair(place, a, b, tick, keep, send):
    for out, u in ((keep, place[2]), (send, place[2] ^ 1)):
        out[...] = (a[u] + b[u].astype(F32)).astype(out.dtype)


def high_core(place, a, b, keep, send):
    for out, u in ((keep, place[2]), (send, place[2] ^ 1)):
        for v in range(2):
            out[v] = (a[u, :, v] + b[u, :, v].astype(F32)).astype(out.dtype)


def high_pair(place, a, b, tick, keep, send):
    for out, v in ((keep, place[3]), (send, place[3] ^ 1)):
        out[...] = (a[v] + b[v].astype(F32)).astype(out.dtype)


def parity_cut(place, a, b, keep, send):
    g = place[4] ^ place[5]
    for u in range(2):
        for out, v in ((keep, u ^ g), (send, u ^ g ^ 1)):
            cut = pl.ds(pl.multiple_of((2 * u + v) * Q, Q), Q)
            out[:, :, u * Q : (u + 1) * Q] = (a[:, :, cut] + b[:, :, cut].astype(F32)).astype(out.dtype)


def high_cut(place, a, b, keep, send):
    for out, u in ((keep, place[4]), (send, place[4] ^ 1)):
        cut = pl.ds(pl.multiple_of(u * 2 * Q, Q), 2 * Q)
        out[...] = (a[:, :, cut] + b[:, :, cut].astype(F32)).astype(out.dtype)


def join_kernel(a, b, c, d, out):
    out[:, :, 0 : 2 * Q] = (a[...] + b[...].astype(F32)).astype(BF16)
    out[:, :, 2 * Q :] = (c[...] + d[...].astype(F32)).astype(BF16)


def depth_kernel(ref, out):
    out[...] = sum(ref[i].astype(F32) for i in range(8)).astype(BF16)


def level_kernel(factor, place, r0, r1, r2, r3, qkv, outw):
    yh, yl = place[4], place[5]

    def add(a, b, at):
        return (a[:, at : at + Q].astype(F32) + b[:, at : at + Q].astype(F32)) * factor

    for a, b, g in ((r0, r3, yh ^ yl), (r1, r2, yh ^ yl ^ 1)):
        qkv[:, pl.ds(pl.multiple_of(g * HW, HW), CW)] = add(a, b, 0)
        second = add(a, b, Q)

        @pl.when(g == 1)
        def _():
            qkv[:, 2 * HW : 2 * HW + CW] = second

        @pl.when(g == 0)
        def _():
            outw[:, 0:CW] = second

    for a, b, high in ((r0, r1, yh), (r2, r3, yh ^ 1)):
        first, second = add(a, b, 2 * Q), add(a, b, 3 * Q)

        @pl.when(high == 0)
        def _():
            qkv[:, CW : 2 * CW] = first
            qkv[:, HW + CW : HW + 2 * CW] = second

        @pl.when(high == 1)
        def _():
            qkv[:, 2 * HW + CW : 2 * HW + 2 * CW] = first
            outw[:, CW : 2 * CW] = second


def permute(x, where):
    pairs = []
    for la in range(NLAT):
        for lo in range(NLON):
            tl, to = where(la, lo)
            pairs.append((la * NLON + lo, tl * NLON + to))
    return lax.ppermute(x, GRID, pairs)


def shift(x, down, right):
    return permute(x, lambda la, lo: ((la + down) % NLAT, (lo + right) % NLON))


def swap(x, axis, flip):
    return lax.ppermute(x, axis, [(i, i ^ flip) for i in range(lax.axis_size(axis))])


def swap_x(x, flip):
    return permute(x, lambda la, lo: (la ^ (flip & 2), lo ^ (flip & 1)))


def halve(name, kernel, shape, operands, specs):
    return call(
        kernel,
        [sds(shape, F32), sds(shape)],
        operands,
        specs,
        2**10,
        2**10,
        limit=16,
        name=name,
    )


def order(c):
    return (3, 1) if c % 2 else (1, 3)


def sum_core(place, keep, send, c):
    fold = (2, 8, 2, 16, W)
    kernel = high_core if c % 2 else parity_core
    recv = swap(send, "core", 1)
    operands = (place, keep.reshape(fold), recv.reshape(fold))
    return halve("sum_core", kernel, (2, 8, 16, W), operands, [smem(), vmem(), vmem()])


def sum_pair(place, keep, send, tick, c):
    kernel = high_pair if c % 2 else parity_pair
    recv = swap_x(send, order(c)[0])
    specs = [smem(), vmem(), vmem(), anywhere()]
    return halve("sum_pair", kernel, (8, 16, W), (place, keep, recv, tick), specs)


def sum_cut(place, keep, send, c):
    recv = swap_x(send, order(c)[1])
    kernel, flip = (high_cut, 3) if c % 2 else (parity_cut, 1)
    keep, send = halve("sum_cut", kernel, (8, 16, 2 * Q), (place, keep, recv), [smem(), vmem(), vmem()])
    return [keep, swap(send, "batch", flip)]


def shards(
    bottom_codes, mask_flags, top_codes, bottom_table, top_table, mask_vector, qkv_weight, out_weight, cotangent
):
    core, xh, xl = lax.axis_index("core"), lax.axis_index("xh"), lax.axis_index("xl")
    y = lax.axis_index("batch")
    place = jnp.stack([2 * xh + core, core, xh, xl, y >> 1, y & 1]).astype(jnp.int32)
    own = jnp.concatenate(
        [bottom_codes[0], mask_flags[0], jnp.pad(top_codes[0], ((0, 0), (0, 8)))], axis=0
    )
    near = (own, shift(own, 1, 0), shift(own, 0, 1), shift(own, 1, 1))
    pin = lambda x: pltpu.with_memory_space_constraint(x, pltpu.HBM)
    grads = pin(cotangent.reshape(TOKENS, MODEL))
    bottom_table, top_table = pin(bottom_table), pin(top_table)
    qkv_weight, out_weight = pin(qkv_weight), pin(out_weight)
    up, left, diag = call(
        slice_kernel,
        [sds((64, MODEL)), sds((MSG, MODEL)), sds((16, MODEL))],
        (grads,),
        [hbm()],
        2**28,
        2**21,
        name="slices",
        scratch=[pltpu.VMEM((TOKENS, MODEL), BF16), pltpu.SemaphoreType.DMA],
    )
    up, left, diag = shift(up, 1, 0), shift(left, 0, 1), shift(diag, 1, 1)
    emb, normed, proj = call(
        embed_kernel,
        [sds((TOKENS, MODEL)), sds((TOKENS, MODEL)), sds((TOKENS, 3 * HW))],
        (*near, bottom_table, top_table, mask_vector, qkv_weight),
        [vmem()] * 4 + [hbm(), hbm(), vmem(), hbm()],
        2 * TOKENS * 1024 * 2560,
        9 * 2**20,
        name="embed",
        scratch=[pltpu.VMEM((2, 512, MODEL), BF16), pltpu.VMEM((MODEL, 3 * HW), BF16), sems(3)],
    )
    outs = [sds((TOKENS, CW)), sds((TOKENS, 3 * CW)), sds((2, 256, W), F32), sds((2, 256, W))]
    column = pltpu.VMEM((MODEL, CW), BF16)
    units = BANDS * CW // 128
    held = [pltpu.VMEM((units, 2, BAND, BAND), F32)] + [pltpu.VMEM((units, 2 * BAND, BAND), BF16)] * 2
    att, gp, keep, send, cot = call(
        attend_first,
        outs + [sds((TOKENS, MODEL))],
        (place, proj, normed, grads, up, left, diag, out_weight),
        [smem(), vmem(), vmem(), hbm(), vmem(), vmem(), vmem(), hbm()],
        2**20,
        2**12,
        name="attend",
        scratch=[pltpu.VMEM((TOKENS, MODEL), BF16), column, sems(2), *held],
    )
    parts, cores = [(att, gp)], [sum_core(place, keep, send, 0)]
    for c in range(1, CHUNKS):
        after = [cores[c - 2][0]] if c > 1 else []
        att, gp, keep, send = call(
            functools.partial(attend_next, c),
            outs,
            (place, proj, normed, cot, out_weight, *after),
            [smem(), vmem(), vmem(), vmem(), hbm()] + [anywhere()] * len(after),
            2**20,
            2**12,
            name="attend",
            scratch=[column, pltpu.SemaphoreType.DMA, *held],
        )
        parts.append((att, gp))
        cores.append(sum_core(place, keep, send, c))
    *sent, tick = call(
        finish_kernel,
        [sds((2, OWN, MODEL)), sds((2, 64, MODEL)), sds((2, MSG, MODEL)), sds((2, 16, MODEL)), sds((8, 128), F32)],
        (emb, cot, qkv_weight, out_weight, *[p[0] for p in parts], *[p[1] for p in parts]),
        [vmem(), vmem(), hbm(), hbm()] + [vmem()] * 2 * CHUNKS,
        2**20,
        2**12,
        name="finish",
        scratch=[
            pltpu.VMEM((MODEL, 3 * HW), BF16),
            pltpu.VMEM((MODEL, HW), BF16),
            pltpu.VMEM((TOKENS, MODEL), F32),
            sems(2),
        ],
    )
    mid, up, left, diag = sent
    up, left, diag = shift(up, -1, 0), shift(left, 0, -1), shift(diag, -1, -1)
    summed = []
    for c, (keep, send) in enumerate(cores):
        keep, send = sum_pair(place, keep, send, diag if c else tick, c)
        summed += sum_cut(place, keep, send, c)
    out, gin = call(
        place_kernel,
        [sds((TOKENS, MODEL))] * 2,
        (mid, up, left, diag),
        [vmem()] * 4,
        2**28,
        5 * 2**20,
        limit=24,
        name="place",
    )
    factor = 1.0 / math.sqrt(TOKENS * NB * NLAT * NLON)
    joined = call(
        join_kernel,
        sds((8, 16, 4 * Q)),
        summed,
        [vmem()] * 4,
        2**19,
        2**21,
        limit=16,
        name="join",
    )
    depth = lax.all_to_all(joined, "z", 0, 0, tiled=True)
    small = dict(flops=2**17, nbytes=2**19, limit=16)
    total = call(depth_kernel, sds((16, 4 * Q)), (depth,), [vmem()], name="depth", **small)
    g_qkv, g_out = call(
        functools.partial(level_kernel, factor),
        [sds((16, 3 * HW), F32), sds((16, HW), F32)],
        (place, total, *[swap(total, "batch", d) for d in (1, 2, 3)]),
        [smem()] + [vmem()] * 4,
        name="level",
        **small,
    )
    shape = (1, ROWS, COLS, MODEL)
    return (out.reshape(shape), gin.reshape(shape), g_qkv, g_out)


def solution(mesh):
    devices = mesh.devices.reshape(NB, 2, 2, 8, 2)
    fine = jax.sharding.Mesh(devices, ("batch",) + GRID)
    rows, cols = ("xh", "core"), ("z", "xl")
    grid, whole = P("batch", rows, cols), P()
    return jax.shard_map(
        shards,
        mesh=fine,
        in_specs=(grid, grid, grid, whole, whole, whole, whole, whole, P("batch", rows, cols, None)),
        out_specs=(
            P("batch", rows, cols, None),
            P("batch", rows, cols, None),
            P(GRID, None),
            P(GRID, None),
        ),
        check_vma=False,
    )
```

```python
import functools
import math

import jax
import jax.numpy as jnp
from jax import lax
from jax.experimental import pallas as pl
from jax.experimental.pallas import tpu as pltpu
from jax.sharding import PartitionSpec as P

HEADS = 8
HDIM = 64
WIN = 8
HW = 512
SHIFT = 4
EPS = 1e-05
MODEL = 1024
ROWS, COLS = 32, 16
TOKENS = ROWS * COLS
BAND = WIN * COLS
BANDS = TOKENS // BAND
CHUNKS = 2
CW = HW // CHUNKS
F32 = jnp.float32
BF16 = jnp.bfloat16
GRID = ("xh", "core", "z", "xl")
NB, NLAT, NLON = 4, 4, 16


def dot(a, b, ca, cb):
    return lax.dot_general(a, b, (((ca,), (cb,)), ((), ())), preferred_element_type=F32)


def vmem():
    return pl.BlockSpec(memory_space=pltpu.VMEM)


def smem():
    return pl.BlockSpec(memory_space=pltpu.SMEM)


def call(kernel, outs, operands, specs, flops, nbytes, trans=0, limit=40, name=None, scratch=()):
    return pl.pallas_call(
        kernel,
        out_shape=outs,
        in_specs=specs,
        out_specs=jax.tree.map(lambda _: vmem(), outs),
        scratch_shapes=scratch,
        compiler_params=pltpu.CompilerParams(vmem_limit_bytes=limit * 2**20),
        cost_estimate=pl.CostEstimate(flops=flops, bytes_accessed=nbytes, transcendentals=trans),
        name=name,
    )(*operands)


def hbm():
    return pl.BlockSpec(memory_space=pltpu.HBM)


def anywhere():
    return pl.BlockSpec(memory_space=pl.ANY)


def sems(n):
    return pltpu.SemaphoreType.DMA((n,))


def sds(shape, dtype=BF16):
    return jax.ShapeDtypeStruct(shape, dtype)


def iota(shape, dim):
    return lax.broadcasted_iota(jnp.int32, shape, dim)


def moments(x):
    mean = jnp.mean(x, axis=1, keepdims=True)
    centred = x - mean
    inverse = lax.rsqrt(jnp.mean(centred * centred, axis=1, keepdims=True) + EPS)
    return centred, inverse


MSG = SHIFT * (ROWS - SHIFT)
OWN = (ROWS - SHIFT) * COLS
LATE = COLS - SHIFT


def hot(mask):
    return mask.astype(F32).astype(BF16)


def late_cells(cells, rows, by_row):
    dims = (0, 1) if by_row else (1, 0)
    shape = (rows, cells) if by_row else (cells, rows)
    m, t = iota(shape, dims[0]), iota(shape, dims[1])
    return hot(t == (m >> 2) * COLS + LATE + (m & 3))


def slice_kernel(cot, up, left, diag, held, sem):
    copy = pltpu.make_async_copy(cot, held, sem)
    copy.start()
    pick, corner = late_cells(OWN, MSG, True), late_cells(64, 16, True)
    copy.wait()
    up[...] = held[OWN:]
    left[...] = dot(pick, held[:OWN], 1, 0).astype(BF16)
    diag[...] = dot(corner, held[OWN:], 1, 0).astype(BF16)


def embed_kernel(own, up, left, diag, bt, tt, mv, wq, emb, normed, proj, tables, masked, weight, sems):
    copies = [
        pltpu.make_async_copy(bt, tables.at[0], sems.at[0]),
        pltpu.make_async_copy(tt, tables.at[1], sems.at[1]),
        pltpu.make_async_copy(mv, masked, sems.at[2]),
        pltpu.make_async_copy(wq, weight, sems.at[3]),
    ]
    for copy in copies[:3]:
        copy.start()
    r, j = iota((80, 16), 0), iota((80, 16), 1)
    low = jnp.where(r >= 64, r - 50, r & 31) >= 28
    late = jnp.where(r >= 64, 2 * j, j) >= LATE
    grid = jnp.where(
        low,
        jnp.where(late, diag[...], up[...]),
        jnp.where(late, left[...], own[...]),
    )
    bottom = jnp.where(grid[32:64] == 1, 512, grid[0:32])
    upper = grid[64:80, 0:8]

    def column(codes, rows, row_of, lane_of):
        width = codes.shape[1]
        parts = jnp.concatenate([codes >> 4, codes & 15], axis=1).astype(F32).astype(BF16)
        pick = hot(row_of(iota((TOKENS, rows), 0)) == iota((TOKENS, rows), 1))
        spread = dot(pick, parts, 1, 0)
        t, lane = iota(spread.shape, 0), iota(spread.shape, 1)
        inside = jnp.where(lane < width, lane, lane - width) == lane_of(t)
        weight = jnp.where(lane < width, 16.0, 1.0)
        code = jnp.sum(jnp.where(inside, spread * weight, 0.0), axis=1, keepdims=True)
        return code.astype(jnp.int32)

    def source_row(t):
        return ((t >> 4) + (ROWS - SHIFT)) & (ROWS - 1)

    code_b = column(bottom, 32, source_row, lambda t: t & 15)
    code_t = column(upper, 16, lambda t: source_row(t) >> 1, lambda t: (t & 15) >> 1)
    for copy in copies[:3]:
        copy.wait()
    copies[3].start()
    step = 256
    for at in range(0, TOKENS, step):
        here = slice(at, at + step)
        cb, ct = code_b[here], code_t[here]
        lane = iota((step, 512), 1)
        x = dot(hot(lane == cb), tables[0], 1, 0)
        x = jnp.where(cb == 512, masked[...].astype(F32).reshape(1, MODEL), x)
        x = (x + dot(hot(lane == ct), tables[1], 1, 0)).astype(BF16)
        emb[here] = x
        centred, inverse = moments(x.astype(F32))
        normed[here] = (centred * inverse).astype(BF16)
    copies[3].wait()
    proj[...] = dot(normed[...], weight[...], 1, 0).astype(BF16)


def merge(cot, grads, up, left, diag):
    p = iota((64, 1), 0) & 15
    corner = dot(late_cells(64, 16, False), diag[...], 1, 0)
    cot[0:64] = jnp.where(p >= LATE, corner, up[...].astype(F32)).astype(BF16)
    for at in range(0, OWN, 64):
        m, t = iota((64, MSG), 1), at + iota((64, MSG), 0)
        spread = hot(t == (m >> 2) * COLS + LATE + (m & 3))
        values = dot(spread, left[...], 1, 0)
        values = jnp.where(p >= LATE, values, grads[at : at + 64].astype(F32))
        cot[64 + at : 128 + at] = values.astype(BF16)


def attend_first(place, proj, normed, grads, up, left, diag, ow, att, gp, keep, send, cot, own, weight, sems, *held):
    copies = [
        pltpu.make_async_copy(grads, own, sems.at[0]),
        pltpu.make_async_copy(ow.at[:, 0:CW], weight, sems.at[1]),
    ]
    for copy in copies:
        copy.start()
    units = forward(0, place, proj, att, *held)
    copies[0].wait()
    merge(cot, own, up, left, diag)
    copies[1].wait()
    backward(units, place, normed, cot, weight, att, gp, keep, send, *held)


def attend_next(chunk, place, proj, normed, cot, ow, *refs):
    att, gp, keep, send, weight, sem, *held = refs[1:] if chunk > 1 else refs
    copy = pltpu.make_async_copy(ow.at[:, chunk * CW : (chunk + 1) * CW], weight, sem)
    copy.start()
    units = forward(chunk, place, proj, att, *held)
    copy.wait()
    backward(units, place, normed, cot, weight, att, gp, keep, send, *held)


def first_lanes():
    return iota((BAND, 128), 1) < 64


def split(x):
    none = jnp.zeros_like(x)
    first = first_lanes()
    return jnp.concatenate([jnp.where(first, x, none), jnp.where(first, none, x)], axis=0)


def forward(chunk, place, proj, att, share, share_bf, ds):
    tk, tq = iota((BAND, BAND), 0), iota((BAND, BAND), 1)

    def side(t):
        c = t & 15
        return ((c >= 4) & (c < 12)).astype(jnp.int32)

    same = side(tk) == side(tq)
    whole = (tk >> 6) == (tq >> 6)
    zero = jnp.zeros((BAND, BAND), F32)
    plain = jnp.where(same, zero, -1e30)
    first = jnp.where(whole | (place[0] != 0), plain, -1e30)
    units = []
    for p in range(CW // 128):
        for b in range(BANDS):
            here, at = slice(b * BAND, (b + 1) * BAND), chunk * CW + p * 128
            loads = [functools.partial(lambda c, h: proj[h, c : c + 128], i * HW + at, here) for i in range(3)]
            units.append((b, here, p * 128, *loads))
    for u, (b, here, at, q, k, v) in enumerate(units):
        share[u] = dot(split(k()), q(), 1, 1).reshape(2, BAND, BAND) * 0.125 + (first if b == 0 else plain)
    for u in range(len(units)):
        s = share[u]
        e = jnp.exp(s - jnp.max(s, axis=1, keepdims=True))
        e = e * (1.0 / jnp.sum(e, axis=1, keepdims=True))
        share[u] = e
        share_bf[u] = e.astype(BF16).reshape(2 * BAND, BAND)
    for u, (b, here, at, q, k, v) in enumerate(units):
        att[here, at : at + 128] = dot(share_bf[u], split(v()), 0, 0).astype(BF16)
    return units


def backward(units, place, normed, cot, ow, att, gp, keep, send, share, share_bf, ds):
    grad = dot(cot[...], ow[...], 1, 0).astype(BF16)
    lane = first_lanes()

    def pick(x):
        return jnp.where(lane, x[:BAND], x[BAND:])

    for u, (b, here, at, q, k, v) in enumerate(units):
        gs = dot(split(v()), grad[here, at : at + 128], 1, 1).reshape(2, BAND, BAND)
        e = share[u]
        delta = jnp.sum(e * gs, axis=1, keepdims=True)
        ds[u] = (e * (gs - delta) * 0.125).astype(BF16).reshape(2 * BAND, BAND)
    for u, (b, here, at, q, k, v) in enumerate(units):
        d = ds[u]
        gp[here, at : at + 128] = dot(d, split(k()), 0, 0).astype(BF16)
        gp[here, CW + at : CW + at + 128] = pick(dot(d, q(), 1, 0)).astype(BF16)
        gp[here, 2 * CW + at : 2 * CW + at + 128] = pick(
            dot(share_bf[u], grad[here, at : at + 128], 1, 0)
        ).astype(BF16)
    core = place[1]
    for half in range(2):
        for out, flip in ((send, 1), (keep, 0)):
            cut = pl.ds(pl.multiple_of(half * 512 + (core ^ flip) * 256, 256), 256)
            out[half, :, 0 : 3 * CW] = dot(normed[:, cut], gp[...], 0, 0).astype(out.dtype)
            out[half, :, 3 * CW :] = dot(cot[:, cut], att[...], 0, 0).astype(out.dtype)


def finish_kernel(emb, cot, wq, ow, *refs):
    atts, gps = refs[:CHUNKS], refs[CHUNKS : 2 * CHUNKS]
    mid, up, left, diag, tick, weight, last, big, sems = refs[2 * CHUNKS :]
    copies = [
        pltpu.make_async_copy(ow, last, sems.at[0]),
        pltpu.make_async_copy(wq, weight, sems.at[1]),
    ]
    for copy in copies:
        copy.start()
    copies[0].wait()

    def put(i, block, values):
        if block == 0:
            up[i] = values[:64]
            mid[i, 0:64] = values[64:]
        else:
            at = block * BAND - 64
            mid[i, at : at + BAND] = values

    def each(i, update):
        for block in range(BANDS):
            here = slice(block * BAND, (block + 1) * BAND)
            put(i, block, update(here, emb[here].astype(F32), big[here]).astype(BF16))

    def gradient(here, x, gst):
        centred, inverse = moments(x)
        standard = centred * inverse
        m1 = jnp.mean(gst, axis=1, keepdims=True)
        m2 = jnp.mean(gst * standard, axis=1, keepdims=True)
        return cot[here].astype(F32) + inverse * (gst - m1 - standard * m2)

    att = jnp.concatenate([a[...] for a in atts], axis=1)
    big[...] = dot(att, last[...], 1, 1)
    each(0, lambda here, x, branch: x + branch)
    copies[1].wait()
    parts = []
    for i in range(3):
        parts += [g[:, i * CW : (i + 1) * CW] for g in gps]
    big[...] = dot(jnp.concatenate(parts, axis=1), weight[...], 1, 1)
    each(1, gradient)
    pick, corner = late_cells(OWN, MSG, True), late_cells(64, 16, True)
    for i in range(2):
        left[i] = dot(pick, mid[i], 1, 0).astype(BF16)
        diag[i] = dot(corner, up[i], 1, 0).astype(BF16)
    tick[...] = jnp.zeros(tick.shape, F32)


def place_kernel(mid, up, left, diag, out, gin):
    late = (iota((64, 1), 0) & 15) >= LATE
    corner = late_cells(64, 16, False)
    for i, ref in enumerate((out, gin)):
        ref[OWN:] = jnp.where(late, dot(corner, diag[i], 1, 0), up[i].astype(F32)).astype(BF16)
        for at in range(0, OWN, 64):
            m, t = iota((64, MSG), 1), at + iota((64, MSG), 0)
            spread = hot(t == (m >> 2) * COLS + LATE + (m & 3))
            values = dot(spread, left[i], 1, 0)
            ref[at : at + 64] = jnp.where(late, values, mid[i, at : at + 64].astype(F32)).astype(BF16)


W = 4 * CW
Q = W // 4


def parity_core(place, a, b, keep, send):
    g = place[2] ^ place[3]
    for u in range(2):
        for out, v in ((keep, u ^ g), (send, u ^ g ^ 1)):
            out[u] = (a[u, :, v] + b[u, :, v].astype(F32)).astype(out.dtype)


def parity_pair(place, a, b, tick, halo, keep, send, passed):
    passed[...] = halo[...]
    for out, u in ((keep, place[2]), (send, place[2] ^ 1)):
        out[...] = (a[u] + b[u].astype(F32)).astype(out.dtype)


def high_core(place, a, b, keep, send):
    for out, u in ((keep, place[2]), (send, place[2] ^ 1)):
        for v in range(2):
            out[v] = (a[u, :, v] + b[u, :, v].astype(F32)).astype(out.dtype)


def high_pair(place, a, b, tick, keep, send):
    for out, v in ((keep, place[3]), (send, place[3] ^ 1)):
        out[...] = (a[v] + b[v].astype(F32)).astype(out.dtype)


def parity_cut(place, a, b, keep, send):
    g = place[4] ^ place[5]
    for u in range(2):
        for out, v in ((keep, u ^ g), (send, u ^ g ^ 1)):
            cut = pl.ds(pl.multiple_of((2 * u + v) * Q, Q), Q)
            out[:, :, u * Q : (u + 1) * Q] = (a[:, :, cut] + b[:, :, cut].astype(F32)).astype(out.dtype)


def high_cut(place, a, b, keep, send):
    for out, u in ((keep, place[4]), (send, place[4] ^ 1)):
        cut = pl.ds(pl.multiple_of(u * 2 * Q, Q), 2 * Q)
        out[...] = (a[:, :, cut] + b[:, :, cut].astype(F32)).astype(out.dtype)


def join_kernel(a, b, c, d, arrived, out):
    out[:, :, 0 : 2 * Q] = (a[...] + b[...].astype(F32)).astype(BF16)
    out[:, :, 2 * Q :] = (c[...] + d[...].astype(F32)).astype(BF16)


def depth_kernel(ref, out):
    out[...] = sum(ref[i].astype(F32) for i in range(8)).astype(BF16)


def level_kernel(factor, place, r0, r1, r2, r3, qkv, outw):
    yh, yl = place[4], place[5]

    def add(a, b, at):
        return (a[:, at : at + Q].astype(F32) + b[:, at : at + Q].astype(F32)) * factor

    for a, b, g in ((r0, r3, yh ^ yl), (r1, r2, yh ^ yl ^ 1)):
        qkv[:, pl.ds(pl.multiple_of(g * HW, HW), CW)] = add(a, b, 0)
        second = add(a, b, Q)

        @pl.when(g == 1)
        def _():
            qkv[:, 2 * HW : 2 * HW + CW] = second

        @pl.when(g == 0)
        def _():
            outw[:, 0:CW] = second

    for a, b, high in ((r0, r1, yh), (r2, r3, yh ^ 1)):
        first, second = add(a, b, 2 * Q), add(a, b, 3 * Q)

        @pl.when(high == 0)
        def _():
            qkv[:, CW : 2 * CW] = first
            qkv[:, HW + CW : HW + 2 * CW] = second

        @pl.when(high == 1)
        def _():
            qkv[:, 2 * HW + CW : 2 * HW + 2 * CW] = first
            outw[:, CW : 2 * CW] = second


def permute(x, where):
    pairs = []
    for la in range(NLAT):
        for lo in range(NLON):
            tl, to = where(la, lo)
            pairs.append((la * NLON + lo, tl * NLON + to))
    return lax.ppermute(x, GRID, pairs)


def shift(x, down, right):
    return permute(x, lambda la, lo: ((la + down) % NLAT, (lo + right) % NLON))


def swap(x, axis, flip):
    return lax.ppermute(x, axis, [(i, i ^ flip) for i in range(lax.axis_size(axis))])


def swap_x(x, flip):
    return permute(x, lambda la, lo: (la ^ (flip & 2), lo ^ (flip & 1)))


def halve(name, kernel, shape, operands, specs, more=()):
    return call(
        kernel,
        [sds(shape, F32), sds(shape), *more],
        operands,
        specs,
        2**10,
        2**10,
        limit=16,
        name=name,
    )


def order(c):
    return (3, 1) if c % 2 else (1, 3)


def sum_core(place, keep, send, c):
    fold = (2, 8, 2, 16, W)
    kernel = high_core if c % 2 else parity_core
    recv = swap(send, "core", 1)
    operands = (place, keep.reshape(fold), recv.reshape(fold))
    return halve("sum_core", kernel, (2, 8, 16, W), operands, [smem(), vmem(), vmem()])


def sum_pair(place, keep, send, tick, c, halo=()):
    kernel = high_pair if c % 2 else parity_pair
    recv = swap_x(send, order(c)[0])
    specs = [smem(), vmem(), vmem(), anywhere()] + [vmem()] * len(halo)
    return halve("sum_pair", kernel, (8, 16, W), (place, keep, recv, tick, *halo), specs, [sds(h.shape) for h in halo])


def sum_cut(place, keep, send, c):
    recv = swap_x(send, order(c)[1])
    kernel, flip = (high_cut, 3) if c % 2 else (parity_cut, 1)
    keep, send = halve("sum_cut", kernel, (8, 16, 2 * Q), (place, keep, recv), [smem(), vmem(), vmem()])
    return [keep, swap(send, "batch", flip)]


def shards(
    bottom_codes, mask_flags, top_codes, bottom_table, top_table, mask_vector, qkv_weight, out_weight, cotangent
):
    core, xh, xl = lax.axis_index("core"), lax.axis_index("xh"), lax.axis_index("xl")
    y = lax.axis_index("batch")
    place = jnp.stack([2 * xh + core, core, xh, xl, y >> 1, y & 1]).astype(jnp.int32)
    own = jnp.concatenate(
        [bottom_codes[0], mask_flags[0], jnp.pad(top_codes[0], ((0, 0), (0, 8)))], axis=0
    )
    near = (own, shift(own, 1, 0), shift(own, 0, 1), shift(own, 1, 1))
    pin = lambda x: pltpu.with_memory_space_constraint(x, pltpu.HBM)
    grads = pin(cotangent.reshape(TOKENS, MODEL))
    bottom_table, top_table = pin(bottom_table), pin(top_table)
    mask_vector, qkv_weight, out_weight = pin(mask_vector), pin(qkv_weight), pin(out_weight)
    up, left, diag = call(
        slice_kernel,
        [sds((64, MODEL)), sds((MSG, MODEL)), sds((16, MODEL))],
        (grads,),
        [hbm()],
        2**28,
        2**21,
        name="slices",
        scratch=[pltpu.VMEM((TOKENS, MODEL), BF16), pltpu.SemaphoreType.DMA],
    )
    up, left, diag = shift(up, 1, 0), shift(left, 0, 1), shift(diag, 1, 1)
    emb, normed, proj = call(
        embed_kernel,
        [sds((TOKENS, MODEL)), sds((TOKENS, MODEL)), sds((TOKENS, 3 * HW))],
        (*near, bottom_table, top_table, mask_vector, qkv_weight),
        [vmem()] * 4 + [hbm()] * 4,
        2 * TOKENS * 1024 * 2560,
        9 * 2**20,
        name="embed",
        scratch=[
            pltpu.VMEM((2, 512, MODEL), BF16),
            pltpu.VMEM((MODEL,), BF16),
            pltpu.VMEM((MODEL, 3 * HW), BF16),
            sems(4),
        ],
    )
    outs = [sds((TOKENS, CW)), sds((TOKENS, 3 * CW)), sds((2, 256, W), F32), sds((2, 256, W))]
    column = pltpu.VMEM((MODEL, CW), BF16)
    units = BANDS * CW // 128
    held = [pltpu.VMEM((units, 2, BAND, BAND), F32)] + [pltpu.VMEM((units, 2 * BAND, BAND), BF16)] * 2
    att, gp, keep, send, cot = call(
        attend_first,
        outs + [sds((TOKENS, MODEL))],
        (place, proj, normed, grads, up, left, diag, out_weight),
        [smem(), vmem(), vmem(), hbm(), vmem(), vmem(), vmem(), hbm()],
        2**20,
        2**12,
        name="attend",
        scratch=[pltpu.VMEM((TOKENS, MODEL), BF16), column, sems(2), *held],
    )
    parts, cores = [(att, gp)], [sum_core(place, keep, send, 0)]
    for c in range(1, CHUNKS):
        after = [cores[c - 2][0]] if c > 1 else []
        att, gp, keep, send = call(
            functools.partial(attend_next, c),
            outs,
            (place, proj, normed, cot, out_weight, *after),
            [smem(), vmem(), vmem(), vmem(), hbm()] + [anywhere()] * len(after),
            2**20,
            2**12,
            name="attend",
            scratch=[column, pltpu.SemaphoreType.DMA, *held],
        )
        parts.append((att, gp))
        cores.append(sum_core(place, keep, send, c))
    *sent, tick = call(
        finish_kernel,
        [sds((2, OWN, MODEL)), sds((2, 64, MODEL)), sds((2, MSG, MODEL)), sds((2, 16, MODEL)), sds((8, 128), F32)],
        (emb, cot, qkv_weight, out_weight, *[p[0] for p in parts], *[p[1] for p in parts]),
        [vmem(), vmem(), hbm(), hbm()] + [vmem()] * 2 * CHUNKS,
        2**20,
        2**12,
        name="finish",
        scratch=[
            pltpu.VMEM((MODEL, 3 * HW), BF16),
            pltpu.VMEM((MODEL, HW), BF16),
            pltpu.VMEM((TOKENS, MODEL), F32),
            sems(2),
        ],
    )
    mid, up, left, diag = sent
    up, diag = shift(up, -1, 0), shift(diag, -1, -1)
    (keep0, send0), (keep1, send1) = cores
    keep0, send0, left = sum_pair(place, keep0, send0, tick, 0, (left,))
    keep1, send1 = sum_pair(place, keep1, send1, diag, 1)
    left = shift(left, 0, -1)
    summed = sum_cut(place, keep0, send0, 0) + sum_cut(place, keep1, send1, 1)
    out, gin = call(
        place_kernel,
        [sds((TOKENS, MODEL))] * 2,
        (mid, up, left, diag),
        [vmem()] * 4,
        2**28,
        5 * 2**20,
        limit=24,
        name="place",
    )
    factor = 1.0 / math.sqrt(TOKENS * NB * NLAT * NLON)
    joined = call(
        join_kernel,
        sds((8, 16, 4 * Q)),
        (*summed, left),
        [vmem()] * 4 + [anywhere()],
        2**19,
        2**21,
        limit=16,
        name="join",
    )
    depth = lax.all_to_all(joined, "z", 0, 0, tiled=True)
    small = dict(flops=2**17, nbytes=2**19, limit=16)
    total = call(depth_kernel, sds((16, 4 * Q)), (depth,), [vmem()], name="depth", **small)
    g_qkv, g_out = call(
        functools.partial(level_kernel, factor),
        [sds((16, 3 * HW), F32), sds((16, HW), F32)],
        (place, total, *[swap(total, "batch", d) for d in (1, 2, 3)]),
        [smem()] + [vmem()] * 4,
        name="level",
        **small,
    )
    shape = (1, ROWS, COLS, MODEL)
    return (out.reshape(shape), gin.reshape(shape), g_qkv, g_out)


def solution(mesh):
    devices = mesh.devices.reshape(NB, 2, 2, 8, 2)
    fine = jax.sharding.Mesh(devices, ("batch",) + GRID)
    rows, cols = ("xh", "core"), ("z", "xl")
    grid, whole = P("batch", rows, cols), P()
    return jax.shard_map(
        shards,
        mesh=fine,
        in_specs=(grid, grid, grid, whole, whole, whole, whole, whole, P("batch", rows, cols, None)),
        out_specs=(
            P("batch", rows, cols, None),
            P("batch", rows, cols, None),
            P(GRID, None),
            P(GRID, None),
        ),
        check_vma=False,
    )
```

```python
import functools
import math

import jax
import jax.numpy as jnp
from jax import lax
from jax.experimental import pallas as pl
from jax.experimental.pallas import tpu as pltpu
from jax.sharding import PartitionSpec as P

HEADS = 8
HDIM = 64
WIN = 8
HW = 512
SHIFT = 4
EPS = 1e-05
MODEL = 1024
ROWS, COLS = 32, 16
TOKENS = ROWS * COLS
BAND = WIN * COLS
BANDS = TOKENS // BAND
CHUNKS = 2
CW = HW // CHUNKS
F32 = jnp.float32
BF16 = jnp.bfloat16
GRID = ("xh", "core", "z", "xl")
NB, NLAT, NLON = 4, 4, 16


def dot(a, b, ca, cb):
    return lax.dot_general(a, b, (((ca,), (cb,)), ((), ())), preferred_element_type=F32)


def vmem():
    return pl.BlockSpec(memory_space=pltpu.VMEM)


def smem():
    return pl.BlockSpec(memory_space=pltpu.SMEM)


def call(kernel, outs, operands, specs, flops, nbytes, trans=0, limit=40, name=None, scratch=()):
    return pl.pallas_call(
        kernel,
        out_shape=outs,
        in_specs=specs,
        out_specs=jax.tree.map(lambda _: vmem(), outs),
        scratch_shapes=scratch,
        compiler_params=pltpu.CompilerParams(vmem_limit_bytes=limit * 2**20),
        cost_estimate=pl.CostEstimate(flops=flops, bytes_accessed=nbytes, transcendentals=trans),
        name=name,
    )(*operands)


def hbm():
    return pl.BlockSpec(memory_space=pltpu.HBM)


def anywhere():
    return pl.BlockSpec(memory_space=pl.ANY)


def sems(n):
    return pltpu.SemaphoreType.DMA((n,))


def sds(shape, dtype=BF16):
    return jax.ShapeDtypeStruct(shape, dtype)


def iota(shape, dim):
    return lax.broadcasted_iota(jnp.int32, shape, dim)


def moments(x):
    mean = jnp.mean(x, axis=1, keepdims=True)
    centred = x - mean
    inverse = lax.rsqrt(jnp.mean(centred * centred, axis=1, keepdims=True) + EPS)
    return centred, inverse


MSG = SHIFT * (ROWS - SHIFT)
OWN = (ROWS - SHIFT) * COLS
LATE = COLS - SHIFT


def hot(mask):
    return mask.astype(F32).astype(BF16)


def late_cells(cells, rows, by_row):
    dims = (0, 1) if by_row else (1, 0)
    shape = (rows, cells) if by_row else (cells, rows)
    m, t = iota(shape, dims[0]), iota(shape, dims[1])
    return hot(t == (m >> 2) * COLS + LATE + (m & 3))


def slice_kernel(cot, up, left, diag, held, sem):
    copy = pltpu.make_async_copy(cot, held, sem)
    copy.start()
    pick, corner = late_cells(OWN, MSG, True), late_cells(64, 16, True)
    copy.wait()
    up[...] = held[OWN:]
    left[...] = dot(pick, held[:OWN], 1, 0).astype(BF16)
    diag[...] = dot(corner, held[OWN:], 1, 0).astype(BF16)


def embed_kernel(own, up, left, diag, bt, tt, mv, wq, emb, normed, proj, tables, masked, weight, sems):
    copies = [
        pltpu.make_async_copy(bt, tables.at[0], sems.at[0]),
        pltpu.make_async_copy(tt, tables.at[1], sems.at[1]),
        pltpu.make_async_copy(mv, masked, sems.at[2]),
        pltpu.make_async_copy(wq, weight, sems.at[3]),
    ]
    for copy in copies[:3]:
        copy.start()
    r, j = iota((80, 16), 0), iota((80, 16), 1)
    low = jnp.where(r >= 64, r - 50, r & 31) >= 28
    late = jnp.where(r >= 64, 2 * j, j) >= LATE
    grid = jnp.where(
        low,
        jnp.where(late, diag[...], up[...]),
        jnp.where(late, left[...], own[...]),
    )
    bottom = jnp.where(grid[32:64] == 1, 512, grid[0:32])
    upper = grid[64:80, 0:8]

    def column(codes, rows, row_of, lane_of):
        width = codes.shape[1]
        parts = jnp.concatenate([codes >> 4, codes & 15], axis=1).astype(F32).astype(BF16)
        pick = hot(row_of(iota((TOKENS, rows), 0)) == iota((TOKENS, rows), 1))
        spread = dot(pick, parts, 1, 0)
        t, lane = iota(spread.shape, 0), iota(spread.shape, 1)
        inside = jnp.where(lane < width, lane, lane - width) == lane_of(t)
        weight = jnp.where(lane < width, 16.0, 1.0)
        code = jnp.sum(jnp.where(inside, spread * weight, 0.0), axis=1, keepdims=True)
        return code.astype(jnp.int32)

    def source_row(t):
        return ((t >> 4) + (ROWS - SHIFT)) & (ROWS - 1)

    code_b = column(bottom, 32, source_row, lambda t: t & 15)
    code_t = column(upper, 16, lambda t: source_row(t) >> 1, lambda t: (t & 15) >> 1)
    for copy in copies[:3]:
        copy.wait()
    copies[3].start()
    step = 256
    for at in range(0, TOKENS, step):
        here = slice(at, at + step)
        cb, ct = code_b[here], code_t[here]
        lane = iota((step, 512), 1)
        x = dot(hot(lane == cb), tables[0], 1, 0)
        x = jnp.where(cb == 512, masked[...].astype(F32).reshape(1, MODEL), x)
        x = (x + dot(hot(lane == ct), tables[1], 1, 0)).astype(BF16)
        emb[here] = x
        centred, inverse = moments(x.astype(F32))
        normed[here] = (centred * inverse).astype(BF16)
    copies[3].wait()
    proj[...] = dot(normed[...], weight[...], 1, 0).astype(BF16)


def merge(cot, grads, up, left, diag):
    p = iota((64, 1), 0) & 15
    corner = dot(late_cells(64, 16, False), diag[...], 1, 0)
    cot[0:64] = jnp.where(p >= LATE, corner, up[...].astype(F32)).astype(BF16)
    for at in range(0, OWN, 64):
        m, t = iota((64, MSG), 1), at + iota((64, MSG), 0)
        spread = hot(t == (m >> 2) * COLS + LATE + (m & 3))
        values = dot(spread, left[...], 1, 0)
        values = jnp.where(p >= LATE, values, grads[at : at + 64].astype(F32))
        cot[64 + at : 128 + at] = values.astype(BF16)


def attend_first(place, proj, normed, grads, up, left, diag, ow, att, gp, keep, send, cot, own, weight, sems, *held):
    copies = [
        pltpu.make_async_copy(grads, own, sems.at[0]),
        pltpu.make_async_copy(ow.at[:, 0:CW], weight, sems.at[1]),
    ]
    for copy in copies:
        copy.start()
    units = forward(0, place, proj, att, *held)
    copies[0].wait()
    merge(cot, own, up, left, diag)
    copies[1].wait()
    backward(units, place, normed, cot, weight, att, gp, keep, send, *held)


def attend_next(chunk, place, proj, normed, cot, ow, *refs):
    att, gp, keep, send, weight, sem, *held = refs[1:] if chunk > 1 else refs
    copy = pltpu.make_async_copy(ow.at[:, chunk * CW : (chunk + 1) * CW], weight, sem)
    copy.start()
    units = forward(chunk, place, proj, att, *held)
    copy.wait()
    backward(units, place, normed, cot, weight, att, gp, keep, send, *held)


def first_lanes():
    return iota((BAND, 128), 1) < 64


def split(x):
    none = jnp.zeros_like(x)
    first = first_lanes()
    return jnp.concatenate([jnp.where(first, x, none), jnp.where(first, none, x)], axis=0)


def forward(chunk, place, proj, att, share, share_bf, ds):
    tk, tq = iota((BAND, BAND), 0), iota((BAND, BAND), 1)

    def side(t):
        c = t & 15
        return ((c >= 4) & (c < 12)).astype(jnp.int32)

    same = side(tk) == side(tq)
    whole = (tk >> 6) == (tq >> 6)
    zero = jnp.zeros((BAND, BAND), F32)
    plain = jnp.where(same, zero, -1e30)
    first = jnp.where(whole | (place[0] != 0), plain, -1e30)
    units = []
    for p in range(CW // 128):
        for b in range(BANDS):
            here, at = slice(b * BAND, (b + 1) * BAND), chunk * CW + p * 128
            loads = [functools.partial(lambda c, h: proj[h, c : c + 128], i * HW + at, here) for i in range(3)]
            units.append((b, here, p * 128, *loads))
    for u, (b, here, at, q, k, v) in enumerate(units):
        share[u] = dot(split(k()), q(), 1, 1).reshape(2, BAND, BAND) * 0.125 + (first if b == 0 else plain)
    for u in range(len(units)):
        s = share[u]
        e = jnp.exp(s - jnp.max(s, axis=1, keepdims=True))
        e = e * (1.0 / jnp.sum(e, axis=1, keepdims=True))
        share[u] = e
        share_bf[u] = e.astype(BF16).reshape(2 * BAND, BAND)
    for u, (b, here, at, q, k, v) in enumerate(units):
        att[here, at : at + 128] = dot(share_bf[u], split(v()), 0, 0).astype(BF16)
    return units


def backward(units, place, normed, cot, ow, att, gp, keep, send, share, share_bf, ds):
    grad = dot(cot[...], ow[...], 1, 0).astype(BF16)
    lane = first_lanes()

    def pick(x):
        return jnp.where(lane, x[:BAND], x[BAND:])

    for u, (b, here, at, q, k, v) in enumerate(units):
        gs = dot(split(v()), grad[here, at : at + 128], 1, 1).reshape(2, BAND, BAND)
        e = share[u]
        delta = jnp.sum(e * gs, axis=1, keepdims=True)
        ds[u] = (e * (gs - delta) * 0.125).astype(BF16).reshape(2 * BAND, BAND)
    for u, (b, here, at, q, k, v) in enumerate(units):
        d = ds[u]
        gp[here, at : at + 128] = dot(d, split(k()), 0, 0).astype(BF16)
        gp[here, CW + at : CW + at + 128] = pick(dot(d, q(), 1, 0)).astype(BF16)
        gp[here, 2 * CW + at : 2 * CW + at + 128] = pick(
            dot(share_bf[u], grad[here, at : at + 128], 1, 0)
        ).astype(BF16)
    core = place[1]
    for half in range(2):
        for out, flip in ((send, 1), (keep, 0)):
            cut = pl.ds(pl.multiple_of(half * 512 + (core ^ flip) * 256, 256), 256)
            out[half, :, 0 : 3 * CW] = dot(normed[:, cut], gp[...], 0, 0).astype(out.dtype)
            out[half, :, 3 * CW :] = dot(cot[:, cut], att[...], 0, 0).astype(out.dtype)


def finish_kernel(emb, cot, wq, ow, *refs):
    atts, gps = refs[:CHUNKS], refs[CHUNKS : 2 * CHUNKS]
    mid, up, left, diag, tick, weight, last, big, sems = refs[2 * CHUNKS :]
    copies = [
        pltpu.make_async_copy(ow, last, sems.at[0]),
        pltpu.make_async_copy(wq, weight, sems.at[1]),
    ]
    for copy in copies:
        copy.start()
    copies[0].wait()

    def put(i, block, values):
        if block == 0:
            up[i] = values[:64]
            mid[i, 0:64] = values[64:]
        else:
            at = block * BAND - 64
            mid[i, at : at + BAND] = values

    def each(i, update):
        for block in range(BANDS):
            here = slice(block * BAND, (block + 1) * BAND)
            put(i, block, update(here, emb[here].astype(F32), big[here]).astype(BF16))

    def gradient(here, x, gst):
        centred, inverse = moments(x)
        standard = centred * inverse
        m1 = jnp.mean(gst, axis=1, keepdims=True)
        m2 = jnp.mean(gst * standard, axis=1, keepdims=True)
        return cot[here].astype(F32) + inverse * (gst - m1 - standard * m2)

    att = jnp.concatenate([a[...] for a in atts], axis=1)
    big[...] = dot(att, last[...], 1, 1)
    each(0, lambda here, x, branch: x + branch)
    copies[1].wait()
    parts = []
    for i in range(3):
        parts += [g[:, i * CW : (i + 1) * CW] for g in gps]
    big[...] = dot(jnp.concatenate(parts, axis=1), weight[...], 1, 1)
    each(1, gradient)
    pick, corner = late_cells(OWN, MSG, True), late_cells(64, 16, True)
    for i in range(2):
        left[i] = dot(pick, mid[i], 1, 0).astype(BF16)
        diag[i] = dot(corner, up[i], 1, 0).astype(BF16)
    tick[...] = jnp.zeros(tick.shape, F32)


def place_kernel(mid, up, left, diag, out, gin):
    late = (iota((64, 1), 0) & 15) >= LATE
    corner = late_cells(64, 16, False)
    for i, ref in enumerate((out, gin)):
        ref[OWN:] = jnp.where(late, dot(corner, diag[i], 1, 0), up[i].astype(F32)).astype(BF16)
        for at in range(0, OWN, 64):
            m, t = iota((64, MSG), 1), at + iota((64, MSG), 0)
            spread = hot(t == (m >> 2) * COLS + LATE + (m & 3))
            values = dot(spread, left[i], 1, 0)
            ref[at : at + 64] = jnp.where(late, values, mid[i, at : at + 64].astype(F32)).astype(BF16)


W = 4 * CW
Q = W // 4


def parity_core(place, a, b, keep, send):
    g = place[2] ^ place[3]
    for u in range(2):
        for out, v in ((keep, u ^ g), (send, u ^ g ^ 1)):
            out[u] = (a[u, :, v] + b[u, :, v].astype(F32)).astype(out.dtype)


def parity_pair(place, a, b, tick, halo, keep, send, passed):
    passed[...] = halo[...]
    for out, u in ((keep, place[2]), (send, place[2] ^ 1)):
        out[...] = (a[u] + b[u].astype(F32)).astype(out.dtype)


def high_core(place, a, b, keep, send):
    for out, u in ((keep, place[2]), (send, place[2] ^ 1)):
        for v in range(2):
            out[v] = (a[u, :, v] + b[u, :, v].astype(F32)).astype(out.dtype)


def high_pair(place, a, b, keep, send):
    for out, v in ((keep, place[3]), (send, place[3] ^ 1)):
        out[...] = (a[v] + b[v].astype(F32)).astype(out.dtype)


def parity_cut(place, a, b, keep, send):
    g = place[4] ^ place[5]
    for u in range(2):
        for out, v in ((keep, u ^ g), (send, u ^ g ^ 1)):
            cut = pl.ds(pl.multiple_of((2 * u + v) * Q, Q), Q)
            out[:, :, u * Q : (u + 1) * Q] = (a[:, :, cut] + b[:, :, cut].astype(F32)).astype(out.dtype)


def high_cut(place, a, b, tick, keep, send):
    for out, u in ((keep, place[4]), (send, place[4] ^ 1)):
        cut = pl.ds(pl.multiple_of(u * 2 * Q, Q), 2 * Q)
        for v in range(2):
            out[v] = (a[v, :, :, cut] + b[v, :, :, cut].astype(F32)).astype(out.dtype)


def join_kernel(a, b, c, d, arrived, out):
    out[:, :, 0 : 2 * Q] = (a[...] + b[...].astype(F32)).astype(BF16)
    out[:, :, 2 * Q :] = (c[...] + d[...].astype(F32)).astype(BF16)


def depth_kernel(ref, out):
    out[...] = sum(ref[i].astype(F32) for i in range(8)).astype(BF16)


def level_kernel(factor, place, r0, r1, r2, r3, qkv, outw):
    yh, yl = place[4], place[5]

    def add(a, b, at):
        return (a[:, at : at + Q].astype(F32) + b[:, at : at + Q].astype(F32)) * factor

    for a, b, g in ((r0, r3, yh ^ yl), (r1, r2, yh ^ yl ^ 1)):
        qkv[:, pl.ds(pl.multiple_of(g * HW, HW), CW)] = add(a, b, 0)
        second = add(a, b, Q)

        @pl.when(g == 1)
        def _():
            qkv[:, 2 * HW : 2 * HW + CW] = second

        @pl.when(g == 0)
        def _():
            outw[:, 0:CW] = second

    for a, b, high in ((r0, r1, yh), (r2, r3, yh ^ 1)):
        first, second = add(a, b, 2 * Q), add(a, b, 3 * Q)

        @pl.when(high == 0)
        def _():
            qkv[:, CW : 2 * CW] = first
            qkv[:, HW + CW : HW + 2 * CW] = second

        @pl.when(high == 1)
        def _():
            qkv[:, 2 * HW + CW : 2 * HW + 2 * CW] = first
            outw[:, CW : 2 * CW] = second


def permute(x, where):
    pairs = []
    for la in range(NLAT):
        for lo in range(NLON):
            tl, to = where(la, lo)
            pairs.append((la * NLON + lo, tl * NLON + to))
    return lax.ppermute(x, GRID, pairs)


def shift(x, down, right):
    return permute(x, lambda la, lo: ((la + down) % NLAT, (lo + right) % NLON))


def swap(x, axis, flip):
    return lax.ppermute(x, axis, [(i, i ^ flip) for i in range(lax.axis_size(axis))])


def swap_x(x, flip):
    return permute(x, lambda la, lo: (la ^ (flip & 2), lo ^ (flip & 1)))


def halve(name, kernel, shape, operands, specs, more=()):
    return call(
        kernel,
        [sds(shape, F32), sds(shape), *more],
        operands,
        specs,
        2**10,
        2**10,
        limit=16,
        name=name,
    )


def sum_core(place, keep, send, c):
    fold = (2, 8, 2, 16, W)
    kernel = high_core if c % 2 else parity_core
    recv = swap(send, "core", 1)
    operands = (place, keep.reshape(fold), recv.reshape(fold))
    return halve("sum_core", kernel, (2, 8, 16, W), operands, [smem(), vmem(), vmem()])


def sum_first(place, keep, send, tick, halo):
    adds = [smem(), vmem(), vmem()]
    operands = (place, keep, swap_x(send, 1), tick, halo)
    specs = adds + [anywhere(), vmem()]
    keep, send, halo = halve("sum_pair", parity_pair, (8, 16, W), operands, specs, [sds(halo.shape)])
    operands = (place, keep, swap_x(send, 3))
    keep, send = halve("sum_cut", parity_cut, (8, 16, 2 * Q), operands, adds)
    return [keep, swap(send, "batch", 1)], halo


def sum_second(place, keep, send, tick):
    adds = [smem(), vmem(), vmem()]
    operands = (place, keep, swap_x(send, 3), tick)
    keep, send = halve("sum_cut", high_cut, (2, 8, 16, 2 * Q), operands, adds + [anywhere()])
    operands = (place, keep, swap(send, "batch", 3))
    keep, send = halve("sum_pair", high_pair, (8, 16, 2 * Q), operands, adds)
    return [keep, swap_x(send, 1)]


def shards(
    bottom_codes, mask_flags, top_codes, bottom_table, top_table, mask_vector, qkv_weight, out_weight, cotangent
):
    core, xh, xl = lax.axis_index("core"), lax.axis_index("xh"), lax.axis_index("xl")
    y = lax.axis_index("batch")
    place = jnp.stack([2 * xh + core, core, xh, xl, y >> 1, y & 1]).astype(jnp.int32)
    own = jnp.concatenate(
        [bottom_codes[0], mask_flags[0], jnp.pad(top_codes[0], ((0, 0), (0, 8)))], axis=0
    )
    near = (own, shift(own, 1, 0), shift(own, 0, 1), shift(own, 1, 1))
    pin = lambda x: pltpu.with_memory_space_constraint(x, pltpu.HBM)
    grads = pin(cotangent.reshape(TOKENS, MODEL))
    bottom_table, top_table = pin(bottom_table), pin(top_table)
    mask_vector, qkv_weight, out_weight = pin(mask_vector), pin(qkv_weight), pin(out_weight)
    up, left, diag = call(
        slice_kernel,
        [sds((64, MODEL)), sds((MSG, MODEL)), sds((16, MODEL))],
        (grads,),
        [hbm()],
        2**28,
        2**21,
        name="slices",
        scratch=[pltpu.VMEM((TOKENS, MODEL), BF16), pltpu.SemaphoreType.DMA],
    )
    up, left, diag = shift(up, 1, 0), shift(left, 0, 1), shift(diag, 1, 1)
    emb, normed, proj = call(
        embed_kernel,
        [sds((TOKENS, MODEL)), sds((TOKENS, MODEL)), sds((TOKENS, 3 * HW))],
        (*near, bottom_table, top_table, mask_vector, qkv_weight),
        [vmem()] * 4 + [hbm()] * 4,
        2 * TOKENS * 1024 * 2560,
        9 * 2**20,
        name="embed",
        scratch=[
            pltpu.VMEM((2, 512, MODEL), BF16),
            pltpu.VMEM((MODEL,), BF16),
            pltpu.VMEM((MODEL, 3 * HW), BF16),
            sems(4),
        ],
    )
    outs = [sds((TOKENS, CW)), sds((TOKENS, 3 * CW)), sds((2, 256, W), F32), sds((2, 256, W))]
    column = pltpu.VMEM((MODEL, CW), BF16)
    units = BANDS * CW // 128
    held = [pltpu.VMEM((units, 2, BAND, BAND), F32)] + [pltpu.VMEM((units, 2 * BAND, BAND), BF16)] * 2
    att, gp, keep, send, cot = call(
        attend_first,
        outs + [sds((TOKENS, MODEL))],
        (place, proj, normed, grads, up, left, diag, out_weight),
        [smem(), vmem(), vmem(), hbm(), vmem(), vmem(), vmem(), hbm()],
        2**20,
        2**12,
        name="attend",
        scratch=[pltpu.VMEM((TOKENS, MODEL), BF16), column, sems(2), *held],
    )
    parts, cores = [(att, gp)], [sum_core(place, keep, send, 0)]
    for c in range(1, CHUNKS):
        after = [cores[c - 2][0]] if c > 1 else []
        att, gp, keep, send = call(
            functools.partial(attend_next, c),
            outs,
            (place, proj, normed, cot, out_weight, *after),
            [smem(), vmem(), vmem(), vmem(), hbm()] + [anywhere()] * len(after),
            2**20,
            2**12,
            name="attend",
            scratch=[column, pltpu.SemaphoreType.DMA, *held],
        )
        parts.append((att, gp))
        cores.append(sum_core(place, keep, send, c))
    *sent, tick = call(
        finish_kernel,
        [sds((2, OWN, MODEL)), sds((2, 64, MODEL)), sds((2, MSG, MODEL)), sds((2, 16, MODEL)), sds((8, 128), F32)],
        (emb, cot, qkv_weight, out_weight, *[p[0] for p in parts], *[p[1] for p in parts]),
        [vmem(), vmem(), hbm(), hbm()] + [vmem()] * 2 * CHUNKS,
        2**20,
        2**12,
        name="finish",
        scratch=[
            pltpu.VMEM((MODEL, 3 * HW), BF16),
            pltpu.VMEM((MODEL, HW), BF16),
            pltpu.VMEM((TOKENS, MODEL), F32),
            sems(2),
        ],
    )
    mid, up, left, diag = sent
    up, diag = shift(up, -1, 0), shift(diag, -1, -1)
    (keep0, send0), (keep1, send1) = cores
    first, left = sum_first(place, keep0, send0, tick, left)
    summed = first + sum_second(place, keep1, send1, diag)
    left = shift(left, 0, -1)
    out, gin = call(
        place_kernel,
        [sds((TOKENS, MODEL))] * 2,
        (mid, up, left, diag),
        [vmem()] * 4,
        2**28,
        5 * 2**20,
        limit=24,
        name="place",
    )
    factor = 1.0 / math.sqrt(TOKENS * NB * NLAT * NLON)
    joined = call(
        join_kernel,
        sds((8, 16, 4 * Q)),
        (*summed, left),
        [vmem()] * 4 + [anywhere()],
        2**19,
        2**21,
        limit=16,
        name="join",
    )
    depth = lax.all_to_all(joined, "z", 0, 0, tiled=True)
    small = dict(flops=2**17, nbytes=2**19, limit=16)
    total = call(depth_kernel, sds((16, 4 * Q)), (depth,), [vmem()], name="depth", **small)
    g_qkv, g_out = call(
        functools.partial(level_kernel, factor),
        [sds((16, 3 * HW), F32), sds((16, HW), F32)],
        (place, total, *[swap(total, "batch", d) for d in (1, 2, 3)]),
        [smem()] + [vmem()] * 4,
        name="level",
        **small,
    )
    shape = (1, ROWS, COLS, MODEL)
    return (out.reshape(shape), gin.reshape(shape), g_qkv, g_out)


def solution(mesh):
    devices = mesh.devices.reshape(NB, 2, 2, 8, 2)
    fine = jax.sharding.Mesh(devices, ("batch",) + GRID)
    rows, cols = ("xh", "core"), ("z", "xl")
    grid, whole = P("batch", rows, cols), P()
    return jax.shard_map(
        shards,
        mesh=fine,
        in_specs=(grid, grid, grid, whole, whole, whole, whole, whole, P("batch", rows, cols, None)),
        out_specs=(
            P("batch", rows, cols, None),
            P("batch", rows, cols, None),
            P(GRID, None),
            P(GRID, None),
        ),
        check_vma=False,
    )
```

```python
import functools
import math

import jax
import jax.numpy as jnp
from jax import lax
from jax.experimental import pallas as pl
from jax.experimental.pallas import tpu as pltpu
from jax.sharding import PartitionSpec as P

HEADS = 8
HDIM = 64
WIN = 8
HW = 512
SHIFT = 4
EPS = 1e-05
MODEL = 1024
ROWS, COLS = 32, 16
TOKENS = ROWS * COLS
BAND = WIN * COLS
BANDS = TOKENS // BAND
CHUNKS = 2
CW = HW // CHUNKS
F32 = jnp.float32
BF16 = jnp.bfloat16
GRID = ("xh", "core", "z", "xl")
NB, NLAT, NLON = 4, 4, 16


def dot(a, b, ca, cb):
    return lax.dot_general(a, b, (((ca,), (cb,)), ((), ())), preferred_element_type=F32)


def vmem():
    return pl.BlockSpec(memory_space=pltpu.VMEM)


def smem():
    return pl.BlockSpec(memory_space=pltpu.SMEM)


def call(kernel, outs, operands, specs, flops, nbytes, trans=0, limit=40, name=None, scratch=()):
    return pl.pallas_call(
        kernel,
        out_shape=outs,
        in_specs=specs,
        out_specs=jax.tree.map(lambda _: vmem(), outs),
        scratch_shapes=scratch,
        compiler_params=pltpu.CompilerParams(vmem_limit_bytes=limit * 2**20),
        cost_estimate=pl.CostEstimate(flops=flops, bytes_accessed=nbytes, transcendentals=trans),
        name=name,
    )(*operands)


def hbm():
    return pl.BlockSpec(memory_space=pltpu.HBM)


def anywhere():
    return pl.BlockSpec(memory_space=pl.ANY)


def sems(n):
    return pltpu.SemaphoreType.DMA((n,))


def sds(shape, dtype=BF16):
    return jax.ShapeDtypeStruct(shape, dtype)


def iota(shape, dim):
    return lax.broadcasted_iota(jnp.int32, shape, dim)


def moments(x):
    mean = jnp.mean(x, axis=1, keepdims=True)
    centred = x - mean
    inverse = lax.rsqrt(jnp.mean(centred * centred, axis=1, keepdims=True) + EPS)
    return centred, inverse


MSG = SHIFT * (ROWS - SHIFT)
OWN = (ROWS - SHIFT) * COLS
LATE = COLS - SHIFT


def hot(mask):
    return mask.astype(F32).astype(BF16)


def late_cells(cells, rows, by_row):
    dims = (0, 1) if by_row else (1, 0)
    shape = (rows, cells) if by_row else (cells, rows)
    m, t = iota(shape, dims[0]), iota(shape, dims[1])
    return hot(t == (m >> 2) * COLS + LATE + (m & 3))


def slice_kernel(cot, up, left, diag, held, sem):
    copy = pltpu.make_async_copy(cot, held, sem)
    copy.start()
    pick, corner = late_cells(OWN, MSG, True), late_cells(64, 16, True)
    copy.wait()
    up[...] = held[OWN:]
    left[...] = dot(pick, held[:OWN], 1, 0).astype(BF16)
    diag[...] = dot(corner, held[OWN:], 1, 0).astype(BF16)


def embed_kernel(
    place, own, up, left, diag, bt, tt, mv, wq, emb, normed, proj, att, share, share_bf, tables, masked, weight, sems
):
    copies = [
        pltpu.make_async_copy(bt, tables.at[0], sems.at[0]),
        pltpu.make_async_copy(tt, tables.at[1], sems.at[1]),
        pltpu.make_async_copy(mv, masked, sems.at[2]),
        pltpu.make_async_copy(wq, weight, sems.at[3]),
    ]
    for copy in copies[:3]:
        copy.start()
    r, j = iota((80, 16), 0), iota((80, 16), 1)
    low = jnp.where(r >= 64, r - 50, r & 31) >= 28
    late = jnp.where(r >= 64, 2 * j, j) >= LATE
    grid = jnp.where(
        low,
        jnp.where(late, diag[...], up[...]),
        jnp.where(late, left[...], own[...]),
    )
    bottom = jnp.where(grid[32:64] == 1, 512, grid[0:32])
    upper = grid[64:80, 0:8]

    def column(codes, rows, row_of, lane_of):
        width = codes.shape[1]
        parts = jnp.concatenate([codes >> 4, codes & 15], axis=1).astype(F32).astype(BF16)
        pick = hot(row_of(iota((TOKENS, rows), 0)) == iota((TOKENS, rows), 1))
        spread = dot(pick, parts, 1, 0)
        t, lane = iota(spread.shape, 0), iota(spread.shape, 1)
        inside = jnp.where(lane < width, lane, lane - width) == lane_of(t)
        weight = jnp.where(lane < width, 16.0, 1.0)
        code = jnp.sum(jnp.where(inside, spread * weight, 0.0), axis=1, keepdims=True)
        return code.astype(jnp.int32)

    def source_row(t):
        return ((t >> 4) + (ROWS - SHIFT)) & (ROWS - 1)

    code_b = column(bottom, 32, source_row, lambda t: t & 15)
    code_t = column(upper, 16, lambda t: source_row(t) >> 1, lambda t: (t & 15) >> 1)
    for copy in copies[:3]:
        copy.wait()
    copies[3].start()
    step = 256
    for at in range(0, TOKENS, step):
        here = slice(at, at + step)
        cb, ct = code_b[here], code_t[here]
        lane = iota((step, 512), 1)
        x = dot(hot(lane == cb), tables[0], 1, 0)
        x = jnp.where(cb == 512, masked[...].astype(F32).reshape(1, MODEL), x)
        x = (x + dot(hot(lane == ct), tables[1], 1, 0)).astype(BF16)
        emb[here] = x
        centred, inverse = moments(x.astype(F32))
        normed[here] = (centred * inverse).astype(BF16)
    copies[3].wait()
    proj[...] = dot(normed[...], weight[...], 1, 0).astype(BF16)
    forward(0, place, proj, att, share, share_bf)


def merge(cot, grads, up, left, diag):
    p = iota((64, 1), 0) & 15
    corner = dot(late_cells(64, 16, False), diag[...], 1, 0)
    cot[0:64] = jnp.where(p >= LATE, corner, up[...].astype(F32)).astype(BF16)
    for at in range(0, OWN, 64):
        m, t = iota((64, MSG), 1), at + iota((64, MSG), 0)
        spread = hot(t == (m >> 2) * COLS + LATE + (m & 3))
        values = dot(spread, left[...], 1, 0)
        values = jnp.where(p >= LATE, values, grads[at : at + 64].astype(F32))
        cot[64 + at : 128 + at] = values.astype(BF16)


def attend_first(
    place, proj, normed, grads, up, left, diag, ow, att, share, share_bf, gp, keep, send, cot, own, weight, sems, ds
):
    copies = [
        pltpu.make_async_copy(grads, own, sems.at[0]),
        pltpu.make_async_copy(ow.at[:, 0:CW], weight, sems.at[1]),
    ]
    for copy in copies:
        copy.start()
    copies[0].wait()
    merge(cot, own, up, left, diag)
    copies[1].wait()
    backward(0, place, proj, normed, cot, weight, att, gp, keep, send, share, share_bf, ds)


def attend_next(chunk, place, proj, normed, cot, ow, *refs):
    att, gp, keep, send, weight, sem, *held = refs[1:] if chunk > 1 else refs
    copy = pltpu.make_async_copy(ow.at[:, chunk * CW : (chunk + 1) * CW], weight, sem)
    copy.start()
    forward(chunk, place, proj, att, *held[:2])
    copy.wait()
    backward(chunk, place, proj, normed, cot, weight, att, gp, keep, send, *held)


def first_lanes():
    return iota((BAND, 128), 1) < 64


def split(x):
    none = jnp.zeros_like(x)
    first = first_lanes()
    return jnp.concatenate([jnp.where(first, x, none), jnp.where(first, none, x)], axis=0)


def units_of(chunk, proj):
    units = []
    for p in range(CW // 128):
        for b in range(BANDS):
            here, at = slice(b * BAND, (b + 1) * BAND), chunk * CW + p * 128
            loads = [functools.partial(lambda c, h: proj[h, c : c + 128], i * HW + at, here) for i in range(3)]
            units.append((b, here, p * 128, *loads))
    return units


def forward(chunk, place, proj, att, share, share_bf):
    tk, tq = iota((BAND, BAND), 0), iota((BAND, BAND), 1)

    def side(t):
        c = t & 15
        return ((c >= 4) & (c < 12)).astype(jnp.int32)

    same = side(tk) == side(tq)
    whole = (tk >> 6) == (tq >> 6)
    zero = jnp.zeros((BAND, BAND), F32)
    plain = jnp.where(same, zero, -1e30)
    first = jnp.where(whole | (place[0] != 0), plain, -1e30)
    units = units_of(chunk, proj)
    for u, (b, here, at, q, k, v) in enumerate(units):
        share[u] = dot(split(k()), q(), 1, 1).reshape(2, BAND, BAND) * 0.125 + (first if b == 0 else plain)
    for u in range(len(units)):
        s = share[u]
        e = jnp.exp(s - jnp.max(s, axis=1, keepdims=True))
        e = e * (1.0 / jnp.sum(e, axis=1, keepdims=True))
        share[u] = e
        share_bf[u] = e.astype(BF16).reshape(2 * BAND, BAND)
    for u, (b, here, at, q, k, v) in enumerate(units):
        att[here, at : at + 128] = dot(share_bf[u], split(v()), 0, 0).astype(BF16)


def backward(chunk, place, proj, normed, cot, ow, att, gp, keep, send, share, share_bf, ds):
    units = units_of(chunk, proj)
    grad = dot(cot[...], ow[...], 1, 0).astype(BF16)
    lane = first_lanes()

    def pick(x):
        return jnp.where(lane, x[:BAND], x[BAND:])

    for u, (b, here, at, q, k, v) in enumerate(units):
        gs = dot(split(v()), grad[here, at : at + 128], 1, 1).reshape(2, BAND, BAND)
        e = share[u]
        delta = jnp.sum(e * gs, axis=1, keepdims=True)
        ds[u] = (e * (gs - delta) * 0.125).astype(BF16).reshape(2 * BAND, BAND)
    for u, (b, here, at, q, k, v) in enumerate(units):
        d = ds[u]
        gp[here, at : at + 128] = dot(d, split(k()), 0, 0).astype(BF16)
        gp[here, CW + at : CW + at + 128] = pick(dot(d, q(), 1, 0)).astype(BF16)
        gp[here, 2 * CW + at : 2 * CW + at + 128] = pick(
            dot(share_bf[u], grad[here, at : at + 128], 1, 0)
        ).astype(BF16)
    core = place[1]
    for half in range(2):
        for out, flip in ((send, 1), (keep, 0)):
            cut = pl.ds(pl.multiple_of(half * 512 + (core ^ flip) * 256, 256), 256)
            out[half, :, 0 : 3 * CW] = dot(normed[:, cut], gp[...], 0, 0).astype(out.dtype)
            out[half, :, 3 * CW :] = dot(cot[:, cut], att[...], 0, 0).astype(out.dtype)


def finish_kernel(emb, cot, wq, ow, *refs):
    atts, gps = refs[:CHUNKS], refs[CHUNKS : 2 * CHUNKS]
    mid, up, left, diag, tick, weight, last, big, sems = refs[2 * CHUNKS :]
    copies = [
        pltpu.make_async_copy(ow, last, sems.at[0]),
        pltpu.make_async_copy(wq, weight, sems.at[1]),
    ]
    for copy in copies:
        copy.start()
    copies[0].wait()

    def put(i, block, values):
        if block == 0:
            up[i] = values[:64]
            mid[i, 0:64] = values[64:]
        else:
            at = block * BAND - 64
            mid[i, at : at + BAND] = values

    def each(i, update):
        for block in range(BANDS):
            here = slice(block * BAND, (block + 1) * BAND)
            put(i, block, update(here, emb[here].astype(F32), big[here]).astype(BF16))

    def gradient(here, x, gst):
        centred, inverse = moments(x)
        standard = centred * inverse
        m1 = jnp.mean(gst, axis=1, keepdims=True)
        m2 = jnp.mean(gst * standard, axis=1, keepdims=True)
        return cot[here].astype(F32) + inverse * (gst - m1 - standard * m2)

    att = jnp.concatenate([a[...] for a in atts], axis=1)
    big[...] = dot(att, last[...], 1, 1)
    each(0, lambda here, x, branch: x + branch)
    copies[1].wait()
    parts = []
    for i in range(3):
        parts += [g[:, i * CW : (i + 1) * CW] for g in gps]
    big[...] = dot(jnp.concatenate(parts, axis=1), weight[...], 1, 1)
    each(1, gradient)
    pick, corner = late_cells(OWN, MSG, True), late_cells(64, 16, True)
    for i in range(2):
        left[i] = dot(pick, mid[i], 1, 0).astype(BF16)
        diag[i] = dot(corner, up[i], 1, 0).astype(BF16)
    tick[...] = jnp.zeros(tick.shape, F32)


def place_kernel(mid, up, left, diag, out, gin):
    late = (iota((64, 1), 0) & 15) >= LATE
    corner = late_cells(64, 16, False)
    for i, ref in enumerate((out, gin)):
        ref[OWN:] = jnp.where(late, dot(corner, diag[i], 1, 0), up[i].astype(F32)).astype(BF16)
        for at in range(0, OWN, 64):
            m, t = iota((64, MSG), 1), at + iota((64, MSG), 0)
            spread = hot(t == (m >> 2) * COLS + LATE + (m & 3))
            values = dot(spread, left[i], 1, 0)
            ref[at : at + 64] = jnp.where(late, values, mid[i, at : at + 64].astype(F32)).astype(BF16)


W = 4 * CW
Q = W // 4


def parity_core(place, a, b, keep, send):
    g = place[2] ^ place[3]
    for u in range(2):
        for out, v in ((keep, u ^ g), (send, u ^ g ^ 1)):
            out[u] = (a[u, :, v] + b[u, :, v].astype(F32)).astype(out.dtype)


def parity_pair(place, a, b, tick, halo, keep, send, passed):
    passed[...] = halo[...]
    for out, u in ((keep, place[2]), (send, place[2] ^ 1)):
        out[...] = (a[u] + b[u].astype(F32)).astype(out.dtype)


def high_core(place, a, b, keep, send):
    for out, u in ((keep, place[2]), (send, place[2] ^ 1)):
        for v in range(2):
            out[v] = (a[u, :, v] + b[u, :, v].astype(F32)).astype(out.dtype)


def high_pair(place, a, b, keep, send):
    for out, v in ((keep, place[3]), (send, place[3] ^ 1)):
        out[...] = (a[v] + b[v].astype(F32)).astype(out.dtype)


def parity_cut(place, a, b, keep, send):
    g = place[4] ^ place[5]
    for u in range(2):
        for out, v in ((keep, u ^ g), (send, u ^ g ^ 1)):
            cut = pl.ds(pl.multiple_of((2 * u + v) * Q, Q), Q)
            out[:, :, u * Q : (u + 1) * Q] = (a[:, :, cut] + b[:, :, cut].astype(F32)).astype(out.dtype)


def high_cut(place, a, b, tick, keep, send):
    for out, u in ((keep, place[4]), (send, place[4] ^ 1)):
        cut = pl.ds(pl.multiple_of(u * 2 * Q, Q), 2 * Q)
        for v in range(2):
            out[v] = (a[v, :, :, cut] + b[v, :, :, cut].astype(F32)).astype(out.dtype)


def join_kernel(a, b, c, d, arrived, out):
    out[:, :, 0 : 2 * Q] = (a[...] + b[...].astype(F32)).astype(BF16)
    out[:, :, 2 * Q :] = (c[...] + d[...].astype(F32)).astype(BF16)


def depth_kernel(ref, out):
    out[...] = sum(ref[i].astype(F32) for i in range(8)).astype(BF16)


def level_kernel(factor, place, r0, r1, r2, r3, qkv, outw):
    yh, yl = place[4], place[5]

    def add(a, b, at):
        return (a[:, at : at + Q].astype(F32) + b[:, at : at + Q].astype(F32)) * factor

    for a, b, g in ((r0, r3, yh ^ yl), (r1, r2, yh ^ yl ^ 1)):
        qkv[:, pl.ds(pl.multiple_of(g * HW, HW), CW)] = add(a, b, 0)
        second = add(a, b, Q)

        @pl.when(g == 1)
        def _():
            qkv[:, 2 * HW : 2 * HW + CW] = second

        @pl.when(g == 0)
        def _():
            outw[:, 0:CW] = second

    for a, b, high in ((r0, r1, yh), (r2, r3, yh ^ 1)):
        first, second = add(a, b, 2 * Q), add(a, b, 3 * Q)

        @pl.when(high == 0)
        def _():
            qkv[:, CW : 2 * CW] = first
            qkv[:, HW + CW : HW + 2 * CW] = second

        @pl.when(high == 1)
        def _():
            qkv[:, 2 * HW + CW : 2 * HW + 2 * CW] = first
            outw[:, CW : 2 * CW] = second


def permute(x, where):
    pairs = []
    for la in range(NLAT):
        for lo in range(NLON):
            tl, to = where(la, lo)
            pairs.append((la * NLON + lo, tl * NLON + to))
    return lax.ppermute(x, GRID, pairs)


def shift(x, down, right):
    return permute(x, lambda la, lo: ((la + down) % NLAT, (lo + right) % NLON))


def swap(x, axis, flip):
    return lax.ppermute(x, axis, [(i, i ^ flip) for i in range(lax.axis_size(axis))])


def swap_x(x, flip):
    return permute(x, lambda la, lo: (la ^ (flip & 2), lo ^ (flip & 1)))


def halve(name, kernel, shape, operands, specs, more=()):
    return call(
        kernel,
        [sds(shape, F32), sds(shape), *more],
        operands,
        specs,
        2**10,
        2**10,
        limit=16,
        name=name,
    )


def sum_core(place, keep, send, c):
    fold = (2, 8, 2, 16, W)
    kernel = high_core if c % 2 else parity_core
    recv = swap(send, "core", 1)
    operands = (place, keep.reshape(fold), recv.reshape(fold))
    return halve("sum_core", kernel, (2, 8, 16, W), operands, [smem(), vmem(), vmem()])


def sum_first(place, keep, send, tick, halo):
    adds = [smem(), vmem(), vmem()]
    operands = (place, keep, swap_x(send, 1), tick, halo)
    specs = adds + [anywhere(), vmem()]
    keep, send, halo = halve("sum_pair", parity_pair, (8, 16, W), operands, specs, [sds(halo.shape)])
    operands = (place, keep, swap_x(send, 3))
    keep, send = halve("sum_cut", parity_cut, (8, 16, 2 * Q), operands, adds)
    return [keep, swap(send, "batch", 1)], halo


def sum_second(place, keep, send, tick):
    adds = [smem(), vmem(), vmem()]
    operands = (place, keep, swap_x(send, 3), tick)
    keep, send = halve("sum_cut", high_cut, (2, 8, 16, 2 * Q), operands, adds + [anywhere()])
    operands = (place, keep, swap(send, "batch", 3))
    keep, send = halve("sum_pair", high_pair, (8, 16, 2 * Q), operands, adds)
    return [keep, swap_x(send, 1)]


def shards(
    bottom_codes, mask_flags, top_codes, bottom_table, top_table, mask_vector, qkv_weight, out_weight, cotangent
):
    core, xh, xl = lax.axis_index("core"), lax.axis_index("xh"), lax.axis_index("xl")
    y = lax.axis_index("batch")
    place = jnp.stack([2 * xh + core, core, xh, xl, y >> 1, y & 1]).astype(jnp.int32)
    own = jnp.concatenate(
        [bottom_codes[0], mask_flags[0], jnp.pad(top_codes[0], ((0, 0), (0, 8)))], axis=0
    )
    near = (own, shift(own, 1, 0), shift(own, 0, 1), shift(own, 1, 1))
    pin = lambda x: pltpu.with_memory_space_constraint(x, pltpu.HBM)
    grads = pin(cotangent.reshape(TOKENS, MODEL))
    bottom_table, top_table = pin(bottom_table), pin(top_table)
    mask_vector, qkv_weight, out_weight = pin(mask_vector), pin(qkv_weight), pin(out_weight)
    up, left, diag = call(
        slice_kernel,
        [sds((64, MODEL)), sds((MSG, MODEL)), sds((16, MODEL))],
        (grads,),
        [hbm()],
        2**28,
        2**21,
        name="slices",
        scratch=[pltpu.VMEM((TOKENS, MODEL), BF16), pltpu.SemaphoreType.DMA],
    )
    up, left, diag = shift(up, 1, 0), shift(left, 0, 1), shift(diag, 1, 1)
    units = BANDS * CW // 128
    score, pairs = (units, 2, BAND, BAND), (units, 2 * BAND, BAND)
    emb, normed, proj, att, share, share_bf = call(
        embed_kernel,
        [sds((TOKENS, MODEL)), sds((TOKENS, MODEL)), sds((TOKENS, 3 * HW)), sds((TOKENS, CW)), sds(score, F32), sds(pairs)],
        (place, *near, bottom_table, top_table, mask_vector, qkv_weight),
        [smem()] + [vmem()] * 4 + [hbm()] * 4,
        2 * TOKENS * 1024 * 2560,
        9 * 2**20,
        name="embed",
        scratch=[
            pltpu.VMEM((2, 512, MODEL), BF16),
            pltpu.VMEM((MODEL,), BF16),
            pltpu.VMEM((MODEL, 3 * HW), BF16),
            sems(4),
        ],
    )
    outs = [sds((TOKENS, 3 * CW)), sds((2, 256, W), F32), sds((2, 256, W))]
    column, ds = pltpu.VMEM((MODEL, CW), BF16), pltpu.VMEM(pairs, BF16)
    held = [pltpu.VMEM(score, F32), pltpu.VMEM(pairs, BF16), ds]
    gp, keep, send, cot = call(
        attend_first,
        outs + [sds((TOKENS, MODEL))],
        (place, proj, normed, grads, up, left, diag, out_weight, att, share, share_bf),
        [smem(), vmem(), vmem(), hbm(), vmem(), vmem(), vmem(), hbm(), vmem(), vmem(), vmem()],
        2**20,
        2**12,
        name="attend",
        scratch=[pltpu.VMEM((TOKENS, MODEL), BF16), column, sems(2), ds],
    )
    parts, cores = [(att, gp)], [sum_core(place, keep, send, 0)]
    for c in range(1, CHUNKS):
        after = [cores[c - 2][0]] if c > 1 else []
        att, gp, keep, send = call(
            functools.partial(attend_next, c),
            [sds((TOKENS, CW))] + outs,
            (place, proj, normed, cot, out_weight, *after),
            [smem(), vmem(), vmem(), vmem(), hbm()] + [anywhere()] * len(after),
            2**20,
            2**12,
            name="attend",
            scratch=[column, pltpu.SemaphoreType.DMA, *held],
        )
        parts.append((att, gp))
        cores.append(sum_core(place, keep, send, c))
    *sent, tick = call(
        finish_kernel,
        [sds((2, OWN, MODEL)), sds((2, 64, MODEL)), sds((2, MSG, MODEL)), sds((2, 16, MODEL)), sds((8, 128), F32)],
        (emb, cot, qkv_weight, out_weight, *[p[0] for p in parts], *[p[1] for p in parts]),
        [vmem(), vmem(), hbm(), hbm()] + [vmem()] * 2 * CHUNKS,
        2**20,
        2**12,
        name="finish",
        scratch=[
            pltpu.VMEM((MODEL, 3 * HW), BF16),
            pltpu.VMEM((MODEL, HW), BF16),
            pltpu.VMEM((TOKENS, MODEL), F32),
            sems(2),
        ],
    )
    mid, up, left, diag = sent
    up, diag = shift(up, -1, 0), shift(diag, -1, -1)
    (keep0, send0), (keep1, send1) = cores
    first, left = sum_first(place, keep0, send0, tick, left)
    summed = first + sum_second(place, keep1, send1, diag)
    left = shift(left, 0, -1)
    out, gin = call(
        place_kernel,
        [sds((TOKENS, MODEL))] * 2,
        (mid, up, left, diag),
        [vmem()] * 4,
        2**28,
        5 * 2**20,
        limit=24,
        name="place",
    )
    factor = 1.0 / math.sqrt(TOKENS * NB * NLAT * NLON)
    joined = call(
        join_kernel,
        sds((8, 16, 4 * Q)),
        (*summed, left),
        [vmem()] * 4 + [anywhere()],
        2**19,
        2**21,
        limit=16,
        name="join",
    )
    depth = lax.all_to_all(joined, "z", 0, 0, tiled=True)
    small = dict(flops=2**17, nbytes=2**19, limit=16)
    total = call(depth_kernel, sds((16, 4 * Q)), (depth,), [vmem()], name="depth", **small)
    g_qkv, g_out = call(
        functools.partial(level_kernel, factor),
        [sds((16, 3 * HW), F32), sds((16, HW), F32)],
        (place, total, *[swap(total, "batch", d) for d in (1, 2, 3)]),
        [smem()] + [vmem()] * 4,
        name="level",
        **small,
    )
    shape = (1, ROWS, COLS, MODEL)
    return (out.reshape(shape), gin.reshape(shape), g_qkv, g_out)


def solution(mesh):
    devices = mesh.devices.reshape(NB, 2, 2, 8, 2)
    fine = jax.sharding.Mesh(devices, ("batch",) + GRID)
    rows, cols = ("xh", "core"), ("z", "xl")
    grid, whole = P("batch", rows, cols), P()
    return jax.shard_map(
        shards,
        mesh=fine,
        in_specs=(grid, grid, grid, whole, whole, whole, whole, whole, P("batch", rows, cols, None)),
        out_specs=(
            P("batch", rows, cols, None),
            P("batch", rows, cols, None),
            P(GRID, None),
            P(GRID, None),
        ),
        check_vma=False,
    )
```

```python
import functools
import math

import jax
import jax.numpy as jnp
from jax import lax
from jax.experimental import pallas as pl
from jax.experimental.pallas import tpu as pltpu
from jax.sharding import PartitionSpec as P

HEADS = 8
HDIM = 64
WIN = 8
HW = 512
SHIFT = 4
EPS = 1e-05
MODEL = 1024
ROWS, COLS = 32, 16
TOKENS = ROWS * COLS
BAND = WIN * COLS
BANDS = TOKENS // BAND
CHUNKS = 2
CW = HW // CHUNKS
F32 = jnp.float32
BF16 = jnp.bfloat16
GRID = ("xh", "core", "z", "xl")
NB, NLAT, NLON = 4, 4, 16


def dot(a, b, ca, cb):
    return lax.dot_general(a, b, (((ca,), (cb,)), ((), ())), preferred_element_type=F32)


def vmem():
    return pl.BlockSpec(memory_space=pltpu.VMEM)


def smem():
    return pl.BlockSpec(memory_space=pltpu.SMEM)


def call(kernel, outs, operands, specs, flops, nbytes, trans=0, limit=40, name=None, scratch=()):
    return pl.pallas_call(
        kernel,
        out_shape=outs,
        in_specs=specs,
        out_specs=jax.tree.map(lambda _: vmem(), outs),
        scratch_shapes=scratch,
        compiler_params=pltpu.CompilerParams(vmem_limit_bytes=limit * 2**20),
        cost_estimate=pl.CostEstimate(flops=flops, bytes_accessed=nbytes, transcendentals=trans),
        name=name,
    )(*operands)


def hbm():
    return pl.BlockSpec(memory_space=pltpu.HBM)


def anywhere():
    return pl.BlockSpec(memory_space=pl.ANY)


def sems(n):
    return pltpu.SemaphoreType.DMA((n,))


def sds(shape, dtype=BF16):
    return jax.ShapeDtypeStruct(shape, dtype)


def iota(shape, dim):
    return lax.broadcasted_iota(jnp.int32, shape, dim)


def moments(x):
    mean = jnp.mean(x, axis=1, keepdims=True)
    centred = x - mean
    inverse = lax.rsqrt(jnp.mean(centred * centred, axis=1, keepdims=True) + EPS)
    return centred, inverse


MSG = SHIFT * (ROWS - SHIFT)
OWN = (ROWS - SHIFT) * COLS
LATE = COLS - SHIFT


def hot(mask):
    return mask.astype(F32).astype(BF16)


def late_cells(cells, rows, by_row):
    dims = (0, 1) if by_row else (1, 0)
    shape = (rows, cells) if by_row else (cells, rows)
    m, t = iota(shape, dims[0]), iota(shape, dims[1])
    return hot(t == (m >> 2) * COLS + LATE + (m & 3))


def slice_kernel(cot, up, left, diag, held, sem):
    copy = pltpu.make_async_copy(cot, held, sem)
    copy.start()
    pick, corner = late_cells(OWN, MSG, True), late_cells(64, 16, True)
    copy.wait()
    up[...] = held[OWN:]
    left[...] = dot(pick, held[:OWN], 1, 0).astype(BF16)
    diag[...] = dot(corner, held[OWN:], 1, 0).astype(BF16)


def embed_kernel(place, own, up, left, diag, bt, tt, mv, wq, ow, *refs):
    emb, normed, proj, att, share, share_bf, last, tables, masked, weight, sems = refs
    copies = [
        pltpu.make_async_copy(bt, tables.at[0], sems.at[0]),
        pltpu.make_async_copy(tt, tables.at[1], sems.at[1]),
        pltpu.make_async_copy(mv, masked, sems.at[2]),
        pltpu.make_async_copy(wq, weight, sems.at[3]),
        pltpu.make_async_copy(ow, last, sems.at[4]),
    ]
    for copy in copies[:3]:
        copy.start()
    r, j = iota((80, 16), 0), iota((80, 16), 1)
    low = jnp.where(r >= 64, r - 50, r & 31) >= 28
    late = jnp.where(r >= 64, 2 * j, j) >= LATE
    grid = jnp.where(
        low,
        jnp.where(late, diag[...], up[...]),
        jnp.where(late, left[...], own[...]),
    )
    bottom = jnp.where(grid[32:64] == 1, 512, grid[0:32])
    upper = grid[64:80, 0:8]

    def column(codes, rows, row_of, lane_of):
        width = codes.shape[1]
        parts = jnp.concatenate([codes >> 4, codes & 15], axis=1).astype(F32).astype(BF16)
        pick = hot(row_of(iota((TOKENS, rows), 0)) == iota((TOKENS, rows), 1))
        spread = dot(pick, parts, 1, 0)
        t, lane = iota(spread.shape, 0), iota(spread.shape, 1)
        inside = jnp.where(lane < width, lane, lane - width) == lane_of(t)
        weight = jnp.where(lane < width, 16.0, 1.0)
        code = jnp.sum(jnp.where(inside, spread * weight, 0.0), axis=1, keepdims=True)
        return code.astype(jnp.int32)

    def source_row(t):
        return ((t >> 4) + (ROWS - SHIFT)) & (ROWS - 1)

    code_b = column(bottom, 32, source_row, lambda t: t & 15)
    code_t = column(upper, 16, lambda t: source_row(t) >> 1, lambda t: (t & 15) >> 1)
    for copy in copies[:3]:
        copy.wait()
    copies[3].start()
    copies[4].start()
    step = 256
    for at in range(0, TOKENS, step):
        here = slice(at, at + step)
        cb, ct = code_b[here], code_t[here]
        lane = iota((step, 512), 1)
        x = dot(hot(lane == cb), tables[0], 1, 0)
        x = jnp.where(cb == 512, masked[...].astype(F32).reshape(1, MODEL), x)
        x = (x + dot(hot(lane == ct), tables[1], 1, 0)).astype(BF16)
        emb[here] = x
        centred, inverse = moments(x.astype(F32))
        normed[here] = (centred * inverse).astype(BF16)
    copies[3].wait()
    proj[...] = dot(normed[...], weight[...], 1, 0).astype(BF16)
    forward(0, place, proj, att, share, share_bf)
    copies[4].wait()


def merge(cot, grads, up, left, diag):
    p = iota((64, 1), 0) & 15
    corner = dot(late_cells(64, 16, False), diag[...], 1, 0)
    cot[0:64] = jnp.where(p >= LATE, corner, up[...].astype(F32)).astype(BF16)
    for at in range(0, OWN, 64):
        m, t = iota((64, MSG), 1), at + iota((64, MSG), 0)
        spread = hot(t == (m >> 2) * COLS + LATE + (m & 3))
        values = dot(spread, left[...], 1, 0)
        values = jnp.where(p >= LATE, values, grads[at : at + 64].astype(F32))
        cot[64 + at : 128 + at] = values.astype(BF16)


def attend_first(place, proj, normed, grads, up, left, diag, ow, att, share, share_bf, gp, keep, send, cot, ds):
    merge(cot, grads, up, left, diag)
    backward(0, place, proj, normed, cot, ow, att, gp, keep, send, share, share_bf, ds)


def attend_next(chunk, place, proj, normed, cot, ow, att, gp, keep, send, *held):
    forward(chunk, place, proj, att, *held[:2])
    backward(chunk, place, proj, normed, cot, ow, att, gp, keep, send, *held)


def first_lanes():
    return iota((BAND, 128), 1) < 64


def split(x):
    none = jnp.zeros_like(x)
    first = first_lanes()
    return jnp.concatenate([jnp.where(first, x, none), jnp.where(first, none, x)], axis=0)


def units_of(chunk, proj):
    units = []
    for p in range(CW // 128):
        for b in range(BANDS):
            here, at = slice(b * BAND, (b + 1) * BAND), chunk * CW + p * 128
            loads = [functools.partial(lambda c, h: proj[h, c : c + 128], i * HW + at, here) for i in range(3)]
            units.append((b, here, p * 128, *loads))
    return units


def forward(chunk, place, proj, att, share, share_bf):
    tk, tq = iota((BAND, BAND), 0), iota((BAND, BAND), 1)

    def side(t):
        c = t & 15
        return ((c >= 4) & (c < 12)).astype(jnp.int32)

    same = side(tk) == side(tq)
    whole = (tk >> 6) == (tq >> 6)
    zero = jnp.zeros((BAND, BAND), F32)
    plain = jnp.where(same, zero, -1e30)
    first = jnp.where(whole | (place[0] != 0), plain, -1e30)
    units = units_of(chunk, proj)
    for u, (b, here, at, q, k, v) in enumerate(units):
        share[u] = dot(split(k()), q(), 1, 1).reshape(2, BAND, BAND) * 0.125 + (first if b == 0 else plain)
    for u in range(len(units)):
        s = share[u]
        e = jnp.exp(s - jnp.max(s, axis=1, keepdims=True))
        e = e * (1.0 / jnp.sum(e, axis=1, keepdims=True))
        share[u] = e
        share_bf[u] = e.astype(BF16).reshape(2 * BAND, BAND)
    for u, (b, here, at, q, k, v) in enumerate(units):
        att[here, at : at + 128] = dot(share_bf[u], split(v()), 0, 0).astype(BF16)


def backward(chunk, place, proj, normed, cot, ow, att, gp, keep, send, share, share_bf, ds):
    units = units_of(chunk, proj)
    grad = dot(cot[...], ow[:, chunk * CW : (chunk + 1) * CW], 1, 0).astype(BF16)
    lane = first_lanes()

    def pick(x):
        return jnp.where(lane, x[:BAND], x[BAND:])

    for u, (b, here, at, q, k, v) in enumerate(units):
        gs = dot(split(v()), grad[here, at : at + 128], 1, 1).reshape(2, BAND, BAND)
        e = share[u]
        delta = jnp.sum(e * gs, axis=1, keepdims=True)
        ds[u] = (e * (gs - delta) * 0.125).astype(BF16).reshape(2 * BAND, BAND)
    for u, (b, here, at, q, k, v) in enumerate(units):
        d = ds[u]
        gp[here, at : at + 128] = dot(d, split(k()), 0, 0).astype(BF16)
        gp[here, CW + at : CW + at + 128] = pick(dot(d, q(), 1, 0)).astype(BF16)
        gp[here, 2 * CW + at : 2 * CW + at + 128] = pick(
            dot(share_bf[u], grad[here, at : at + 128], 1, 0)
        ).astype(BF16)
    core = place[1]
    for half in range(2):
        for out, flip in ((send, 1), (keep, 0)):
            cut = pl.ds(pl.multiple_of(half * 512 + (core ^ flip) * 256, 256), 256)
            out[half, :, 0 : 3 * CW] = dot(normed[:, cut], gp[...], 0, 0).astype(out.dtype)
            out[half, :, 3 * CW :] = dot(cot[:, cut], att[...], 0, 0).astype(out.dtype)


def finish_kernel(emb, cot, wq, last, *refs):
    atts, gps = refs[:CHUNKS], refs[CHUNKS : 2 * CHUNKS]
    mid, up, left, diag, tick, weight, big, sem = refs[2 * CHUNKS :]
    copy = pltpu.make_async_copy(wq, weight, sem)
    copy.start()

    def put(i, block, values):
        if block == 0:
            up[i] = values[:64]
            mid[i, 0:64] = values[64:]
        else:
            at = block * BAND - 64
            mid[i, at : at + BAND] = values

    def each(i, update):
        for block in range(BANDS):
            here = slice(block * BAND, (block + 1) * BAND)
            put(i, block, update(here, emb[here].astype(F32), big[here]).astype(BF16))

    def gradient(here, x, gst):
        centred, inverse = moments(x)
        standard = centred * inverse
        m1 = jnp.mean(gst, axis=1, keepdims=True)
        m2 = jnp.mean(gst * standard, axis=1, keepdims=True)
        return cot[here].astype(F32) + inverse * (gst - m1 - standard * m2)

    att = jnp.concatenate([a[...] for a in atts], axis=1)
    big[...] = dot(att, last[...], 1, 1)
    each(0, lambda here, x, branch: x + branch)
    copy.wait()
    parts = []
    for i in range(3):
        parts += [g[:, i * CW : (i + 1) * CW] for g in gps]
    big[...] = dot(jnp.concatenate(parts, axis=1), weight[...], 1, 1)
    each(1, gradient)
    pick, corner = late_cells(OWN, MSG, True), late_cells(64, 16, True)
    for i in range(2):
        left[i] = dot(pick, mid[i], 1, 0).astype(BF16)
        diag[i] = dot(corner, up[i], 1, 0).astype(BF16)
    tick[...] = jnp.zeros(tick.shape, F32)


def place_kernel(mid, up, left, diag, out, gin):
    late = (iota((64, 1), 0) & 15) >= LATE
    corner = late_cells(64, 16, False)
    for i, ref in enumerate((out, gin)):
        ref[OWN:] = jnp.where(late, dot(corner, diag[i], 1, 0), up[i].astype(F32)).astype(BF16)
        for at in range(0, OWN, 64):
            m, t = iota((64, MSG), 1), at + iota((64, MSG), 0)
            spread = hot(t == (m >> 2) * COLS + LATE + (m & 3))
            values = dot(spread, left[i], 1, 0)
            ref[at : at + 64] = jnp.where(late, values, mid[i, at : at + 64].astype(F32)).astype(BF16)


W = 4 * CW
Q = W // 4


def parity_core(place, a, b, keep, send):
    g = place[2] ^ place[3]
    for u in range(2):
        for out, v in ((keep, u ^ g), (send, u ^ g ^ 1)):
            out[u] = (a[u, :, v] + b[u, :, v].astype(F32)).astype(out.dtype)


def parity_pair(place, a, b, tick, halo, keep, send, passed):
    passed[...] = halo[...]
    for out, u in ((keep, place[2]), (send, place[2] ^ 1)):
        out[...] = (a[u] + b[u].astype(F32)).astype(out.dtype)


def high_core(place, a, b, keep, send):
    for out, u in ((keep, place[2]), (send, place[2] ^ 1)):
        for v in range(2):
            out[v] = (a[u, :, v] + b[u, :, v].astype(F32)).astype(out.dtype)


def high_pair(place, a, b, keep, send):
    for out, v in ((keep, place[3]), (send, place[3] ^ 1)):
        out[...] = (a[v] + b[v].astype(F32)).astype(out.dtype)


def parity_cut(place, a, b, keep, send):
    g = place[4] ^ place[5]
    for u in range(2):
        for out, v in ((keep, u ^ g), (send, u ^ g ^ 1)):
            cut = pl.ds(pl.multiple_of((2 * u + v) * Q, Q), Q)
            out[:, :, u * Q : (u + 1) * Q] = (a[:, :, cut] + b[:, :, cut].astype(F32)).astype(out.dtype)


def high_cut(place, a, b, tick, keep, send):
    for out, u in ((keep, place[4]), (send, place[4] ^ 1)):
        cut = pl.ds(pl.multiple_of(u * 2 * Q, Q), 2 * Q)
        for v in range(2):
            out[v] = (a[v, :, :, cut] + b[v, :, :, cut].astype(F32)).astype(out.dtype)


def join_kernel(a, b, c, d, arrived, out):
    out[:, :, 0 : 2 * Q] = (a[...] + b[...].astype(F32)).astype(BF16)
    out[:, :, 2 * Q :] = (c[...] + d[...].astype(F32)).astype(BF16)


def depth_kernel(ref, out):
    out[...] = sum(ref[i].astype(F32) for i in range(8)).astype(BF16)


def level_kernel(factor, place, r0, r1, r2, r3, qkv, outw):
    yh, yl = place[4], place[5]

    def add(a, b, at):
        return (a[:, at : at + Q].astype(F32) + b[:, at : at + Q].astype(F32)) * factor

    for a, b, g in ((r0, r3, yh ^ yl), (r1, r2, yh ^ yl ^ 1)):
        qkv[:, pl.ds(pl.multiple_of(g * HW, HW), CW)] = add(a, b, 0)
        second = add(a, b, Q)

        @pl.when(g == 1)
        def _():
            qkv[:, 2 * HW : 2 * HW + CW] = second

        @pl.when(g == 0)
        def _():
            outw[:, 0:CW] = second

    for a, b, high in ((r0, r1, yh), (r2, r3, yh ^ 1)):
        first, second = add(a, b, 2 * Q), add(a, b, 3 * Q)

        @pl.when(high == 0)
        def _():
            qkv[:, CW : 2 * CW] = first
            qkv[:, HW + CW : HW + 2 * CW] = second

        @pl.when(high == 1)
        def _():
            qkv[:, 2 * HW + CW : 2 * HW + 2 * CW] = first
            outw[:, CW : 2 * CW] = second


def permute(x, where):
    pairs = []
    for la in range(NLAT):
        for lo in range(NLON):
            tl, to = where(la, lo)
            pairs.append((la * NLON + lo, tl * NLON + to))
    return lax.ppermute(x, GRID, pairs)


def shift(x, down, right):
    return permute(x, lambda la, lo: ((la + down) % NLAT, (lo + right) % NLON))


def swap(x, axis, flip):
    return lax.ppermute(x, axis, [(i, i ^ flip) for i in range(lax.axis_size(axis))])


def swap_x(x, flip):
    return permute(x, lambda la, lo: (la ^ (flip & 2), lo ^ (flip & 1)))


def halve(name, kernel, shape, operands, specs, more=()):
    return call(
        kernel,
        [sds(shape, F32), sds(shape), *more],
        operands,
        specs,
        2**10,
        2**10,
        limit=16,
        name=name,
    )


def sum_core(place, keep, send, c):
    fold = (2, 8, 2, 16, W)
    kernel = high_core if c % 2 else parity_core
    recv = swap(send, "core", 1)
    operands = (place, keep.reshape(fold), recv.reshape(fold))
    return halve("sum_core", kernel, (2, 8, 16, W), operands, [smem(), vmem(), vmem()])


def sum_first(place, keep, send, tick, halo):
    adds = [smem(), vmem(), vmem()]
    operands = (place, keep, swap_x(send, 1), tick, halo)
    specs = adds + [anywhere(), vmem()]
    keep, send, halo = halve("sum_pair", parity_pair, (8, 16, W), operands, specs, [sds(halo.shape)])
    operands = (place, keep, swap_x(send, 3))
    keep, send = halve("sum_cut", parity_cut, (8, 16, 2 * Q), operands, adds)
    return [keep, swap(send, "batch", 1)], halo


def sum_second(place, keep, send, tick):
    adds = [smem(), vmem(), vmem()]
    operands = (place, keep, swap_x(send, 3), tick)
    keep, send = halve("sum_cut", high_cut, (2, 8, 16, 2 * Q), operands, adds + [anywhere()])
    operands = (place, keep, swap(send, "batch", 3))
    keep, send = halve("sum_pair", high_pair, (8, 16, 2 * Q), operands, adds)
    return [keep, swap_x(send, 1)]


def shards(
    bottom_codes, mask_flags, top_codes, bottom_table, top_table, mask_vector, qkv_weight, out_weight, cotangent
):
    core, xh, xl = lax.axis_index("core"), lax.axis_index("xh"), lax.axis_index("xl")
    y = lax.axis_index("batch")
    place = jnp.stack([2 * xh + core, core, xh, xl, y >> 1, y & 1]).astype(jnp.int32)
    own = jnp.concatenate(
        [bottom_codes[0], mask_flags[0], jnp.pad(top_codes[0], ((0, 0), (0, 8)))], axis=0
    )
    near = (own, shift(own, 1, 0), shift(own, 0, 1), shift(own, 1, 1))
    pin = lambda x: pltpu.with_memory_space_constraint(x, pltpu.HBM)
    grads = pin(cotangent.reshape(TOKENS, MODEL))
    bottom_table, top_table = pin(bottom_table), pin(top_table)
    mask_vector, qkv_weight, out_weight = pin(mask_vector), pin(qkv_weight), pin(out_weight)
    up, left, diag, grads = call(
        slice_kernel,
        [sds((64, MODEL)), sds((MSG, MODEL)), sds((16, MODEL)), sds((TOKENS, MODEL))],
        (grads,),
        [hbm()],
        2**28,
        2**21,
        name="slices",
        scratch=[pltpu.SemaphoreType.DMA],
    )
    up, left, diag = shift(up, 1, 0), shift(left, 0, 1), shift(diag, 1, 1)
    units = BANDS * CW // 128
    score, pairs = (units, 2, BAND, BAND), (units, 2 * BAND, BAND)
    emb, normed, proj, att, share, share_bf, last = call(
        embed_kernel,
        [
            sds((TOKENS, MODEL)),
            sds((TOKENS, MODEL)),
            sds((TOKENS, 3 * HW)),
            sds((TOKENS, CW)),
            sds(score, F32),
            sds(pairs),
            sds((MODEL, HW)),
        ],
        (place, *near, bottom_table, top_table, mask_vector, qkv_weight, out_weight),
        [smem()] + [vmem()] * 4 + [hbm()] * 5,
        2 * TOKENS * 1024 * 2560,
        9 * 2**20,
        name="embed",
        scratch=[
            pltpu.VMEM((2, 512, MODEL), BF16),
            pltpu.VMEM((MODEL,), BF16),
            pltpu.VMEM((MODEL, 3 * HW), BF16),
            sems(5),
        ],
    )
    outs = [sds((TOKENS, 3 * CW)), sds((2, 256, W), F32), sds((2, 256, W))]
    ds = pltpu.VMEM(pairs, BF16)
    held = [pltpu.VMEM(score, F32), pltpu.VMEM(pairs, BF16), ds]
    gp, keep, send, cot = call(
        attend_first,
        outs + [sds((TOKENS, MODEL))],
        (place, proj, normed, grads, up, left, diag, last, att, share, share_bf),
        [smem()] + [vmem()] * 10,
        2**20,
        2**12,
        name="attend",
        scratch=[ds],
    )
    parts, cores = [(att, gp)], [sum_core(place, keep, send, 0)]
    for c in range(1, CHUNKS):
        att, gp, keep, send = call(
            functools.partial(attend_next, c),
            [sds((TOKENS, CW))] + outs,
            (place, proj, normed, cot, last),
            [smem()] + [vmem()] * 4,
            2**20,
            2**12,
            name="attend",
            scratch=held,
        )
        parts.append((att, gp))
        cores.append(sum_core(place, keep, send, c))
    *sent, tick = call(
        finish_kernel,
        [sds((2, OWN, MODEL)), sds((2, 64, MODEL)), sds((2, MSG, MODEL)), sds((2, 16, MODEL)), sds((8, 128), F32)],
        (emb, cot, qkv_weight, last, *[p[0] for p in parts], *[p[1] for p in parts]),
        [vmem(), vmem(), hbm(), vmem()] + [vmem()] * 2 * CHUNKS,
        2**20,
        2**12,
        name="finish",
        scratch=[
            pltpu.VMEM((MODEL, 3 * HW), BF16),
            pltpu.VMEM((TOKENS, MODEL), F32),
            pltpu.SemaphoreType.DMA,
        ],
    )
    mid, up, left, diag = sent
    up, diag = shift(up, -1, 0), shift(diag, -1, -1)
    (keep0, send0), (keep1, send1) = cores
    first, left = sum_first(place, keep0, send0, tick, left)
    summed = first + sum_second(place, keep1, send1, diag)
    left = shift(left, 0, -1)
    out, gin = call(
        place_kernel,
        [sds((TOKENS, MODEL))] * 2,
        (mid, up, left, diag),
        [vmem()] * 4,
        2**28,
        5 * 2**20,
        limit=24,
        name="place",
    )
    factor = 1.0 / math.sqrt(TOKENS * NB * NLAT * NLON)
    joined = call(
        join_kernel,
        sds((8, 16, 4 * Q)),
        (*summed, left),
        [vmem()] * 4 + [anywhere()],
        2**19,
        2**21,
        limit=16,
        name="join",
    )
    depth = lax.all_to_all(joined, "z", 0, 0, tiled=True)
    small = dict(flops=2**17, nbytes=2**19, limit=16)
    total = call(depth_kernel, sds((16, 4 * Q)), (depth,), [vmem()], name="depth", **small)
    g_qkv, g_out = call(
        functools.partial(level_kernel, factor),
        [sds((16, 3 * HW), F32), sds((16, HW), F32)],
        (place, total, *[swap(total, "batch", d) for d in (1, 2, 3)]),
        [smem()] + [vmem()] * 4,
        name="level",
        **small,
    )
    shape = (1, ROWS, COLS, MODEL)
    return (out.reshape(shape), gin.reshape(shape), g_qkv, g_out)


def solution(mesh):
    devices = mesh.devices.reshape(NB, 2, 2, 8, 2)
    fine = jax.sharding.Mesh(devices, ("batch",) + GRID)
    rows, cols = ("xh", "core"), ("z", "xl")
    grid, whole = P("batch", rows, cols), P()
    return jax.shard_map(
        shards,
        mesh=fine,
        in_specs=(grid, grid, grid, whole, whole, whole, whole, whole, P("batch", rows, cols, None)),
        out_specs=(
            P("batch", rows, cols, None),
            P("batch", rows, cols, None),
            P(GRID, None),
            P(GRID, None),
        ),
        check_vma=False,
    )
```
